256 devices in a mesh: slab: 64 (over y, z_hi, x), depth: 4 (over z_lo, core).
Axes of the slice: x: 4, y: 4, z: 8 (z_hi: 4, z_lo: 2; z = z_hi * 2 + z_lo), core: 2. Of those that a mesh axis runs over, the one named last changes fastest.
Arguments:
- forcing: float32 [3, 128, 128, 256], P(None, 'slab', 'depth'), may hold values from -18 to 18
- source: float32 [128, 128, 256], P('slab', 'depth'), may hold values from -6 to 6
- viscosity: float32 [128, 128, 256], P('slab', 'depth'), may hold values from 0.1 to 10
Outputs:
- velocity: float32 [3, 128, 128, 256], P(None, 'slab', 'depth')
- pressure: float32 [128, 128, 256], P('slab', 'depth')
The draws below stay inside these ranges and needn't reach their ends.
All inputs are finite; a program needn't handle non-finite values.
Results may differ from the reference program's by a relative error of at most 0.0001.
Values sent between devices are 32-bit elements; how exact they have to be, the bound alone decides.
A program may use at most 64 MiB of HBM per device.

```python
import math
import jax
import jax.numpy as jnp
from jax import lax

CZ = 256
KRYLOV = 3
NX = 128
NY = 128


def draw_forcing(key, part):
    key = jax.random.fold_in(key, 7)
    ramp = 1.0 + 2.0 * lax.iota(jnp.float32, NX) / max(NX - 1, 1)
    base = jnp.clip(jax.random.normal(key, (3, NX, NY, CZ), jnp.float32), -6.0, 6.0)
    return (base * ramp[None, :, None, None]).astype(jnp.float32)


def steps_of(stream_key, extent, cuts, smallest, high):
    level = 1.0
    for dim, parts in cuts:
        steps = jax.random.uniform(jax.random.fold_in(jax.random.fold_in(stream_key, 6), dim), (parts,), jnp.float32, smallest / len(cuts), high / len(cuts))
        level = level * jnp.repeat(jnp.exp(steps), extent[dim] // parts).reshape((-1,) + (1,) * (len(extent) - 1 - dim))
    return level


def scatter_about(own_key, dims, deviation, bound, cuts=(), kind=jnp.bfloat16):
    array = deviation * jax.random.normal(own_key, dims, jnp.float32)
    if cuts:
        array = array * steps_of(own_key, dims, cuts, -0.22, 0.18)
    return jnp.clip(array, -bound, bound).astype(kind)


def setup_inputs(seed: int = 0) -> dict:
    seeds = jax.random.split(jax.random.key(seed), 4)
    return {
        "forcing": draw_forcing(jax.random.fold_in(seeds[3], 71), 0),
        "source": scatter_about(seeds[1], (NX, NY, CZ), 1.0, 6.0, ((0, 64), (1, 4)), jnp.float32),
        "viscosity": jnp.clip(jnp.exp(math.log(10.0) - 4.6051702 * jax.random.uniform(seeds[2], (NX, NY, CZ), jnp.float32) ** steps_of(seeds[2], (NX, NY, CZ), ((0, 64), (1, 4)), -0.2, 0.2)), 0.1, 10.0),
    }


def corner_views(widened, span_slab, span_depth):
    views = []
    for s in range(8):
        offset_a, offset_b, offset_c = (s // 4, s // 2 % 2, s % 2)
        window = widened[:, offset_a:offset_a + span_slab, offset_b:offset_b + span_depth, :]
        if offset_c:
            window = jnp.roll(window, -1, axis=3)
        views.append(window)
    return views

def spread_terms(pieces):
    running = None
    for offset_a in range(2):
        for offset_b in range(2):
            s = 4 * offset_a + 2 * offset_b
            joined = pieces[s] + jnp.roll(pieces[s + 1], 1, axis=3)
            padded = jnp.pad(joined, ((0, 0), (offset_a, 1 - offset_a), (offset_b, 1 - offset_b), (0, 0)))
            running = padded if running is None else running + padded
    return running

def viscous_terms(views, element_visc):
    summed = views[0]
    for s in range(1, 8):
        summed = summed + views[s]
    return [element_visc * (summed * (-1.0 / 12.0) + views[s] * (5.0 / 12.0) + (views[s ^ 1] + views[s ^ 2] + views[s ^ 4]) * (1.0 / 12.0)) for s in range(8)]

def divergence(views):
    running = jnp.zeros_like(views[0][:1])
    for s in range(8):
        for c in range(3):
            offset = s >> 2 - c & 1
            running = running + (0.5 * offset - 0.25) * views[s][c:c + 1]
    return running

def gradient_terms(pressure_field):
    pieces = []
    for s in range(8):
        pieces.append(jnp.concatenate([(0.5 * (s >> 2 - c & 1) - 0.25) * pressure_field for c in range(3)], axis=0))
    return pieces

def inner_local(left, right):
    return jnp.sum(left[0] * right[0]) + jnp.sum(left[1] * right[1])

def small_solve(hessenberg, start_value):
    count = len(hessenberg[0])
    normal_matrix = []
    for a in range(count):
        line = []
        for b in range(count):
            element = hessenberg[0][a] * hessenberg[0][b]
            for r in range(1, count + 1):
                element = element + hessenberg[r][a] * hessenberg[r][b]
            line.append(element)
        normal_matrix.append(line)
    factor = [[0.0] * count for a in range(count)]
    for a in range(count):
        element = normal_matrix[a][a]
        for k in range(a):
            element = element - factor[a][k] * factor[a][k]
        factor[a][a] = jnp.sqrt(element)
        for b in range(a + 1, count):
            element = normal_matrix[b][a]
            for k in range(a):
                element = element - factor[b][k] * factor[a][k]
            factor[b][a] = element / factor[a][a]
    forward = []
    for a in range(count):
        element = start_value * hessenberg[0][a]
        for k in range(a):
            element = element - factor[a][k] * forward[k]
        forward.append(element / factor[a][a])
    coefficients = [0.0] * count
    for a in reversed(range(count)):
        element = forward[a]
        for k in range(a + 1, count):
            element = element - factor[k][a] * coefficients[k]
        coefficients[a] = element / factor[a][a]
    return coefficients

def reference(forcing, source, viscosity):
    slab_rows = lax.iota(jnp.int32, NX)
    depth_rows = lax.iota(jnp.int32, NY)
    free_mask = ((slab_rows > 0)[:, None] & (depth_rows > 0)[None, :]).astype(jnp.float32)[None, :, :, None]
    element_visc = viscosity[None]

    def widen(field):
        return jnp.pad(field, ((0, 0), (0, 1), (0, 1), (0, 0)))

    def owned(partial_value):
        return partial_value[:, :-1, :-1, :]
    diagonal = owned(spread_terms([element_visc / 3.0] * 8))
    inverse_diag = free_mask / diagonal
    schur_views = corner_views(widen(inverse_diag), NX, NY)
    schur_diag = schur_views[0]
    for s in range(1, 8):
        schur_diag = schur_diag + schur_views[s]
    schur_diag = 0.1875 * schur_diag

    def viscous(field):
        return owned(spread_terms(viscous_terms(corner_views(widen(field), NX, NY), element_visc))) * free_mask

    def grad_nodes(pressure_field):
        return owned(spread_terms(gradient_terms(pressure_field))) * free_mask

    def precondition(pair):
        jacobi_start = inverse_diag * pair[0]
        jacobi = jacobi_start + inverse_diag * (pair[0] - viscous(jacobi_start))
        mass_defect = divergence(corner_views(widen(jacobi), NX, NY)) - pair[1]
        pressure_first = mass_defect / schur_diag
        correction = inverse_diag * grad_nodes(pressure_first)
        pressure_next = pressure_first + (mass_defect - divergence(corner_views(widen(correction), NX, NY))) / schur_diag
        return (jacobi - inverse_diag * grad_nodes(pressure_next), pressure_next)

    def stokes_apply(pair):
        views = corner_views(widen(pair[0]), NX, NY)
        nodal = owned(spread_terms(viscous_terms(views, element_visc)) + spread_terms(gradient_terms(pair[1]))) * free_mask
        return (nodal, divergence(views))
    start = (forcing * free_mask, source[None])
    start_value = jnp.sqrt(inner_local(start, start))
    directions = [(start[0] / start_value, start[1] / start_value)]
    searches = []
    hessenberg = [[0.0] * KRYLOV for r in range(KRYLOV + 1)]
    for j in range(KRYLOV):
        search = precondition(directions[j])
        searches.append(search)
        image = stokes_apply(search)
        projections = [inner_local(image, directions[i]) for i in range(j + 1)]
        image_u, image_p = image
        for i in range(j + 1):
            image_u = image_u - projections[i] * directions[i][0]
            image_p = image_p - projections[i] * directions[i][1]
        rest_norm = jnp.sqrt(inner_local((image_u, image_p), (image_u, image_p)))
        for i in range(j + 1):
            hessenberg[i][j] = projections[i]
        hessenberg[j + 1][j] = rest_norm
        directions.append((image_u / rest_norm, image_p / rest_norm))
    coefficients = small_solve(hessenberg, start_value)
    velocity = coefficients[0] * searches[0][0]
    pressure = coefficients[0] * searches[0][1]
    for j in range(1, KRYLOV):
        velocity = velocity + coefficients[j] * searches[j][0]
        pressure = pressure + coefficients[j] * searches[j][1]
    return (velocity, pressure[0])
```

```python
import functools

import jax
import jax.numpy as jnp
from jax import lax
from jax.experimental import pallas as pl
from jax.experimental.pallas import tpu as pltpu
from jax.sharding import PartitionSpec as P

KRYLOV = 3
ROWS = 32
TALL = 40
LANES = 256
MESH_ID = pl.DeviceIdType.MESH


def next_z(x):
    return pltpu.roll(x, LANES - 1, 1)


def prev_z(x):
    return pltpu.roll(x, 1, 1)


def next_y(x):
    return pltpu.roll(x, TALL - 1, 0)


def prev_y(x):
    return pltpu.roll(x, 1, 0)


def forward_modes(u):
    ahead = next_z(u)
    zs = ahead + u
    zd = ahead - u
    zs_ahead = next_y(zs)
    zd_ahead = next_y(zd)
    return zs_ahead + zs, zs_ahead - zs, zd_ahead + zd, zd_ahead - zd


def element_modes(low, high):
    return (
        high[0] - low[0],
        high[1] - low[1],
        high[1] + low[1],
        high[2] - low[2],
        high[2] + low[2],
        high[3] - low[3],
        high[3] + low[3],
    )


def weigh(modes, visc):
    v16 = visc * (1.0 / 16.0)
    v24 = visc * (1.0 / 24.0)
    v48 = visc * (1.0 / 48.0)
    return (
        modes[0] * v16,
        modes[1] * v24,
        modes[2] * v16,
        modes[3] * v24,
        modes[4] * v16,
        modes[5] * v48,
        modes[6] * v24,
    )


def back_to_nodes(before, after):
    ss = before[0] - after[0]
    ds = (before[2] + before[1]) + (after[2] - after[1])
    sd = (before[4] + before[3]) + (after[4] - after[3])
    dd = (before[6] + before[5]) + (after[6] - after[5])
    zs = (ss - ds) + prev_y(ss + ds)
    zd = (sd - dd) + prev_y(sd + dd)
    return (zs - zd) + prev_z(zs + zd)


def divergence_halves(u):
    x_ahead = next_z(u[0])
    y_ahead = next_z(u[1])
    z_ahead = next_z(u[2])
    zs_x = x_ahead + u[0]
    zs_y = y_ahead + u[1]
    zd_z = z_ahead - u[2]
    ss_x = next_y(zs_x) + zs_x
    rest = (zd_z - zs_y) + next_y(zd_z + zs_y)
    return rest + ss_x, rest - ss_x


def gradient(before, after):
    diff = before - after
    both = before + after
    diff_y = diff + prev_y(diff)
    both_back = prev_y(both)
    sum_y = both + both_back
    dif_y = both_back - both
    return (
        diff_y + prev_z(diff_y),
        dif_y + prev_z(dif_y),
        prev_z(sum_y) - sum_y,
    )


def fold(product):
    tile = product[0:8] + product[8:16] + product[16:24] + product[24:32]
    return tile[:, :128] + tile[:, 128:]


def kernel(
    f_hbm, s_hbm, v_hbm, vel_ref, pre_ref,
    V, VM, VH, JS, DH, QP, QH, T, R3, INV, ISC, FW, E, JAC, PN, ZU, ZP, WU, WP, QU, Q0, DOT, ARA, ARB, PART,
    load_sem, s_send, s_recv, i_send, i_recv, a_send, a_recv, b_send, b_recv,
):
    slab = lax.axis_index("slab")
    depth = lax.axis_index("depth")
    slab_next = lax.rem(slab + 1, 64)
    slab_prev = lax.rem(slab + 63, 64)
    depth_next = lax.rem(depth + 1, 4)
    depth_prev = lax.rem(depth + 3, 4)
    to_next = (slab_next, depth)
    to_prev = (slab_prev, depth)
    to_up = (slab, depth_next)
    to_down = (slab, depth_prev)

    loads = [
        pltpu.make_async_copy(v_hbm, V.at[2:4, 0:ROWS], load_sem.at[0]),
        pltpu.make_async_copy(s_hbm, QP.at[0, 1:3, 0:ROWS], load_sem.at[1]),
        pltpu.make_async_copy(f_hbm, Q0, load_sem.at[2]),
    ]
    for load in loads:
        load.start()

    a_me = lax.rem(slab, 4) * 4 + depth
    b_me = slab // 4

    def a_peer(i):
        other = lax.rem(a_me + i, 16)
        return ((slab // 4) * 4 + other // 4, lax.rem(other, 4))

    def b_peer(i):
        other = lax.rem(b_me + i, 16)
        return (other * 4 + lax.rem(slab, 4), depth)

    barrier = pltpu.get_barrier_semaphore()
    for peer in (to_next, to_prev, to_up, to_down):
        pl.semaphore_signal(barrier, inc=1, device_id=peer, device_id_type=MESH_ID)

    @pl.loop(1, 16)
    def _(i):
        pl.semaphore_signal(barrier, inc=1, device_id=a_peer(i), device_id_type=MESH_ID)
        pl.semaphore_signal(barrier, inc=1, device_id=b_peer(i), device_id_type=MESH_ID)

    pl.semaphore_wait(barrier, 34)

    def remote(src, dst, send, recv, peer):
        return pltpu.make_async_remote_copy(
            src_ref=src, dst_ref=dst, send_sem=send, recv_sem=recv, device_id=peer, device_id_type=MESH_ID
        )

    def setup_copy(k, src, dst, peer):
        return lambda: remote(src, dst, s_send.at[k], s_recv.at[k], peer)

    def setup_copies():
        return dict(
            near_next=setup_copy(0, V.at[3, 0:ROWS], V.at[1, 0:ROWS], to_next),
            near_prev=setup_copy(1, V.at[2, 0:ROWS], V.at[4, 0:ROWS], to_prev),
            up=setup_copy(2, V.at[2:4, 24:32], VH.at[0], to_up),
            down=setup_copy(3, V.at[2:4, 0:8], VH.at[1], to_down),
            tile_next=setup_copy(4, V.at[3, 32:40], V.at[1, 32:40], to_next),
            tile_prev=setup_copy(5, V.at[2, 32:40], V.at[4, 32:40], to_prev),
            far_next=setup_copy(6, V.at[2], V.at[0], to_next),
            source=setup_copy(7, QP.at[0, 2, 0:ROWS], QP.at[0, 0, 0:ROWS], to_next),
        )

    def step_copies(j):
        def copy(k, src, dst, peer):
            return lambda: remote(src, dst, i_send.at[j, k], i_recv.at[j, k], peer)

        return dict(
            near_next=copy(0, JS.at[j, 3, :, 0:ROWS], JS.at[j, 1, :, 0:ROWS], to_next),
            near_prev=copy(1, JS.at[j, 2, :, 0:ROWS], JS.at[j, 4, :, 0:ROWS], to_prev),
            up=copy(2, JS.at[j, 2:4, :, 24:32], DH.at[j, 0], to_up),
            down=copy(3, JS.at[j, 2:4, :, 0:8], DH.at[j, 1], to_down),
            p_up=copy(4, QP.at[j, :, 24:32], QH.at[j, 0], to_up),
            p_down=copy(5, QP.at[j, :, 0:8], QH.at[j, 1], to_down),
            tile_next=copy(6, JS.at[j, 3, :, 32:40], JS.at[j, 1, :, 32:40], to_next),
            tile_prev=copy(7, JS.at[j, 2, :, 32:40], JS.at[j, 4, :, 32:40], to_prev),
            far_next=copy(8, JS.at[j, 2], JS.at[j, 0], to_next),
            far_prev=copy(9, JS.at[j, 3], JS.at[j, 5], to_prev),
            r3_next=copy(10, T.at[j, 0], R3.at[j, 0], to_next),
            r3_prev=copy(11, T.at[j, 1], R3.at[j, 1], to_prev),
        )

    FIRST = ("up", "down", "near_next", "near_prev", "p_up", "p_down")

    setup = setup_copies()
    loads[0].wait()
    for name in ("up", "down", "near_next", "near_prev"):
        setup[name]().start()
    loads[1].wait()
    setup["source"]().start()

    top = lax.broadcasted_iota(jnp.int32, (8, LANES), 0) < 4

    def halo_tile(above, below):
        return jnp.where(top, above, below)

    setup["up"]().wait_recv()
    setup["down"]().wait_recv()
    for n in range(2):
        V[2 + n, 32:40] = halo_tile(VH[1, n], VH[0, n])
    for name in ("tile_next", "tile_prev", "far_next"):
        setup[name]().start()

    row = lax.broadcasted_iota(jnp.int32, (TALL, LANES), 0)
    row = depth * ROWS + jnp.where(row < 36, row, row - TALL)
    element_row = ((row >= 0) & (row < 128)).astype(jnp.float32)
    node_row = ((row >= 1) & (row < 128)).astype(jnp.float32)

    def slab_flag(n, low):
        place = slab * 2 + n
        return ((place >= low) & (place < 128)).astype(jnp.float32)

    def viscosity_plane(n):
        VM[n + 2] = V[n + 2] * (element_row * slab_flag(n, 0))

    def inverse_plane(n):
        both = VM[n + 1] + VM[n + 2]
        both = both + prev_y(both)
        both = both + prev_z(both)
        free = node_row * slab_flag(n, 1)
        INV[n + 1] = free * 3.0 / jnp.where(free > 0.0, both, 1.0)

    for name in ("near_next", "near_prev", "tile_next", "tile_prev"):
        setup[name]().wait_recv()
    for n in (-1, 0, 1):
        viscosity_plane(n)
    inverse_plane(0)
    inverse_plane(1)
    loads[2].wait()
    for n in range(2):
        free = (node_row * slab_flag(n, 1))[0:ROWS]
        inverse = INV[n + 1, 0:ROWS]
        for c in range(3):
            q = Q0[c, n] * free
            Q0[c, n] = q
            QU[c, n] = q
            JS[0, 2 + n, c, 0:ROWS] = q * inverse
    first = step_copies(0)
    setup["source"]().wait_recv()
    for name in FIRST:
        first[name]().start()

    setup["far_next"]().wait_recv()
    viscosity_plane(-2)
    viscosity_plane(2)
    inverse_plane(-1)
    inverse_plane(2)
    for e in (-1, 0, 1):
        both = INV[e + 1] + INV[e + 2]
        both = both + next_y(both)
        both = both + next_z(both)
        there = element_row * slab_flag(e, 0)
        ISC[e + 1] = there / jnp.where(there > 0.0, 0.1875 * both, 1.0)

    @pl.loop(0, KRYLOV)
    def _(j):
        copies = step_copies(j)
        for name in ("up", "down"):
            copies[name]().wait_recv()
        for n in range(2):
            for c in range(3):
                JS[j, 2 + n, c, 32:40] = halo_tile(DH[j, 1, n, c], DH[j, 0, n, c])
        for name in ("tile_next", "tile_prev", "far_next", "far_prev"):
            copies[name]().start()

        def forward(n, c):
            modes = forward_modes(JS[j, n + 2, c])
            for m in range(4):
                FW[c, n + 2, m] = modes[m]

        def element(e, c):
            low = [FW[c, e + 2, m] for m in range(4)]
            high = [FW[c, e + 3, m] for m in range(4)]
            modes = weigh(element_modes(low, high), VM[e + 2])
            for m in range(7):
                E[c, e + 2, m] = modes[m]

        def jacobi(n, c):
            before = [E[c, n + 1, m] for m in range(7)]
            after = [E[c, n + 2, m] for m in range(7)]
            JAC[n + 1, c] = 2.0 * JS[j, n + 2, c] - INV[n + 1] * back_to_nodes(before, after)

        for c in range(3):
            forward(0, c)
            forward(1, c)
            element(0, c)
        for name in ("near_next", "near_prev", "tile_next", "tile_prev"):
            copies[name]().wait_recv()
        for c in range(3):
            forward(-1, c)
            element(-1, c)
            jacobi(0, c)
            forward(2, c)
            element(1, c)
            jacobi(1, c)
        for name in ("far_next", "far_prev"):
            copies[name]().wait_recv()
        for c in range(3):
            forward(-2, c)
            element(-2, c)
            jacobi(-1, c)
            forward(3, c)
            element(2, c)
            jacobi(2, c)
        for name in ("p_up", "p_down"):
            copies[name]().wait_recv()
        for e in range(3):
            QP[j, e, 32:40] = halo_tile(QH[j, 1, e], QH[j, 0, e])

        halves = [divergence_halves([JAC[n, c] for c in range(3)]) for n in range(4)]
        defect = [0.25 * (halves[e + 1][0] + halves[e][1]) - QP[j, e] for e in range(3)]
        first_p = [defect[e] * ISC[e] for e in range(3)]
        cor = []
        for n in range(2):
            slope = gradient(first_p[n], first_p[n + 1])
            scale = 0.25 * INV[n + 1]
            cor.append(divergence_halves([scale * slope[c] for c in range(3)]))
        middle = first_p[1] + (defect[1] - 0.25 * (cor[1][0] + cor[0][1])) * ISC[1]
        T[j, 0, 0] = cor[1][1]
        T[j, 0, 1] = middle
        T[j, 1, 0] = cor[0][0]
        T[j, 1, 1] = middle
        copies["r3_next"]().start()
        copies["r3_prev"]().start()
        PN[2] = middle
        ZP[j, 0] = middle[0:ROWS]
        low_p = first_p[0] + (defect[0] - 0.25 * cor[0][0]) * ISC[0]
        high_p = first_p[2] + (defect[2] - 0.25 * cor[1][1]) * ISC[2]
        copies["r3_next"]().wait_recv()
        copies["r3_prev"]().wait_recv()
        PN[1] = low_p - 0.25 * R3[j, 0, 0] * ISC[0]
        high_p = high_p - 0.25 * R3[j, 1, 0] * ISC[2]
        PN[3] = high_p
        ZP[j, 1] = high_p[0:ROWS]
        PN[0] = R3[j, 0, 1]
        PN[4] = R3[j, 1, 1]

        div = [None] * 3
        for n in range(4):
            slope = gradient(PN[n], PN[n + 1])
            scale = 0.25 * INV[n]
            for c in range(3):
                z = JAC[n, c] - scale * slope[c]
                if n in (1, 2):
                    ZU[j, c, n - 1] = z[0:ROWS]
                modes = forward_modes(z)
                for m in range(4):
                    FW[c, n, m] = modes[m]
        for c in range(3):
            for e in range(3):
                low = [FW[c, e, m] for m in range(4)]
                high = [FW[c, e + 1, m] for m in range(4)]
                modes = element_modes(low, high)
                own = modes[(0, 2, 4)[c]]
                div[e] = own if c == 0 else div[e] + own
                modes = list(weigh(modes, VM[e + 1]))
                modes[(0, 2, 4)[c]] = modes[(0, 2, 4)[c]] + 0.25 * PN[e + 1]
                for m in range(7):
                    E[c, e, m] = modes[m]
        for e in range(3):
            w = 0.25 * div[e][0:ROWS]
            WP[j, e] = w
            QP[j + 1, e, 0:ROWS] = w - QP[j, e, 0:ROWS]
        for n in range(2):
            free = (node_row * slab_flag(n, 1))[0:ROWS]
            inverse = INV[n + 1, 0:ROWS]
            for c in range(3):
                before = [E[c, n, m] for m in range(7)]
                after = [E[c, n + 1, m] for m in range(7)]
                w = back_to_nodes(before, after)[0:ROWS] * free
                WU[j, c, n] = w
                q = w - QU[c, n]
                QU[c, n] = q
                JS[j + 1, 2 + n, c, 0:ROWS] = q * inverse

        @pl.when(j < KRYLOV - 1)
        def _():
            later = step_copies(j + 1)
            for name in FIRST:
                later[name]().start()

        def inner(left_u, left_p):
            total = None
            for n in range(2):
                for c in range(3):
                    term = fold(WU[j, c, n] * left_u(c, n))
                    total = term if total is None else total + term
                total = total + fold(WP[j, n + 1] * left_p(n))
            return total

        DOT[j * 4 + 3] = inner(lambda c, n: Q0[c, n], lambda n: QP[0, n + 1, 0:ROWS])

        @pl.loop(0, j + 1)
        def _(k):
            DOT[j * 4 + k] = inner(lambda c, n: WU[k, c, n], lambda n: WP[k, n + 1])

    order = [(0, 0), (1, 0), (2, 0), (1, 1), (2, 1), (2, 2), (0, 3), (1, 3), (2, 3)]
    rows16 = lax.broadcasted_iota(jnp.int32, (16, 128), 0)
    stacked = jnp.zeros((16, 128), jnp.float32)
    for place, (a, b) in enumerate(order):
        line = jnp.sum(DOT[a * 4 + b], axis=0, keepdims=True)
        stacked = jnp.where(rows16 == place, line, stacked)
    folded = stacked + pltpu.roll(stacked, 64, 1)
    left = lax.broadcasted_iota(jnp.int32, (8, 128), 1) < 64
    tile = jnp.where(left, folded[0:8], folded[8:16])

    def reduce(tile, stage, buffer, me, peer, send, recv):
        buffer[me] = tile
        PART[stage] = tile

        def copy(i):
            return remote(PART.at[stage], buffer.at[me], send.at[i], recv.at[me], peer(i))

        def arrival(i):
            other = lax.rem(me + i, 16)
            return remote(PART.at[stage], buffer.at[other], send.at[i], recv.at[other], peer(i))

        @pl.loop(1, 16)
        def _(i):
            copy(i).start()

        @pl.loop(1, 16)
        def _(i):
            arrival(i).wait_recv()

        @pl.loop(1, 16)
        def _(i):
            copy(i).wait_send()

        total = buffer[0]
        for i in range(1, 16):
            total = total + buffer[i]
        return total

    tile = reduce(tile, 0, ARA, a_me, a_peer, a_send, a_recv)
    tile = reduce(tile, 1, ARB, b_me, b_peer, b_send, b_recv)
    sums_a = jnp.sum(jnp.where(left, tile, 0.0), axis=1, keepdims=True)
    sums_b = jnp.sum(jnp.where(left, 0.0, tile), axis=1, keepdims=True)
    a00, a10, a20, a11, a21, a22, b0, b1 = [sums_a[i : i + 1] for i in range(8)]
    b2 = sums_b[0:1]
    l00 = jnp.sqrt(a00)
    l10 = a10 / l00
    l20 = a20 / l00
    l11 = jnp.sqrt(a11 - l10 * l10)
    l21 = (a21 - l20 * l10) / l11
    l22 = jnp.sqrt(a22 - l20 * l20 - l21 * l21)
    y0 = b0 / l00
    y1 = (b1 - l10 * y0) / l11
    y2 = (b2 - l20 * y0 - l21 * y1) / l22
    c2 = y2 / l22
    c1 = (y1 - l21 * c2) / l11
    c0 = (y0 - l10 * c1 - l20 * c2) / l00
    for n in range(2):
        for c in range(3):
            vel_ref[c, n] = c0 * ZU[0, c, n] + c1 * ZU[1, c, n] + c2 * ZU[2, c, n]
        pre_ref[n] = c0 * ZP[0, n] + c1 * ZP[1, n] + c2 * ZP[2, n]

    for copy in setup.values():
        copy().wait_send()

    @pl.loop(0, KRYLOV)
    def _(j):
        for copy in step_copies(j).values():
            copy().wait_send()


def body(forcing, source, viscosity):
    f32 = jnp.float32
    vmem = lambda *shape: pltpu.VMEM(shape, f32)
    dma = lambda *shape: pltpu.SemaphoreType.DMA(shape)
    K = KRYLOV
    return pl.pallas_call(
        kernel,
        out_shape=(
            jax.ShapeDtypeStruct((3, 2, ROWS, LANES), f32),
            jax.ShapeDtypeStruct((2, ROWS, LANES), f32),
        ),
        in_specs=[pl.BlockSpec(memory_space=pl.ANY)] * 3,
        out_specs=(pl.BlockSpec(memory_space=pltpu.VMEM), pl.BlockSpec(memory_space=pltpu.VMEM)),
        scratch_shapes=[
            vmem(5, TALL, LANES),
            vmem(5, TALL, LANES),
            vmem(2, 2, 8, LANES),
            vmem(K + 1, 6, 3, TALL, LANES),
            vmem(K, 2, 2, 3, 8, LANES),
            vmem(K + 1, 3, TALL, LANES),
            vmem(K, 2, 3, 8, LANES),
            vmem(K, 2, 2, TALL, LANES),
            vmem(K, 2, 2, TALL, LANES),
            vmem(4, TALL, LANES),
            vmem(3, TALL, LANES),
            vmem(3, 6, 4, TALL, LANES),
            vmem(3, 5, 7, TALL, LANES),
            vmem(4, 3, TALL, LANES),
            vmem(5, TALL, LANES),
            vmem(K, 3, 2, ROWS, LANES),
            vmem(K, 2, ROWS, LANES),
            vmem(K, 3, 2, ROWS, LANES),
            vmem(K, 3, ROWS, LANES),
            vmem(3, 2, ROWS, LANES),
            vmem(3, 2, ROWS, LANES),
            vmem(4 * K, 8, 128),
            vmem(16, 8, 128),
            vmem(16, 8, 128),
            vmem(2, 8, 128),
            dma(3),
            dma(8),
            dma(8),
            dma(K, 12),
            dma(K, 12),
            dma(16),
            dma(16),
            dma(16),
            dma(16),
        ],
        compiler_params=pltpu.CompilerParams(
            collective_id=0, has_side_effects=True, vmem_limit_bytes=48 * 1024 * 1024
        ),
        name="stokes_cycle",
    )(forcing, source, viscosity)


def solution(mesh):
    placed = (P(None, "slab", "depth", None), P("slab", "depth", None), P("slab", "depth", None))
    return jax.shard_map(
        body,
        mesh=mesh,
        in_specs=placed,
        out_specs=(P(None, "slab", "depth", None), P("slab", "depth", None)),
        check_vma=False,
    )
```

```python
import jax
import jax.numpy as jnp
from jax import lax
from jax.experimental import pallas as pl
from jax.experimental.pallas import tpu as pltpu
from jax.sharding import PartitionSpec as P

KRYLOV = 3
EDGE = 8
WIDE = 16
OFF = 4
LANES = 256
MESH_ID = pl.DeviceIdType.MESH


def next_z(x):
    return pltpu.roll(x, LANES - 1, 1)


def prev_z(x):
    return pltpu.roll(x, 1, 1)


def next_y(x):
    return pltpu.roll(x, WIDE - 1, 0)


def prev_y(x):
    return pltpu.roll(x, 1, 0)


def forward_modes(u):
    ahead = next_z(u)
    zs = ahead + u
    zd = ahead - u
    zs_ahead = next_y(zs)
    zd_ahead = next_y(zd)
    return zs_ahead + zs, zs_ahead - zs, zd_ahead + zd, zd_ahead - zd


def element_modes(low, high):
    return (
        high[0] - low[0],
        high[1] - low[1],
        high[1] + low[1],
        high[2] - low[2],
        high[2] + low[2],
        high[3] - low[3],
        high[3] + low[3],
    )


def weigh(modes, visc):
    v16 = visc * (1.0 / 16.0)
    v24 = visc * (1.0 / 24.0)
    v48 = visc * (1.0 / 48.0)
    return (
        modes[0] * v16,
        modes[1] * v24,
        modes[2] * v16,
        modes[3] * v24,
        modes[4] * v16,
        modes[5] * v48,
        modes[6] * v24,
    )


def from_before(modes):
    return modes[0], modes[2] + modes[1], modes[4] + modes[3], modes[6] + modes[5]


def from_after(modes):
    return modes[0], modes[2] - modes[1], modes[4] - modes[3], modes[6] - modes[5]


def back_to_nodes(before, after):
    ss = before[0] - after[0]
    ds = before[1] + after[1]
    sd = before[2] + after[2]
    dd = before[3] + after[3]
    zs = (ss - ds) + prev_y(ss + ds)
    zd = (sd - dd) + prev_y(sd + dd)
    return (zs - zd) + prev_z(zs + zd)


def divergence_halves(u):
    x_ahead = next_z(u[0])
    y_ahead = next_z(u[1])
    z_ahead = next_z(u[2])
    zs_x = x_ahead + u[0]
    zs_y = y_ahead + u[1]
    zd_z = z_ahead - u[2]
    ss_x = next_y(zs_x) + zs_x
    rest = (zd_z - zs_y) + next_y(zd_z + zs_y)
    return rest + ss_x, rest - ss_x


def gradient(before, after):
    diff = before - after
    both = before + after
    diff_y = diff + prev_y(diff)
    both_back = prev_y(both)
    sum_y = both + both_back
    dif_y = both_back - both
    return (
        diff_y + prev_z(diff_y),
        dif_y + prev_z(dif_y),
        prev_z(sum_y) - sum_y,
    )


def fold(product):
    return product[:, :128] + product[:, 128:]


def block_of(slab, depth):
    x = lax.rem(slab, 4)
    y = slab // 16
    z = lax.rem(slab // 4, 4) * 2 + depth // 2
    odd = lax.rem(y, 2)
    return y * 4 + x + odd * (3 - 2 * x), z * 2 + lax.rem(depth, 2)


def device_of(across, along):
    y = across // 4
    place = lax.rem(across, 4)
    odd = lax.rem(y, 2)
    x = place + odd * (3 - 2 * place)
    z = along // 2
    return y * 16 + (z // 2) * 4 + x, lax.rem(z, 2) * 2 + lax.rem(along, 2)


def kernel(
    f_hbm, s_hbm, v_hbm, vel_ref, pre_ref,
    V, VM, X, INV, ISC, JAC, MID, MD, P1, PN, Z, ZS, DIV, W, Q, Q0, OUT, HOME, DOT, ARA, ARB, PART,
    in_send, in_recv, in_local, s_send, s_recv, i_send, i_recv, out_send, out_recv, out_local,
    a_send, a_recv, b_send, b_recv,
):
    slab = lax.axis_index("slab")
    depth = lax.axis_index("depth")
    across, along = block_of(slab, depth)
    to_next = device_of(lax.rem(across + 1, 16), along)
    to_prev = device_of(lax.rem(across + 15, 16), along)
    to_up = device_of(across, lax.rem(along + 1, 16))
    to_down = device_of(across, lax.rem(along + 15, 16))

    my_k = lax.rem(slab, 4)
    my_tile = lax.rem(along, 4)
    goes_to = [device_of(slab // 4, depth * 4 + i) for i in range(4)]
    comes_from = [(across * 4 + k, along // 4) for k in range(4)]

    def is_me(device):
        return (device[0] == slab) & (device[1] == depth)

    def a_peer(i):
        return device_of(lax.rem(across + i, 16), along)

    def b_peer(i):
        return device_of(across, lax.rem(along + i, 16))

    barrier = pltpu.get_barrier_semaphore()

    def greet(device):
        pl.semaphore_signal(barrier, inc=1, device_id=device, device_id_type=MESH_ID)

    for device in goes_to + comes_from:
        greet(device)

    @pl.loop(1, 16)
    def _(i):
        greet(a_peer(i))
        greet(b_peer(i))

    pl.semaphore_wait(barrier, 38)

    def remote(src, dst, send, recv, peer):
        return pltpu.make_async_remote_copy(
            src_ref=src, dst_ref=dst, send_sem=send, recv_sem=recv, device_id=peer, device_id_type=MESH_ID
        )

    def rows(i):
        return pl.ds(pl.multiple_of(i * EDGE, EDGE), EDGE)

    def fields(i, k):
        return (
            (v_hbm.at[:, rows(i)], V.at[pl.ds(OFF + 2 * k, 2), 0:EDGE]),
            (f_hbm.at[:, :, rows(i)], Q0.at[0:3, pl.ds(2 * k, 2)]),
            (s_hbm.at[:, rows(i)], Q0.at[3, pl.ds(2 * k, 2)]),
        )

    def give(t, i):
        src, dst = fields(i, my_k)[t]
        return remote(src, dst, in_send.at[t, i], in_recv.at[t, my_k], goes_to[i])

    def take(t, k):
        src, dst = fields(0, k)[t]
        return remote(src, dst, in_send.at[t, 0], in_recv.at[t, k], comes_from[k])

    def keep(t):
        src, dst = fields(my_tile, my_k)[t]
        return pltpu.make_async_copy(src, dst, in_local.at[t])

    home = is_me(device_of(slab // 4, depth * 4 + my_tile))
    for t in range(3):
        pl.when(home)(lambda t=t: keep(t).start())
        for i in range(4):
            pl.when(jnp.logical_not(is_me(goes_to[i])))(lambda t=t, i=i: give(t, i).start())

    def taken(t):
        pl.when(home)(lambda: keep(t).wait())
        for k in range(4):
            pl.when(jnp.logical_not(is_me(comes_from[k])))(lambda k=k: take(t, k).wait_recv())

    def setup_copy(k, src, dst, peer):
        return lambda: remote(src, dst, s_send.at[k], s_recv.at[k], peer)

    setup = dict(
        up=setup_copy(0, V.at[4:12, 4:8], V.at[4:12, 12:16], to_up),
        down=setup_copy(1, V.at[4:12, 0:4], V.at[4:12, 8:12], to_down),
        next=setup_copy(2, V.at[8:12], V.at[0:4], to_next),
        prev=setup_copy(3, V.at[4:8], V.at[12:16], to_prev),
    )

    def step_copies(j):
        def copy(k, src, dst, peer):
            return lambda: remote(src, dst, i_send.at[j, k], i_recv.at[j, k], peer)

        return dict(
            up=copy(0, X.at[j, :, 4:12, 4:8], X.at[j, :, 4:12, 12:16], to_up),
            down=copy(1, X.at[j, :, 4:12, 0:4], X.at[j, :, 4:12, 8:12], to_down),
            main_next=copy(2, X.at[j, :, 8:12, 0:8], X.at[j, :, 0:4, 0:8], to_next),
            main_prev=copy(3, X.at[j, :, 4:8, 0:8], X.at[j, :, 12:16, 0:8], to_prev),
            tile_next=copy(4, X.at[j, :, 8:12, 8:16], X.at[j, :, 0:4, 8:16], to_next),
            tile_prev=copy(5, X.at[j, :, 4:8, 8:16], X.at[j, :, 12:16, 8:16], to_prev),
        )

    FIRST = ("up", "down", "main_next", "main_prev")

    taken(0)
    setup["up"]().start()
    setup["down"]().start()

    row = lax.broadcasted_iota(jnp.int32, (WIDE, LANES), 0)
    row = along * EDGE + jnp.where(row < 12, row, row - WIDE)
    element_row = ((row >= 0) & (row < 128)).astype(jnp.float32)
    node_row = ((row >= 1) & (row < 128)).astype(jnp.float32)

    def plane_flag(n, low):
        place = across * EDGE + n
        return ((place >= low) & (place < 128)).astype(jnp.float32)

    setup["up"]().wait_recv()
    setup["down"]().wait_recv()
    setup["next"]().start()
    setup["prev"]().start()

    def inverse_plane(n):
        both = VM[n + OFF - 1] + VM[n + OFF]
        both = both + prev_y(both)
        both = both + prev_z(both)
        free = node_row * plane_flag(n, 1)
        INV[n + OFF] = free * 3.0 / jnp.where(free > 0.0, both, 1.0)

    for n in range(8):
        VM[n + OFF] = V[n + OFF] * (element_row * plane_flag(n, 0))
    for n in range(1, 8):
        inverse_plane(n)
    setup["next"]().wait_recv()
    setup["prev"]().wait_recv()
    for n in (-4, -3, -2, -1, 8, 9, 10, 11):
        VM[n + OFF] = V[n + OFF] * (element_row * plane_flag(n, 0))
    inverse_plane(0)
    taken(1)
    taken(2)
    for n in range(8):
        free = (node_row * plane_flag(n, 1))[0:EDGE]
        inverse = INV[n + OFF, 0:EDGE]
        for c in range(3):
            q = Q0[c, n] * free
            Q0[c, n] = q
            Q[c, n] = q
            X[0, c, n + OFF, 0:EDGE] = q * inverse
        p = Q0[3, n]
        Q[3, n] = p
        X[0, 3, n + OFF, 0:EDGE] = p
    first = step_copies(0)
    for name in FIRST:
        first[name]().start()
    for n in (-3, -2, -1, 8, 9, 10):
        inverse_plane(n)
    for e in range(-3, 10):
        both = INV[e + OFF] + INV[e + OFF + 1]
        both = both + next_y(both)
        both = both + next_z(both)
        there = element_row * plane_flag(e, 0)
        ISC[e + OFF] = there / jnp.where(there > 0.0, 0.1875 * both, 1.0)

    @pl.loop(0, KRYLOV)
    def _(j):
        copies = step_copies(j)
        for name in ("up", "down"):
            copies[name]().wait_recv()
        for name in ("tile_next", "tile_prev"):
            copies[name]().start()

        def modes_of(n, c):
            return forward_modes(X[j, c, n + OFF])

        def jacobi(n, c, before, after):
            JAC[c, n + OFF] = 2.0 * X[j, c, n + OFF] - INV[n + OFF] * back_to_nodes(before, after)

        def sweep(first, last, c, before, keep_first, keep_last):
            low = modes_of(first, c)
            for e in range(first, last + 1):
                high = modes_of(e + 1, c)
                weighted = weigh(element_modes(low, high), VM[e + OFF])
                after = from_after(weighted)
                if before is not None:
                    jacobi(e, c, before, after)
                elif keep_first is not None:
                    for m in range(4):
                        MID[c, keep_first, m] = after[m]
                before = from_before(weighted)
                low = high
            if keep_last is not None:
                for m in range(4):
                    MID[c, keep_last, m] = before[m]
            return before

        for c in range(3):
            sweep(0, 6, c, None, 0, 1)
        for name in ("main_next", "main_prev", "tile_next", "tile_prev"):
            copies[name]().wait_recv()
        for c in range(3):
            before = sweep(-4, -1, c, None, None, None)
            jacobi(0, c, before, [MID[c, 0, m] for m in range(4)])
            sweep(7, 10, c, [MID[c, 1, m] for m in range(4)], None, None)

        low = None
        for n in range(-3, 11):
            high, own = divergence_halves([JAC[c, n + OFF] for c in range(3)])
            if low is not None:
                e = n - 1
                defect = 0.25 * (high + low) - X[j, 3, e + OFF]
                MD[e + OFF] = defect
                P1[e + OFF] = defect * ISC[e + OFF]
            low = own
        low = None
        for n in range(-2, 10):
            slope = gradient(P1[n + OFF - 1], P1[n + OFF])
            scale = 0.25 * INV[n + OFF]
            high, own = divergence_halves([scale * slope[c] for c in range(3)])
            if low is not None:
                e = n - 1
                PN[e + OFF] = P1[e + OFF] + (MD[e + OFF] - 0.25 * (high + low)) * ISC[e + OFF]
            low = own
        for n in range(-1, 9):
            slope = gradient(PN[n + OFF - 1], PN[n + OFF])
            scale = 0.25 * INV[n + OFF]
            for c in range(3):
                z = JAC[c, n + OFF] - scale * slope[c]
                Z[c, n + OFF] = z
                if 0 <= n < 8:
                    ZS[j, c, n] = z[0:EDGE]
            if 0 <= n < 8:
                ZS[j, 3, n] = PN[n + OFF, 0:EDGE]
        for c in range(3):
            low = forward_modes(Z[c, OFF - 1])
            before = None
            for e in range(-1, 8):
                high = forward_modes(Z[c, e + 1 + OFF])
                modes = element_modes(low, high)
                place = (0, 2, 4)[c]
                if e >= 0:
                    own = modes[place][0:EDGE]
                    DIV[e] = own if c == 0 else DIV[e] + own
                weighted = list(weigh(modes, VM[e + OFF]))
                weighted[place] = weighted[place] + 0.25 * PN[e + OFF]
                after = from_after(weighted)
                if before is not None:
                    free = (node_row * plane_flag(e, 1))[0:EDGE]
                    w = back_to_nodes(before, after)[0:EDGE] * free
                    W[j, c, e] = w
                    q = w - Q[c, e]
                    Q[c, e] = q
                    X[j + 1, c, e + OFF, 0:EDGE] = q * INV[e + OFF, 0:EDGE]
                before = from_before(weighted)
                low = high
        for e in range(8):
            w = 0.25 * DIV[e]
            W[j, 3, e] = w
            q = w - Q[3, e]
            Q[3, e] = q
            X[j + 1, 3, e + OFF, 0:EDGE] = q

        @pl.when(j < KRYLOV - 1)
        def _():
            later = step_copies(j + 1)
            for name in FIRST:
                later[name]().start()

        def inner(other):
            total = None
            for n in range(8):
                for c in range(4):
                    term = W[j, c, n] * other(c, n)
                    total = term if total is None else total + term
            return fold(total)

        DOT[j * 4 + 3] = inner(lambda c, n: Q0[c, n])

        @pl.loop(0, j + 1)
        def _(k):
            DOT[j * 4 + k] = inner(lambda c, n: W[k, c, n])

    order = [(0, 0), (1, 0), (2, 0), (1, 1), (2, 1), (2, 2), (0, 3), (1, 3), (2, 3)]
    rows16 = lax.broadcasted_iota(jnp.int32, (16, 128), 0)
    stacked = jnp.zeros((16, 128), jnp.float32)
    for place, (a, b) in enumerate(order):
        line = jnp.sum(DOT[a * 4 + b], axis=0, keepdims=True)
        stacked = jnp.where(rows16 == place, line, stacked)
    folded = stacked + pltpu.roll(stacked, 64, 1)
    left = lax.broadcasted_iota(jnp.int32, (8, 128), 1) < 64
    tile = jnp.where(left, folded[0:8], folded[8:16])

    def reduce(tile, stage, buffer, me, peer, send, recv):
        buffer[me] = tile
        PART[stage] = tile

        def copy(i):
            return remote(PART.at[stage], buffer.at[me], send.at[i], recv.at[me], peer(i))

        def arrival(i):
            other = lax.rem(me + i, 16)
            return remote(PART.at[stage], buffer.at[other], send.at[i], recv.at[other], peer(i))

        @pl.loop(1, 16)
        def _(i):
            copy(i).start()

        @pl.loop(1, 16)
        def _(i):
            arrival(i).wait_recv()

        @pl.loop(1, 16)
        def _(i):
            copy(i).wait_send()

        total = buffer[0]
        for i in range(1, 16):
            total = total + buffer[i]
        return total

    tile = reduce(tile, 0, ARA, across, a_peer, a_send, a_recv)
    tile = reduce(tile, 1, ARB, along, b_peer, b_send, b_recv)
    sums_a = jnp.sum(jnp.where(left, tile, 0.0), axis=1, keepdims=True)
    sums_b = jnp.sum(jnp.where(left, 0.0, tile), axis=1, keepdims=True)
    a00, a10, a20, a11, a21, a22, b0, b1 = [sums_a[i : i + 1] for i in range(8)]
    b2 = sums_b[0:1]
    l00 = jnp.sqrt(a00)
    l10 = a10 / l00
    l20 = a20 / l00
    l11 = jnp.sqrt(a11 - l10 * l10)
    l21 = (a21 - l20 * l10) / l11
    l22 = jnp.sqrt(a22 - l20 * l20 - l21 * l21)
    y0 = b0 / l00
    y1 = (b1 - l10 * y0) / l11
    y2 = (b2 - l20 * y0 - l21 * y1) / l22
    c2 = y2 / l22
    c1 = (y1 - l21 * c2) / l11
    c0 = (y0 - l10 * c1 - l20 * c2) / l00
    for n in range(8):
        for c in range(4):
            OUT[c, n] = c0 * ZS[0, c, n] + c1 * ZS[1, c, n] + c2 * ZS[2, c, n]

    def back(k):
        return remote(
            OUT.at[:, 2 * k : 2 * k + 2], HOME.at[:, :, rows(my_tile)], out_send.at[k], out_recv.at[my_tile], comes_from[k]
        )

    def arrive(i):
        return remote(
            OUT.at[:, 0:2], HOME.at[:, :, EDGE * i : EDGE * i + EDGE], out_send.at[0], out_recv.at[i], goes_to[i]
        )

    def stay():
        return pltpu.make_async_copy(
            OUT.at[:, pl.ds(2 * my_k, 2)], HOME.at[:, :, rows(my_tile)], out_local.at[0]
        )

    pl.when(home)(lambda: stay().start())
    for k in range(4):
        pl.when(jnp.logical_not(is_me(comes_from[k])))(lambda k=k: back(k).start())

    for copy in setup.values():
        copy().wait_send()

    @pl.loop(0, KRYLOV)
    def _(j):
        for copy in step_copies(j).values():
            copy().wait_send()

    for t in range(3):
        for i in range(4):
            pl.when(jnp.logical_not(is_me(goes_to[i])))(lambda t=t, i=i: give(t, i).wait_send())

    pl.when(home)(lambda: stay().wait())
    for i in range(4):
        pl.when(jnp.logical_not(is_me(goes_to[i])))(lambda i=i: arrive(i).wait_recv())
    for c in range(3):
        vel_ref[c] = HOME[c]
    pre_ref[...] = HOME[3]
    for k in range(4):
        pl.when(jnp.logical_not(is_me(comes_from[k])))(lambda k=k: back(k).wait_send())


def body(forcing, source, viscosity):
    f32 = jnp.float32
    vmem = lambda *shape: pltpu.VMEM(shape, f32)
    dma = lambda *shape: pltpu.SemaphoreType.DMA(shape)
    K = KRYLOV
    return pl.pallas_call(
        kernel,
        out_shape=(
            jax.ShapeDtypeStruct((3, 2, 32, LANES), f32),
            jax.ShapeDtypeStruct((2, 32, LANES), f32),
        ),
        in_specs=[pl.BlockSpec(memory_space=pl.ANY)] * 3,
        out_specs=(pl.BlockSpec(memory_space=pltpu.VMEM), pl.BlockSpec(memory_space=pltpu.VMEM)),
        scratch_shapes=[
            vmem(WIDE, WIDE, LANES),
            vmem(WIDE, WIDE, LANES),
            vmem(K + 1, 4, WIDE, WIDE, LANES),
            vmem(WIDE, WIDE, LANES),
            vmem(WIDE, WIDE, LANES),
            vmem(3, WIDE, WIDE, LANES),
            vmem(3, 2, 4, WIDE, LANES),
            vmem(WIDE, WIDE, LANES),
            vmem(WIDE, WIDE, LANES),
            vmem(WIDE, WIDE, LANES),
            vmem(3, WIDE, WIDE, LANES),
            vmem(K, 4, EDGE, EDGE, LANES),
            vmem(EDGE, EDGE, LANES),
            vmem(K, 4, EDGE, EDGE, LANES),
            vmem(4, EDGE, EDGE, LANES),
            vmem(4, EDGE, EDGE, LANES),
            vmem(4, EDGE, EDGE, LANES),
            vmem(4, 2, 32, LANES),
            vmem(4 * K, 8, 128),
            vmem(16, 8, 128),
            vmem(16, 8, 128),
            vmem(2, 8, 128),
            dma(3, 4),
            dma(3, 4),
            dma(3),
            dma(4),
            dma(4),
            dma(K, 6),
            dma(K, 6),
            dma(4),
            dma(4),
            dma(1),
            dma(16),
            dma(16),
            dma(16),
            dma(16),
        ],
        compiler_params=pltpu.CompilerParams(
            collective_id=0, has_side_effects=True, vmem_limit_bytes=48 * 1024 * 1024
        ),
        name="stokes_cycle",
    )(forcing, source, viscosity)


def solution(mesh):
    placed = (P(None, "slab", "depth", None), P("slab", "depth", None), P("slab", "depth", None))
    return jax.shard_map(
        body,
        mesh=mesh,
        in_specs=placed,
        out_specs=(P(None, "slab", "depth", None), P("slab", "depth", None)),
        check_vma=False,
    )
```

```python
import jax
import jax.numpy as jnp
from jax import lax
from jax.experimental import pallas as pl
from jax.experimental.pallas import tpu as pltpu
from jax.sharding import PartitionSpec as P

KRYLOV = 3
EDGE = 8
WIDE = 16
OFF = 4
LANES = 256
MESH_ID = pl.DeviceIdType.MESH


def next_z(x):
    return jnp.concatenate([x[:, 128:], pltpu.roll(x[:, :128], 127, 1)], axis=1)


def prev_z(x):
    return jnp.concatenate([pltpu.roll(x[:, 128:], 1, 1), x[:, :128]], axis=1)


def permute(x, matrix):
    return jnp.dot(x, matrix, precision=lax.Precision.HIGHEST, preferred_element_type=jnp.float32)


def next_y(x):
    return pltpu.roll(x, WIDE - 1, 0)


def prev_y(x):
    return pltpu.roll(x, 1, 0)


def forward_modes(u):
    ahead = next_z(u)
    zs = ahead + u
    zd = ahead - u
    zs_ahead = next_y(zs)
    zd_ahead = next_y(zd)
    return zs_ahead + zs, zs_ahead - zs, zd_ahead + zd, zd_ahead - zd


def element_modes(low, high):
    return (
        high[0] - low[0],
        high[1] - low[1],
        high[1] + low[1],
        high[2] - low[2],
        high[2] + low[2],
        high[3] - low[3],
        high[3] + low[3],
    )


def weigh(modes, visc):
    v16 = visc * (1.0 / 16.0)
    v24 = visc * (1.0 / 24.0)
    v48 = visc * (1.0 / 48.0)
    return (
        modes[0] * v16,
        modes[1] * v24,
        modes[2] * v16,
        modes[3] * v24,
        modes[4] * v16,
        modes[5] * v48,
        modes[6] * v24,
    )


def from_before(modes):
    return modes[0], modes[2] + modes[1], modes[4] + modes[3], modes[6] + modes[5]


def from_after(modes):
    return modes[0], modes[2] - modes[1], modes[4] - modes[3], modes[6] - modes[5]


def back_to_nodes(before, after):
    ss = before[0] - after[0]
    ds = before[1] + after[1]
    sd = before[2] + after[2]
    dd = before[3] + after[3]
    zs = (ss - ds) + prev_y(ss + ds)
    zd = (sd - dd) + prev_y(sd + dd)
    return (zs - zd) + prev_z(zs + zd)


def divergence_halves(u):
    x_ahead = next_z(u[0])
    y_ahead = next_z(u[1])
    z_ahead = next_z(u[2])
    zs_x = x_ahead + u[0]
    zs_y = y_ahead + u[1]
    zd_z = z_ahead - u[2]
    ss_x = next_y(zs_x) + zs_x
    rest = (zd_z - zs_y) + next_y(zd_z + zs_y)
    return rest + ss_x, rest - ss_x


def gradient(before, after):
    diff = before - after
    both = before + after
    diff_y = diff + prev_y(diff)
    both_back = prev_y(both)
    sum_y = both + both_back
    dif_y = both_back - both
    return (
        diff_y + prev_z(diff_y),
        dif_y + prev_z(dif_y),
        prev_z(sum_y) - sum_y,
    )


def fold(product):
    return product[:, :128] + product[:, 128:]


def block_of(slab, depth):
    x = lax.rem(slab, 4)
    y = slab // 16
    z = lax.rem(slab // 4, 4) * 2 + depth // 2
    odd = lax.rem(y, 2)
    return y * 4 + x + odd * (3 - 2 * x), z * 2 + lax.rem(depth, 2)


def device_of(across, along):
    y = across // 4
    place = lax.rem(across, 4)
    odd = lax.rem(y, 2)
    x = place + odd * (3 - 2 * place)
    z = along // 2
    return y * 16 + (z // 2) * 4 + x, lax.rem(z, 2) * 2 + lax.rem(along, 2)


def kernel(
    f_hbm, s_hbm, v_hbm, vel_ref, pre_ref,
    RAW, V, VM, X, INV, ISC, JAC, MID, MD, P1, PN, Z, ZS, DIV, W, Q, Q0, OUT, RELAY, HOME, DOT, ARA, ARB, PART,
    in_send, in_recv, in_local, s_send, s_recv, i_send, i_recv, x_send, x_recv, out_send, out_recv, out_local,
    a_send, a_recv, b_send, b_recv,
):
    slab = lax.axis_index("slab")
    depth = lax.axis_index("depth")
    across, along = block_of(slab, depth)
    to_next = device_of(lax.rem(across + 1, 16), along)
    to_prev = device_of(lax.rem(across + 15, 16), along)
    to_up = device_of(across, lax.rem(along + 1, 16))
    to_down = device_of(across, lax.rem(along + 15, 16))

    my_k = lax.rem(slab, 4)
    my_tile = lax.rem(along, 4)
    goes_to = [device_of(slab // 4, depth * 4 + i) for i in range(4)]
    comes_from = [(across * 4 + k, along // 4) for k in range(4)]

    def is_me(device):
        return (device[0] == slab) & (device[1] == depth)

    core = lax.rem(depth, 2)
    x_me = lax.rem(slab, 4)
    y_me = slab // 16
    same_z = slab - x_me - y_me * 16
    same_xy = y_me * 16 + x_me
    a_me = y_me * 4 + x_me
    b_me = along
    a_peers = [(i // 4 * 16 + i % 4 + same_z, depth) for i in range(16)]
    b_peers = [(same_xy + i // 4 * 4, i // 2 % 2 * 2 + i % 2) for i in range(16)]
    x_line = [(slab - x_me + k, depth) for k in range(4)]
    odd = lax.rem(y_me, 2)
    z_home = [(same_xy + 4 * (k + odd * (3 - 2 * k)), along // 4) for k in range(4)]

    barrier = pltpu.get_barrier_semaphore()

    def greet(device):
        pl.semaphore_signal(barrier, inc=1, device_id=device, device_id_type=MESH_ID)

    for device in goes_to + comes_from + a_peers + b_peers:
        greet(device)
    pl.semaphore_wait(barrier, 40)

    def remote(src, dst, send, recv, peer):
        return pltpu.make_async_remote_copy(
            src_ref=src, dst_ref=dst, send_sem=send, recv_sem=recv, device_id=peer, device_id_type=MESH_ID
        )

    def rows(i):
        return pl.ds(pl.multiple_of(i * EDGE, EDGE), EDGE)

    def fields(i, k):
        return (
            (v_hbm.at[:, rows(i)], RAW.at[4, pl.ds(2 * k, 2)]),
            (f_hbm.at[:, :, rows(i)], RAW.at[0:3, pl.ds(2 * k, 2)]),
            (s_hbm.at[:, rows(i)], RAW.at[3, pl.ds(2 * k, 2)]),
        )

    def give(t, i):
        src, dst = fields(i, my_k)[t]
        return remote(src, dst, in_send.at[t, i], in_recv.at[t, my_k], goes_to[i])

    def take(t, k):
        src, dst = fields(0, k)[t]
        return remote(src, dst, in_send.at[t, 0], in_recv.at[t, k], comes_from[k])

    def keep(t):
        src, dst = fields(my_tile, my_k)[t]
        return pltpu.make_async_copy(src, dst, in_local.at[t])

    home = is_me(device_of(slab // 4, depth * 4 + my_tile))
    for t in range(3):
        pl.when(home)(lambda t=t: keep(t).start())
        for i in range(4):
            pl.when(jnp.logical_not(is_me(goes_to[i])))(lambda t=t, i=i: give(t, i).start())

    def taken(t):
        pl.when(home)(lambda: keep(t).wait())
        for k in range(4):
            pl.when(jnp.logical_not(is_me(comes_from[k])))(lambda k=k: take(t, k).wait_recv())

    def setup_copy(k, src, dst, peer):
        return lambda: remote(src, dst, s_send.at[k], s_recv.at[k], peer)

    setup = dict(
        up=setup_copy(0, V.at[4:12, 4:8], V.at[4:12, 12:16], to_up),
        down=setup_copy(1, V.at[4:12, 0:4], V.at[4:12, 8:12], to_down),
        next=setup_copy(2, V.at[8:12], V.at[0:4], to_next),
        prev=setup_copy(3, V.at[4:8], V.at[12:16], to_prev),
    )

    def step_copies(j):
        def copy(k, src, dst, peer):
            return lambda: remote(src, dst, i_send.at[j, k], i_recv.at[j, k], peer)

        return dict(
            up=copy(0, X.at[j, :, 4:12, 4:8], X.at[j, :, 4:12, 12:16], to_up),
            down=copy(1, X.at[j, :, 4:12, 0:4], X.at[j, :, 4:12, 8:12], to_down),
            main_next=copy(2, X.at[j, :, 8:12, 0:8], X.at[j, :, 0:4, 0:8], to_next),
            main_prev=copy(3, X.at[j, :, 4:8, 0:8], X.at[j, :, 12:16, 0:8], to_prev),
            below_next=copy(4, X.at[j, :, 8:12, 12:16], X.at[j, :, 0:4, 12:16], to_next),
            below_prev=copy(5, X.at[j, :, 4:8, 12:16], X.at[j, :, 12:16, 12:16], to_prev),
            above_next=copy(4, X.at[j, :, 8:12, 8:12], X.at[j, :, 0:4, 8:12], to_next),
            above_prev=copy(5, X.at[j, :, 4:8, 8:12], X.at[j, :, 12:16, 8:12], to_prev),
            low_up=copy(6, X.at[j, :, 0:4, 4:8], X.at[j, :, 0:4, 12:16], to_up),
            high_up=copy(7, X.at[j, :, 12:16, 4:8], X.at[j, :, 12:16, 12:16], to_up),
            low_down=copy(6, X.at[j, :, 0:4, 0:4], X.at[j, :, 0:4, 8:12], to_down),
            high_down=copy(7, X.at[j, :, 12:16, 0:4], X.at[j, :, 12:16, 8:12], to_down),
        )

    FIRST = ("up", "down", "main_next", "main_prev")

    place_in = lax.broadcasted_iota(jnp.int32, (LANES, LANES), 0)
    place_out = lax.broadcasted_iota(jnp.int32, (LANES, LANES), 1)
    split = place_in == jnp.where(place_out < 128, 2 * place_out, 2 * place_out - 255)
    split = split.astype(jnp.float32)
    taken(0)
    moved = permute(RAW[4].reshape(64, LANES), split)
    for n in range(8):
        V[n + OFF, 0:EDGE] = moved[8 * n : 8 * n + 8]
    setup["up"]().start()
    setup["down"]().start()

    row = lax.broadcasted_iota(jnp.int32, (WIDE, LANES), 0)
    row = along * EDGE + jnp.where(row < 12, row, row - WIDE)
    element_row = ((row >= 0) & (row < 128)).astype(jnp.float32)
    node_row = ((row >= 1) & (row < 128)).astype(jnp.float32)

    def plane_flag(n, low):
        place = across * EDGE + n
        return ((place >= low) & (place < 128)).astype(jnp.float32)

    setup["up"]().wait_recv()
    setup["down"]().wait_recv()
    setup["next"]().start()
    setup["prev"]().start()

    def inverse_plane(n):
        both = VM[n + OFF - 1] + VM[n + OFF]
        both = both + prev_y(both)
        both = both + prev_z(both)
        free = node_row * plane_flag(n, 1)
        INV[n + OFF] = free * 3.0 / jnp.where(free > 0.0, both, 1.0)

    for n in range(8):
        VM[n + OFF] = V[n + OFF] * (element_row * plane_flag(n, 0))
    for n in range(1, 8):
        inverse_plane(n)
    setup["next"]().wait_recv()
    setup["prev"]().wait_recv()
    for n in (-4, -3, -2, -1, 8, 9, 10, 11):
        VM[n + OFF] = V[n + OFF] * (element_row * plane_flag(n, 0))
    inverse_plane(0)
    taken(1)
    taken(2)
    moved = permute(RAW[0:4].reshape(256, LANES), split)
    for n in range(8):
        free = (node_row * plane_flag(n, 1))[0:EDGE]
        inverse = INV[n + OFF, 0:EDGE]
        for c in range(3):
            q = moved[64 * c + 8 * n : 64 * c + 8 * n + 8] * free
            Q0[c, n] = q
            Q[c, n] = q
            X[0, c, n + OFF, 0:EDGE] = q * inverse
        p = moved[192 + 8 * n : 200 + 8 * n]
        Q0[3, n] = p
        Q[3, n] = p
        X[0, 3, n + OFF, 0:EDGE] = p
    first = step_copies(0)
    for name in FIRST:
        first[name]().start()
    for n in (-3, -2, -1, 8, 9, 10):
        inverse_plane(n)
    for e in range(-3, 10):
        both = INV[e + OFF] + INV[e + OFF + 1]
        both = both + next_y(both)
        both = both + next_z(both)
        there = element_row * plane_flag(e, 0)
        ISC[e + OFF] = there / jnp.where(there > 0.0, 0.1875 * both, 1.0)

    @pl.loop(0, KRYLOV)
    def _(j):
        copies = step_copies(j)
        for name in ("up", "down"):
            copies[name]().wait_recv()
        def on_core(number, *names):
            pl.when(core == number)(lambda: [copies[name]().start() for name in names] and None)

        on_core(0, "below_next", "below_prev")
        on_core(1, "above_next", "above_prev")

        def modes_of(n, c):
            return forward_modes(X[j, c, n + OFF])

        def jacobi(n, c, before, after):
            JAC[c, n + OFF] = 2.0 * X[j, c, n + OFF] - INV[n + OFF] * back_to_nodes(before, after)

        def sweep(first, last, c, before, keep_first, keep_last):
            low = modes_of(first, c)
            for e in range(first, last + 1):
                high = modes_of(e + 1, c)
                weighted = weigh(element_modes(low, high), VM[e + OFF])
                after = from_after(weighted)
                if before is not None:
                    jacobi(e, c, before, after)
                elif keep_first is not None:
                    for m in range(4):
                        MID[c, keep_first, m] = after[m]
                before = from_before(weighted)
                low = high
            if keep_last is not None:
                for m in range(4):
                    MID[c, keep_last, m] = before[m]
            return before

        for c in range(3):
            sweep(0, 6, c, None, 0, 1)
        copies["main_next"]().wait_recv()
        on_core(0, "low_up")
        on_core(1, "low_down")
        copies["main_prev"]().wait_recv()
        on_core(0, "high_up")
        on_core(1, "high_down")

        @pl.when(core == 0)
        def _():
            for name in ("low_down", "high_down", "below_next", "below_prev"):
                copies[name]().wait_recv()

        @pl.when(core == 1)
        def _():
            for name in ("low_up", "high_up", "above_next", "above_prev"):
                copies[name]().wait_recv()

        for c in range(3):
            before = sweep(-4, -1, c, None, None, None)
            jacobi(0, c, before, [MID[c, 0, m] for m in range(4)])
            sweep(7, 10, c, [MID[c, 1, m] for m in range(4)], None, None)

        low = None
        for n in range(-3, 11):
            high, own = divergence_halves([JAC[c, n + OFF] for c in range(3)])
            if low is not None:
                e = n - 1
                defect = 0.25 * (high + low) - X[j, 3, e + OFF]
                MD[e + OFF] = defect
                P1[e + OFF] = defect * ISC[e + OFF]
            low = own
        low = None
        for n in range(-2, 10):
            slope = gradient(P1[n + OFF - 1], P1[n + OFF])
            scale = 0.25 * INV[n + OFF]
            high, own = divergence_halves([scale * slope[c] for c in range(3)])
            if low is not None:
                e = n - 1
                PN[e + OFF] = P1[e + OFF] + (MD[e + OFF] - 0.25 * (high + low)) * ISC[e + OFF]
            low = own
        for n in range(-1, 9):
            slope = gradient(PN[n + OFF - 1], PN[n + OFF])
            scale = 0.25 * INV[n + OFF]
            for c in range(3):
                z = JAC[c, n + OFF] - scale * slope[c]
                Z[c, n + OFF] = z
                if 0 <= n < 8:
                    ZS[j, c, n] = z[0:EDGE]
            if 0 <= n < 8:
                ZS[j, 3, n] = PN[n + OFF, 0:EDGE]
        for c in range(3):
            low = forward_modes(Z[c, OFF - 1])
            before = None
            for e in range(-1, 8):
                high = forward_modes(Z[c, e + 1 + OFF])
                modes = element_modes(low, high)
                place = (0, 2, 4)[c]
                if e >= 0:
                    own = modes[place][0:EDGE]
                    DIV[e] = own if c == 0 else DIV[e] + own
                weighted = list(weigh(modes, VM[e + OFF]))
                weighted[place] = weighted[place] + 0.25 * PN[e + OFF]
                after = from_after(weighted)
                if before is not None:
                    free = (node_row * plane_flag(e, 1))[0:EDGE]
                    w = back_to_nodes(before, after)[0:EDGE] * free
                    W[j, c, e] = w
                    q = w - Q[c, e]
                    Q[c, e] = q
                    X[j + 1, c, e + OFF, 0:EDGE] = q * INV[e + OFF, 0:EDGE]
                before = from_before(weighted)
                low = high
        for e in range(8):
            w = 0.25 * DIV[e]
            W[j, 3, e] = w
            q = w - Q[3, e]
            Q[3, e] = q
            X[j + 1, 3, e + OFF, 0:EDGE] = q

        @pl.when(j < KRYLOV - 1)
        def _():
            later = step_copies(j + 1)
            for name in FIRST:
                later[name]().start()

        def inner(other):
            total = None
            for n in range(8):
                for c in range(4):
                    term = W[j, c, n] * other(c, n)
                    total = term if total is None else total + term
            return fold(total)

        DOT[j * 4 + 3] = inner(lambda c, n: Q0[c, n])

        @pl.loop(0, j + 1)
        def _(k):
            DOT[j * 4 + k] = inner(lambda c, n: W[k, c, n])

    order = [(0, 0), (1, 0), (2, 0), (1, 1), (2, 1), (2, 2), (0, 3), (1, 3), (2, 3)]
    rows16 = lax.broadcasted_iota(jnp.int32, (16, 128), 0)
    stacked = jnp.zeros((16, 128), jnp.float32)
    for place, (a, b) in enumerate(order):
        line = jnp.sum(DOT[a * 4 + b], axis=0, keepdims=True)
        stacked = jnp.where(rows16 == place, line, stacked)
    folded = stacked + pltpu.roll(stacked, 64, 1)
    left = lax.broadcasted_iota(jnp.int32, (8, 128), 1) < 64
    tile = jnp.where(left, folded[0:8], folded[8:16])

    def reduce(tile, stage, buffer, me, peers, send, recv):
        PART[stage] = tile

        def copy(i, slot):
            return remote(PART.at[stage], buffer.at[slot], send.at[i], recv.at[slot], peers[i])

        for i in range(16):
            pl.when(me != i)(lambda i=i: copy(i, me).start())
        buffer[me] = tile
        for i in range(16):
            pl.when(me != i)(lambda i=i: copy(i, i).wait_recv())
        total = buffer[0]
        for i in range(1, 16):
            total = total + buffer[i]
        for i in range(16):
            pl.when(me != i)(lambda i=i: copy(i, me).wait_send())
        return total

    tile = reduce(tile, 0, ARA, a_me, a_peers, a_send, a_recv)
    tile = reduce(tile, 1, ARB, b_me, b_peers, b_send, b_recv)
    sums_a = jnp.sum(jnp.where(left, tile, 0.0), axis=1, keepdims=True)
    sums_b = jnp.sum(jnp.where(left, 0.0, tile), axis=1, keepdims=True)
    a00, a10, a20, a11, a21, a22, b0, b1 = [sums_a[i : i + 1] for i in range(8)]
    b2 = sums_b[0:1]
    l00 = jnp.sqrt(a00)
    l10 = a10 / l00
    l20 = a20 / l00
    l11 = jnp.sqrt(a11 - l10 * l10)
    l21 = (a21 - l20 * l10) / l11
    l22 = jnp.sqrt(a22 - l20 * l20 - l21 * l21)
    y0 = b0 / l00
    y1 = (b1 - l10 * y0) / l11
    y2 = (b2 - l20 * y0 - l21 * y1) / l22
    c2 = y2 / l22
    c1 = (y1 - l21 * c2) / l11
    c0 = (y0 - l10 * c1 - l20 * c2) / l00
    join = place_out == jnp.where(place_in < 128, 2 * place_in, 2 * place_in - 255)
    join = join.astype(jnp.float32)
    for c in range(4):
        mixed = c0 * ZS[0, c] + c1 * ZS[1, c] + c2 * ZS[2, c]
        OUT[c] = permute(mixed.reshape(64, LANES), join).reshape(EDGE, EDGE, LANES)

    def along_x(k, slot):
        return remote(OUT.at[:, 2 * k : 2 * k + 2], RELAY.at[slot], x_send.at[k], x_recv.at[slot], x_line[k])

    for k in range(4):
        pl.when(x_me != k)(lambda k=k: along_x(k, x_me).start())
    RELAY[x_me] = OUT[:, pl.ds(2 * x_me, 2)]

    def back(k):
        return remote(RELAY.at[k], HOME.at[:, :, rows(my_tile)], out_send.at[k], out_recv.at[my_tile], z_home[k])

    def arrive(i, holder):
        return remote(RELAY.at[0], HOME.at[:, :, EDGE * i : EDGE * i + EDGE], out_send.at[0], out_recv.at[i], holder)

    def b_peer_of(i):
        tile = depth * 4 + i
        return same_xy + tile // 4 * 4, lax.rem(tile // 2, 2) * 2 + lax.rem(tile, 2)

    def stay(k):
        return pltpu.make_async_copy(RELAY.at[k], HOME.at[:, :, rows(my_tile)], out_local.at[0])

    for k in range(4):
        pl.when(x_me != k)(lambda k=k: along_x(k, k).wait_recv())
        pl.when(is_me(z_home[k]))(lambda k=k: stay(k).start())
        pl.when(jnp.logical_not(is_me(z_home[k])))(lambda k=k: back(k).start())

    for copy in setup.values():
        copy().wait_send()

    @pl.loop(0, KRYLOV)
    def _(j):
        copies = step_copies(j)
        for name in FIRST:
            copies[name]().wait_send()

        @pl.when(core == 0)
        def _():
            for name in ("low_up", "high_up", "below_next", "below_prev"):
                copies[name]().wait_send()

        @pl.when(core == 1)
        def _():
            for name in ("low_down", "high_down", "above_next", "above_prev"):
                copies[name]().wait_send()

    for t in range(3):
        for i in range(4):
            pl.when(jnp.logical_not(is_me(goes_to[i])))(lambda t=t, i=i: give(t, i).wait_send())

    for i in range(4):
        holder = b_peer_of(i)
        pl.when(is_me(holder))(lambda: stay(0).wait())
        pl.when(jnp.logical_not(is_me(holder)))(lambda i=i, holder=holder: arrive(i, holder).wait_recv())
    for c in range(3):
        vel_ref[c] = HOME[c]
    pre_ref[...] = HOME[3]
    for k in range(4):
        pl.when(x_me != k)(lambda k=k: along_x(k, x_me).wait_send())
        pl.when(jnp.logical_not(is_me(z_home[k])))(lambda k=k: back(k).wait_send())


def body(forcing, source, viscosity):
    f32 = jnp.float32
    vmem = lambda *shape: pltpu.VMEM(shape, f32)
    dma = lambda *shape: pltpu.SemaphoreType.DMA(shape)
    K = KRYLOV
    return pl.pallas_call(
        kernel,
        out_shape=(
            jax.ShapeDtypeStruct((3, 2, 32, LANES), f32),
            jax.ShapeDtypeStruct((2, 32, LANES), f32),
        ),
        in_specs=[pl.BlockSpec(memory_space=pl.ANY)] * 3,
        out_specs=(pl.BlockSpec(memory_space=pltpu.VMEM), pl.BlockSpec(memory_space=pltpu.VMEM)),
        scratch_shapes=[
            vmem(5, EDGE, EDGE, LANES),
            vmem(WIDE, WIDE, LANES),
            vmem(WIDE, WIDE, LANES),
            vmem(K + 1, 4, WIDE, WIDE, LANES),
            vmem(WIDE, WIDE, LANES),
            vmem(WIDE, WIDE, LANES),
            vmem(3, WIDE, WIDE, LANES),
            vmem(3, 2, 4, WIDE, LANES),
            vmem(WIDE, WIDE, LANES),
            vmem(WIDE, WIDE, LANES),
            vmem(WIDE, WIDE, LANES),
            vmem(3, WIDE, WIDE, LANES),
            vmem(K, 4, EDGE, EDGE, LANES),
            vmem(EDGE, EDGE, LANES),
            vmem(K, 4, EDGE, EDGE, LANES),
            vmem(4, EDGE, EDGE, LANES),
            vmem(4, EDGE, EDGE, LANES),
            vmem(4, EDGE, EDGE, LANES),
            vmem(4, 4, 2, EDGE, LANES),
            vmem(4, 2, 32, LANES),
            vmem(4 * K, 8, 128),
            vmem(16, 8, 128),
            vmem(16, 8, 128),
            vmem(2, 8, 128),
            dma(3, 4),
            dma(3, 4),
            dma(3),
            dma(4),
            dma(4),
            dma(K, 8),
            dma(K, 8),
            dma(4),
            dma(4),
            dma(4),
            dma(4),
            dma(1),
            dma(16),
            dma(16),
            dma(16),
            dma(16),
        ],
        compiler_params=pltpu.CompilerParams(
            collective_id=0, has_side_effects=True, vmem_limit_bytes=60 * 1024 * 1024
        ),
        name="stokes_cycle",
    )(forcing, source, viscosity)


def solution(mesh):
    placed = (P(None, "slab", "depth", None), P("slab", "depth", None), P("slab", "depth", None))
    return jax.shard_map(
        body,
        mesh=mesh,
        in_specs=placed,
        out_specs=(P(None, "slab", "depth", None), P("slab", "depth", None)),
        check_vma=False,
    )
```

```python
import jax
import jax.numpy as jnp
from jax import lax
from jax.experimental import pallas as pl
from jax.experimental.pallas import tpu as pltpu
from jax.sharding import PartitionSpec as P

KRYLOV = 3
EDGE = 8
WIDE = 16
OFF = 4
LANES = 256
MESH_ID = pl.DeviceIdType.MESH


def next_z(x):
    return jnp.concatenate([x[:, 128:], pltpu.roll(x[:, :128], 127, 1)], axis=1)


def prev_z(x):
    return jnp.concatenate([pltpu.roll(x[:, 128:], 1, 1), x[:, :128]], axis=1)


def permute(x, matrix):
    return jnp.dot(x, matrix, precision=lax.Precision.HIGHEST, preferred_element_type=jnp.float32)


def next_y(x):
    return pltpu.roll(x, WIDE - 1, 0)


def prev_y(x):
    return pltpu.roll(x, 1, 0)


def forward_modes(u):
    ahead = next_z(u)
    zs = ahead + u
    zd = ahead - u
    zs_ahead = next_y(zs)
    zd_ahead = next_y(zd)
    return zs_ahead + zs, zs_ahead - zs, zd_ahead + zd, zd_ahead - zd


def element_modes(low, high):
    return (
        high[0] - low[0],
        high[1] - low[1],
        high[1] + low[1],
        high[2] - low[2],
        high[2] + low[2],
        high[3] - low[3],
        high[3] + low[3],
    )


def weigh(modes, visc):
    v16 = visc * (1.0 / 16.0)
    v24 = visc * (1.0 / 24.0)
    v48 = visc * (1.0 / 48.0)
    return (
        modes[0] * v16,
        modes[1] * v24,
        modes[2] * v16,
        modes[3] * v24,
        modes[4] * v16,
        modes[5] * v48,
        modes[6] * v24,
    )


def from_before(modes):
    return modes[0], modes[2] + modes[1], modes[4] + modes[3], modes[6] + modes[5]


def from_after(modes):
    return modes[0], modes[2] - modes[1], modes[4] - modes[3], modes[6] - modes[5]


def back_to_nodes(before, after):
    ss = before[0] - after[0]
    ds = before[1] + after[1]
    sd = before[2] + after[2]
    dd = before[3] + after[3]
    zs = (ss - ds) + prev_y(ss + ds)
    zd = (sd - dd) + prev_y(sd + dd)
    return (zs - zd) + prev_z(zs + zd)


def divergence_halves(u):
    x_ahead = next_z(u[0])
    y_ahead = next_z(u[1])
    z_ahead = next_z(u[2])
    zs_x = x_ahead + u[0]
    zs_y = y_ahead + u[1]
    zd_z = z_ahead - u[2]
    ss_x = next_y(zs_x) + zs_x
    rest = (zd_z - zs_y) + next_y(zd_z + zs_y)
    return rest + ss_x, rest - ss_x


def gradient(before, after):
    diff = before - after
    both = before + after
    diff_y = diff + prev_y(diff)
    both_back = prev_y(both)
    sum_y = both + both_back
    dif_y = both_back - both
    return (
        diff_y + prev_z(diff_y),
        dif_y + prev_z(dif_y),
        prev_z(sum_y) - sum_y,
    )


def fold(product):
    return product[:, :128] + product[:, 128:]


def block_of(slab, depth):
    x = lax.rem(slab, 4)
    y = slab // 16
    z = lax.rem(slab // 4, 4) * 2 + depth // 2
    odd = lax.rem(y, 2)
    return y * 4 + x + odd * (3 - 2 * x), z * 2 + lax.rem(depth, 2)


def device_of(across, along):
    y = across // 4
    place = lax.rem(across, 4)
    odd = lax.rem(y, 2)
    x = place + odd * (3 - 2 * place)
    z = along // 2
    return y * 16 + (z // 2) * 4 + x, lax.rem(z, 2) * 2 + lax.rem(along, 2)


def kernel(
    f_hbm, s_hbm, v_hbm, vel_ref, pre_ref,
    RAW, V, VM, X, INV, ISC, JAC, MID, MD, P1, PN, Z, ZS, DIV, W, Q, Q0, OUT, RELAY, HOME, DOT, ARA, ARB, PART,
    in_send, in_recv, in_local, s_send, s_recv, i_send, i_recv, x_send, x_recv, out_send, out_recv, out_local,
    a_send, a_recv, b_send, b_recv,
):
    slab = lax.axis_index("slab")
    depth = lax.axis_index("depth")
    across, along = block_of(slab, depth)
    has = dict(next=across < 15, prev=across > 0, up=along < 15, down=along > 0)
    opposite = dict(next="prev", prev="next", up="down", down="up")
    to_next = device_of(lax.rem(across + 1, 16), along)
    to_prev = device_of(lax.rem(across + 15, 16), along)
    to_up = device_of(across, lax.rem(along + 1, 16))
    to_down = device_of(across, lax.rem(along + 15, 16))

    my_k = lax.rem(slab, 4)
    my_tile = lax.rem(along, 4)
    goes_to = [device_of(slab // 4, depth * 4 + i) for i in range(4)]
    comes_from = [(across * 4 + k, along // 4) for k in range(4)]

    def is_me(device):
        return (device[0] == slab) & (device[1] == depth)

    core = lax.rem(depth, 2)
    x_me = lax.rem(slab, 4)
    y_me = slab // 16
    same_z = slab - x_me - y_me * 16
    same_xy = y_me * 16 + x_me
    a_me = y_me * 4 + x_me
    b_me = along
    a_peers = [(i // 4 * 16 + i % 4 + same_z, depth) for i in range(16)]
    b_peers = [(same_xy + i // 4 * 4, i // 2 % 2 * 2 + i % 2) for i in range(16)]
    x_line = [(slab - x_me + k, depth) for k in range(4)]
    odd = lax.rem(y_me, 2)
    z_home = [(same_xy + 4 * (k + odd * (3 - 2 * k)), along // 4) for k in range(4)]

    barrier = pltpu.get_barrier_semaphore()

    def greet(device):
        pl.semaphore_signal(barrier, inc=1, device_id=device, device_id_type=MESH_ID)

    zeros = jnp.zeros((4, WIDE, LANES), jnp.float32)
    for name, place in (("prev", 0), ("next", 12)):

        @pl.when(jnp.logical_not(has[name]))
        def _(place=place):
            V[place : place + 4] = zeros
            for j in range(KRYLOV):
                for c in range(4):
                    X[j, c, place : place + 4] = zeros

    zeros = jnp.zeros((WIDE, 4, LANES), jnp.float32)
    for name, place in (("down", 12), ("up", 8)):

        @pl.when(jnp.logical_not(has[name]))
        def _(place=place):
            V[:, place : place + 4] = zeros
            for j in range(KRYLOV):
                for c in range(4):
                    X[j, c, :, place : place + 4] = zeros

    for device in goes_to + comes_from + a_peers + b_peers:
        greet(device)
    pl.semaphore_wait(barrier, 40)

    def remote(src, dst, send, recv, peer):
        return pltpu.make_async_remote_copy(
            src_ref=src, dst_ref=dst, send_sem=send, recv_sem=recv, device_id=peer, device_id_type=MESH_ID
        )

    def rows(i):
        return pl.ds(pl.multiple_of(i * EDGE, EDGE), EDGE)

    def fields(i, k):
        return (
            (v_hbm.at[:, rows(i)], RAW.at[4, pl.ds(2 * k, 2)]),
            (f_hbm.at[:, :, rows(i)], RAW.at[0:3, pl.ds(2 * k, 2)]),
            (s_hbm.at[:, rows(i)], RAW.at[3, pl.ds(2 * k, 2)]),
        )

    def give(t, i):
        src, dst = fields(i, my_k)[t]
        return remote(src, dst, in_send.at[t, i], in_recv.at[t, my_k], goes_to[i])

    def take(t, k):
        src, dst = fields(0, k)[t]
        return remote(src, dst, in_send.at[t, 0], in_recv.at[t, k], comes_from[k])

    def keep(t):
        src, dst = fields(my_tile, my_k)[t]
        return pltpu.make_async_copy(src, dst, in_local.at[t])

    home = is_me(device_of(slab // 4, depth * 4 + my_tile))
    for t in range(3):
        pl.when(home)(lambda t=t: keep(t).start())
        for i in range(4):
            pl.when(jnp.logical_not(is_me(goes_to[i])))(lambda t=t, i=i: give(t, i).start())

    def taken(t):
        pl.when(home)(lambda: keep(t).wait())
        for k in range(4):
            pl.when(jnp.logical_not(is_me(comes_from[k])))(lambda k=k: take(t, k).wait_recv())

    def start(copies, *names):
        for name in names:
            pl.when(has[name.split("_")[-1]])(lambda name=name: copies[name]().start())

    def received(copies, *names):
        for name in names:
            pl.when(has[opposite[name.split("_")[-1]]])(lambda name=name: copies[name]().wait_recv())

    def sent(copies, *names):
        for name in names:
            pl.when(has[name.split("_")[-1]])(lambda name=name: copies[name]().wait_send())

    def setup_copy(k, src, dst, peer):
        return lambda: remote(src, dst, s_send.at[k], s_recv.at[k], peer)

    setup = dict(
        up=setup_copy(0, V.at[4:12, 4:8], V.at[4:12, 12:16], to_up),
        down=setup_copy(1, V.at[4:12, 0:4], V.at[4:12, 8:12], to_down),
        next=setup_copy(2, V.at[8:12], V.at[0:4], to_next),
        prev=setup_copy(3, V.at[4:8], V.at[12:16], to_prev),
    )

    def step_copies(j):
        def copy(k, src, dst, peer):
            return lambda: remote(src, dst, i_send.at[j, k], i_recv.at[j, k], peer)

        return dict(
            up=copy(0, X.at[j, :, 4:12, 4:8], X.at[j, :, 4:12, 12:16], to_up),
            down=copy(1, X.at[j, :, 4:12, 0:4], X.at[j, :, 4:12, 8:12], to_down),
            upper_next=copy(2, X.at[j, :, 8:12, 4:8], X.at[j, :, 0:4, 4:8], to_next),
            upper_prev=copy(3, X.at[j, :, 4:8, 4:8], X.at[j, :, 12:16, 4:8], to_prev),
            lower_next=copy(8, X.at[j, :, 8:12, 0:4], X.at[j, :, 0:4, 0:4], to_next),
            lower_prev=copy(9, X.at[j, :, 4:8, 0:4], X.at[j, :, 12:16, 0:4], to_prev),
            below_next=copy(4, X.at[j, :, 8:12, 12:16], X.at[j, :, 0:4, 12:16], to_next),
            below_prev=copy(5, X.at[j, :, 4:8, 12:16], X.at[j, :, 12:16, 12:16], to_prev),
            above_next=copy(4, X.at[j, :, 8:12, 8:12], X.at[j, :, 0:4, 8:12], to_next),
            above_prev=copy(5, X.at[j, :, 4:8, 8:12], X.at[j, :, 12:16, 8:12], to_prev),
            low_up=copy(6, X.at[j, :, 0:4, 4:8], X.at[j, :, 0:4, 12:16], to_up),
            high_up=copy(7, X.at[j, :, 12:16, 4:8], X.at[j, :, 12:16, 12:16], to_up),
            low_down=copy(6, X.at[j, :, 0:4, 0:4], X.at[j, :, 0:4, 8:12], to_down),
            high_down=copy(7, X.at[j, :, 12:16, 0:4], X.at[j, :, 12:16, 8:12], to_down),
        )

    UPPER = ("upper_next", "upper_prev")
    LOWER = ("lower_next", "lower_prev")
    ROWS_0 = ("low_up", "high_up", "below_next", "below_prev")
    ROWS_1 = ("low_down", "high_down", "above_next", "above_prev")

    def on_core(number, action, copies, *names):
        pl.when(core == number)(lambda: action(copies, *names))

    def begin(j):
        copies = step_copies(j)
        start(copies, "up", "down")
        on_core(0, start, copies, *UPPER, *LOWER)
        on_core(1, start, copies, *LOWER, *UPPER)

    place_in = lax.broadcasted_iota(jnp.int32, (LANES, LANES), 0)
    place_out = lax.broadcasted_iota(jnp.int32, (LANES, LANES), 1)
    split = place_in == jnp.where(place_out < 128, 2 * place_out, 2 * place_out - 255)
    split = split.astype(jnp.float32)
    taken(0)
    moved = permute(RAW[4].reshape(64, LANES), split)
    for n in range(8):
        V[n + OFF, 0:EDGE] = moved[8 * n : 8 * n + 8]
    start(setup, "up")
    start(setup, "down")

    row = lax.broadcasted_iota(jnp.int32, (WIDE, LANES), 0)
    row = along * EDGE + jnp.where(row < 12, row, row - WIDE)
    element_row = ((row >= 0) & (row < 128)).astype(jnp.float32)
    node_row = ((row >= 1) & (row < 128)).astype(jnp.float32)

    def plane_flag(n, low):
        place = across * EDGE + n
        return ((place >= low) & (place < 128)).astype(jnp.float32)

    received(setup, "up")
    received(setup, "down")
    start(setup, "next")
    start(setup, "prev")

    def inverse_plane(n):
        both = VM[n + OFF - 1] + VM[n + OFF]
        both = both + prev_y(both)
        both = both + prev_z(both)
        free = node_row * plane_flag(n, 1)
        INV[n + OFF] = free * 3.0 / jnp.where(free > 0.0, both, 1.0)

    for n in range(8):
        VM[n + OFF] = V[n + OFF] * (element_row * plane_flag(n, 0))
    for n in range(1, 8):
        inverse_plane(n)
    received(setup, "next")
    received(setup, "prev")
    for n in (-4, -3, -2, -1, 8, 9, 10, 11):
        VM[n + OFF] = V[n + OFF] * (element_row * plane_flag(n, 0))
    inverse_plane(0)
    taken(1)
    taken(2)
    moved = permute(RAW[0:4].reshape(256, LANES), split)
    for n in range(8):
        free = (node_row * plane_flag(n, 1))[0:EDGE]
        inverse = INV[n + OFF, 0:EDGE]
        for c in range(3):
            q = moved[64 * c + 8 * n : 64 * c + 8 * n + 8] * free
            Q0[c, n] = q
            Q[c, n] = q
            X[0, c, n + OFF, 0:EDGE] = q * inverse
        p = moved[192 + 8 * n : 200 + 8 * n]
        Q0[3, n] = p
        Q[3, n] = p
        X[0, 3, n + OFF, 0:EDGE] = p
    begin(0)
    for n in (-3, -2, -1, 8, 9, 10):
        inverse_plane(n)
    for e in range(-3, 10):
        both = INV[e + OFF] + INV[e + OFF + 1]
        both = both + next_y(both)
        both = both + next_z(both)
        there = element_row * plane_flag(e, 0)
        ISC[e + OFF] = there / jnp.where(there > 0.0, 0.1875 * both, 1.0)

    def along_x(j, k, slot):
        return remote(ZS.at[j, :, 2 * k : 2 * k + 2], RELAY.at[j, slot], x_send.at[j, k], x_recv.at[j, slot], x_line[k])

    def x_begin(j):
        for k in range(4):
            pl.when(x_me != k)(lambda k=k: along_x(j, k, x_me).start())
        RELAY[j, x_me] = ZS[j, :, pl.ds(2 * x_me, 2)]

    @pl.loop(0, KRYLOV)
    def _(j):
        copies = step_copies(j)
        received(copies, "up", "down")
        on_core(0, start, copies, "below_next", "below_prev")
        on_core(1, start, copies, "above_next", "above_prev")

        def modes_of(n, c):
            return forward_modes(X[j, c, n + OFF])

        def jacobi(n, c, before, after):
            JAC[c, n + OFF] = 2.0 * X[j, c, n + OFF] - INV[n + OFF] * back_to_nodes(before, after)

        def sweep(first, last, c, before, keep_first, keep_last):
            low = modes_of(first, c)
            for e in range(first, last + 1):
                high = modes_of(e + 1, c)
                weighted = weigh(element_modes(low, high), VM[e + OFF])
                after = from_after(weighted)
                if before is not None:
                    jacobi(e, c, before, after)
                elif keep_first is not None:
                    for m in range(4):
                        MID[c, keep_first, m] = after[m]
                before = from_before(weighted)
                low = high
            if keep_last is not None:
                for m in range(4):
                    MID[c, keep_last, m] = before[m]
            return before

        for c in range(3):
            sweep(0, 6, c, None, 0, 1)
        def pass_on(names, others, ahead):
            received(copies, names[0])
            pl.when(has["prev"])(lambda: start(copies, others[0]))
            received(copies, names[1])
            pl.when(has["next"])(lambda: start(copies, others[1]))
            received(copies, *ahead)

        on_core(0, lambda c: pass_on(UPPER, ROWS_0[:2], LOWER), copies)
        on_core(1, lambda c: pass_on(LOWER, ROWS_1[:2], UPPER), copies)

        def corners(here, theirs):
            pl.when(has["prev"])(lambda: received(copies, theirs[0]))
            pl.when(has["next"])(lambda: received(copies, theirs[1]))
            received(copies, *here[2:])

        on_core(0, lambda c: corners(ROWS_0, ROWS_1), copies)
        on_core(1, lambda c: corners(ROWS_1, ROWS_0), copies)

        @pl.when(j == 1)
        def _():
            x_begin(0)

        @pl.when(j == 2)
        def _():
            x_begin(1)

        for c in range(3):
            before = sweep(-4, -1, c, None, None, None)
            jacobi(0, c, before, [MID[c, 0, m] for m in range(4)])
            sweep(7, 10, c, [MID[c, 1, m] for m in range(4)], None, None)

        low = None
        for n in range(-3, 11):
            high, own = divergence_halves([JAC[c, n + OFF] for c in range(3)])
            if low is not None:
                e = n - 1
                defect = 0.25 * (high + low) - X[j, 3, e + OFF]
                MD[e + OFF] = defect
                P1[e + OFF] = defect * ISC[e + OFF]
            low = own
        low = None
        for n in range(-2, 10):
            slope = gradient(P1[n + OFF - 1], P1[n + OFF])
            scale = 0.25 * INV[n + OFF]
            high, own = divergence_halves([scale * slope[c] for c in range(3)])
            if low is not None:
                e = n - 1
                PN[e + OFF] = P1[e + OFF] + (MD[e + OFF] - 0.25 * (high + low)) * ISC[e + OFF]
            low = own
        for n in range(-1, 9):
            slope = gradient(PN[n + OFF - 1], PN[n + OFF])
            scale = 0.25 * INV[n + OFF]
            for c in range(3):
                z = JAC[c, n + OFF] - scale * slope[c]
                Z[c, n + OFF] = z
                if 0 <= n < 8:
                    ZS[j, c, n] = z[0:EDGE]
            if 0 <= n < 8:
                ZS[j, 3, n] = PN[n + OFF, 0:EDGE]
        @pl.when(j == 2)
        def _():
            x_begin(2)

        for c in range(3):
            low = forward_modes(Z[c, OFF - 1])
            before = None
            for e in range(-1, 8):
                high = forward_modes(Z[c, e + 1 + OFF])
                modes = element_modes(low, high)
                place = (0, 2, 4)[c]
                if e >= 0:
                    own = modes[place][0:EDGE]
                    DIV[e] = own if c == 0 else DIV[e] + own
                weighted = list(weigh(modes, VM[e + OFF]))
                weighted[place] = weighted[place] + 0.25 * PN[e + OFF]
                after = from_after(weighted)
                if before is not None:
                    free = (node_row * plane_flag(e, 1))[0:EDGE]
                    w = back_to_nodes(before, after)[0:EDGE] * free
                    W[j, c, e] = w
                    q = w - Q[c, e]
                    Q[c, e] = q
                    X[j + 1, c, e + OFF, 0:EDGE] = q * INV[e + OFF, 0:EDGE]
                before = from_before(weighted)
                low = high
        for e in range(8):
            w = 0.25 * DIV[e]
            W[j, 3, e] = w
            q = w - Q[3, e]
            Q[3, e] = q
            X[j + 1, 3, e + OFF, 0:EDGE] = q

        @pl.when(j < KRYLOV - 1)
        def _():
            begin(j + 1)

        def inner(other):
            total = None
            for n in range(8):
                for c in range(4):
                    term = W[j, c, n] * other(c, n)
                    total = term if total is None else total + term
            return fold(total)

        DOT[j * 4 + 3] = inner(lambda c, n: Q0[c, n])

        @pl.loop(0, j + 1)
        def _(k):
            DOT[j * 4 + k] = inner(lambda c, n: W[k, c, n])

    order = [(0, 0), (1, 0), (2, 0), (1, 1), (2, 1), (2, 2), (0, 3), (1, 3), (2, 3)]
    rows16 = lax.broadcasted_iota(jnp.int32, (16, 128), 0)
    stacked = jnp.zeros((16, 128), jnp.float32)
    for place, (a, b) in enumerate(order):
        line = jnp.sum(DOT[a * 4 + b], axis=0, keepdims=True)
        stacked = jnp.where(rows16 == place, line, stacked)
    folded = stacked + pltpu.roll(stacked, 64, 1)
    left = lax.broadcasted_iota(jnp.int32, (8, 128), 1) < 64
    tile = jnp.where(left, folded[0:8], folded[8:16])

    def reduce(tile, stage, buffer, me, peers, send, recv):
        PART[stage] = tile

        def copy(i, slot):
            return remote(PART.at[stage], buffer.at[slot], send.at[i], recv.at[slot], peers[i])

        for i in range(16):
            pl.when(me != i)(lambda i=i: copy(i, me).start())
        buffer[me] = tile
        for i in range(16):
            pl.when(me != i)(lambda i=i: copy(i, i).wait_recv())
        total = buffer[0]
        for i in range(1, 16):
            total = total + buffer[i]
        for i in range(16):
            pl.when(me != i)(lambda i=i: copy(i, me).wait_send())
        return total

    tile = reduce(tile, 0, ARA, a_me, a_peers, a_send, a_recv)
    tile = reduce(tile, 1, ARB, b_me, b_peers, b_send, b_recv)
    sums_a = jnp.sum(jnp.where(left, tile, 0.0), axis=1, keepdims=True)
    sums_b = jnp.sum(jnp.where(left, 0.0, tile), axis=1, keepdims=True)
    a00, a10, a20, a11, a21, a22, b0, b1 = [sums_a[i : i + 1] for i in range(8)]
    b2 = sums_b[0:1]
    l00 = jnp.sqrt(a00)
    l10 = a10 / l00
    l20 = a20 / l00
    l11 = jnp.sqrt(a11 - l10 * l10)
    l21 = (a21 - l20 * l10) / l11
    l22 = jnp.sqrt(a22 - l20 * l20 - l21 * l21)
    y0 = b0 / l00
    y1 = (b1 - l10 * y0) / l11
    y2 = (b2 - l20 * y0 - l21 * y1) / l22
    c2 = y2 / l22
    c1 = (y1 - l21 * c2) / l11
    c0 = (y0 - l10 * c1 - l20 * c2) / l00
    join = place_out == jnp.where(place_in < 128, 2 * place_in, 2 * place_in - 255)
    join = join.astype(jnp.float32)
    def back(k):
        return remote(OUT.at[k], HOME.at[:, :, rows(my_tile)], out_send.at[k], out_recv.at[my_tile], z_home[k])

    def arrive(i, holder):
        return remote(OUT.at[0], HOME.at[:, :, EDGE * i : EDGE * i + EDGE], out_send.at[0], out_recv.at[i], holder)

    def b_peer_of(i):
        tile = depth * 4 + i
        return same_xy + tile // 4 * 4, lax.rem(tile // 2, 2) * 2 + lax.rem(tile, 2)

    def stay(k):
        return pltpu.make_async_copy(OUT.at[k], HOME.at[:, :, rows(my_tile)], out_local.at[0])

    for k in range(4):
        for j in range(KRYLOV):
            pl.when(x_me != k)(lambda j=j, k=k: along_x(j, k, k).wait_recv())
        mixed = c0 * RELAY[0, k] + c1 * RELAY[1, k] + c2 * RELAY[2, k]
        OUT[k] = permute(mixed.reshape(64, LANES), join).reshape(4, 2, EDGE, LANES)
        pl.when(is_me(z_home[k]))(lambda k=k: stay(k).start())
        pl.when(jnp.logical_not(is_me(z_home[k])))(lambda k=k: back(k).start())

    sent(setup, *setup)

    @pl.loop(0, KRYLOV)
    def _(j):
        copies = step_copies(j)
        sent(copies, "up", "down", *UPPER, *LOWER)

        def corner_sent(mine):
            pl.when(has["prev"])(lambda: sent(copies, mine[0]))
            pl.when(has["next"])(lambda: sent(copies, mine[1]))
            sent(copies, *mine[2:])

        on_core(0, lambda c: corner_sent(ROWS_0), copies)
        on_core(1, lambda c: corner_sent(ROWS_1), copies)

    for t in range(3):
        for i in range(4):
            pl.when(jnp.logical_not(is_me(goes_to[i])))(lambda t=t, i=i: give(t, i).wait_send())

    for i in range(4):
        holder = b_peer_of(i)
        pl.when(is_me(holder))(lambda: stay(0).wait())
        pl.when(jnp.logical_not(is_me(holder)))(lambda i=i, holder=holder: arrive(i, holder).wait_recv())
    for c in range(3):
        vel_ref[c] = HOME[c]
    pre_ref[...] = HOME[3]
    for k in range(4):
        for j in range(KRYLOV):
            pl.when(x_me != k)(lambda j=j, k=k: along_x(j, k, x_me).wait_send())
        pl.when(jnp.logical_not(is_me(z_home[k])))(lambda k=k: back(k).wait_send())


def body(forcing, source, viscosity):
    f32 = jnp.float32
    vmem = lambda *shape: pltpu.VMEM(shape, f32)
    dma = lambda *shape: pltpu.SemaphoreType.DMA(shape)
    K = KRYLOV
    return pl.pallas_call(
        kernel,
        out_shape=(
            jax.ShapeDtypeStruct((3, 2, 32, LANES), f32),
            jax.ShapeDtypeStruct((2, 32, LANES), f32),
        ),
        in_specs=[pl.BlockSpec(memory_space=pl.ANY)] * 3,
        out_specs=(pl.BlockSpec(memory_space=pltpu.VMEM), pl.BlockSpec(memory_space=pltpu.VMEM)),
        scratch_shapes=[
            vmem(5, EDGE, EDGE, LANES),
            vmem(WIDE, WIDE, LANES),
            vmem(WIDE, WIDE, LANES),
            vmem(K + 1, 4, WIDE, WIDE, LANES),
            vmem(WIDE, WIDE, LANES),
            vmem(WIDE, WIDE, LANES),
            vmem(3, WIDE, WIDE, LANES),
            vmem(3, 2, 4, WIDE, LANES),
            vmem(WIDE, WIDE, LANES),
            vmem(WIDE, WIDE, LANES),
            vmem(WIDE, WIDE, LANES),
            vmem(3, WIDE, WIDE, LANES),
            vmem(K, 4, EDGE, EDGE, LANES),
            vmem(EDGE, EDGE, LANES),
            vmem(K, 4, EDGE, EDGE, LANES),
            vmem(4, EDGE, EDGE, LANES),
            vmem(4, EDGE, EDGE, LANES),
            vmem(4, 4, 2, EDGE, LANES),
            vmem(K, 4, 4, 2, EDGE, LANES),
            vmem(4, 2, 32, LANES),
            vmem(4 * K, 8, 128),
            vmem(16, 8, 128),
            vmem(16, 8, 128),
            vmem(2, 8, 128),
            dma(3, 4),
            dma(3, 4),
            dma(3),
            dma(4),
            dma(4),
            dma(K, 10),
            dma(K, 10),
            dma(K, 4),
            dma(K, 4),
            dma(4),
            dma(4),
            dma(1),
            dma(16),
            dma(16),
            dma(16),
            dma(16),
        ],
        compiler_params=pltpu.CompilerParams(
            collective_id=0, has_side_effects=True, vmem_limit_bytes=60 * 1024 * 1024
        ),
        name="stokes_cycle",
    )(forcing, source, viscosity)


def solution(mesh):
    placed = (P(None, "slab", "depth", None), P("slab", "depth", None), P("slab", "depth", None))
    return jax.shard_map(
        body,
        mesh=mesh,
        in_specs=placed,
        out_specs=(P(None, "slab", "depth", None), P("slab", "depth", None)),
        check_vma=False,
    )
```

```python
import jax
import jax.numpy as jnp
from jax import lax
from jax.experimental import pallas as pl
from jax.experimental.pallas import tpu as pltpu
from jax.sharding import PartitionSpec as P

KRYLOV = 3
EDGE = 8
WIDE = 16
OFF = 4
LANES = 256
MESH_ID = pl.DeviceIdType.MESH


def next_z(x):
    return jnp.concatenate([x[:, 128:], pltpu.roll(x[:, :128], 127, 1)], axis=1)


def prev_z(x):
    return jnp.concatenate([pltpu.roll(x[:, 128:], 1, 1), x[:, :128]], axis=1)


def permute(x, matrix):
    return jnp.dot(x, matrix, precision=lax.Precision.HIGHEST, preferred_element_type=jnp.float32)


def next_y(x):
    return pltpu.roll(x, WIDE - 1, 0)


def prev_y(x):
    return pltpu.roll(x, 1, 0)


def forward_modes(u):
    ahead = next_z(u)
    zs = ahead + u
    zd = ahead - u
    zs_ahead = next_y(zs)
    zd_ahead = next_y(zd)
    return zs_ahead + zs, zs_ahead - zs, zd_ahead + zd, zd_ahead - zd


def element_modes(low, high):
    return (
        high[0] - low[0],
        high[1] - low[1],
        high[1] + low[1],
        high[2] - low[2],
        high[2] + low[2],
        high[3] - low[3],
        high[3] + low[3],
    )


def weigh(modes, visc):
    v16 = visc * (1.0 / 16.0)
    v24 = visc * (1.0 / 24.0)
    v48 = visc * (1.0 / 48.0)
    return (
        modes[0] * v16,
        modes[1] * v24,
        modes[2] * v16,
        modes[3] * v24,
        modes[4] * v16,
        modes[5] * v48,
        modes[6] * v24,
    )


def from_before(modes):
    return modes[0], modes[2] + modes[1], modes[4] + modes[3], modes[6] + modes[5]


def from_after(modes):
    return modes[0], modes[2] - modes[1], modes[4] - modes[3], modes[6] - modes[5]


def back_to_nodes(before, after):
    ss = before[0] - after[0]
    ds = before[1] + after[1]
    sd = before[2] + after[2]
    dd = before[3] + after[3]
    zs = (ss - ds) + prev_y(ss + ds)
    zd = (sd - dd) + prev_y(sd + dd)
    return (zs - zd) + prev_z(zs + zd)


def divergence_halves(u):
    x_ahead = next_z(u[0])
    y_ahead = next_z(u[1])
    z_ahead = next_z(u[2])
    zs_x = x_ahead + u[0]
    zs_y = y_ahead + u[1]
    zd_z = z_ahead - u[2]
    ss_x = next_y(zs_x) + zs_x
    rest = (zd_z - zs_y) + next_y(zd_z + zs_y)
    return rest + ss_x, rest - ss_x


def gradient(before, after):
    diff = before - after
    both = before + after
    diff_y = diff + prev_y(diff)
    both_back = prev_y(both)
    sum_y = both + both_back
    dif_y = both_back - both
    return (
        diff_y + prev_z(diff_y),
        dif_y + prev_z(dif_y),
        prev_z(sum_y) - sum_y,
    )


def fold(product):
    return product[:, :128] + product[:, 128:]


def block_of(slab, depth):
    x = lax.rem(slab, 4)
    y = slab // 16
    z = lax.rem(slab // 4, 4) * 2 + depth // 2
    odd = lax.rem(y, 2)
    return y * 4 + x + odd * (3 - 2 * x), z * 2 + lax.rem(depth, 2)


def device_of(across, along):
    y = across // 4
    place = lax.rem(across, 4)
    odd = lax.rem(y, 2)
    x = place + odd * (3 - 2 * place)
    z = along // 2
    return y * 16 + (z // 2) * 4 + x, lax.rem(z, 2) * 2 + lax.rem(along, 2)


def kernel(
    f_hbm, s_hbm, v_hbm, vel_ref, pre_ref,
    RAW, V, VM, X, INV, ISC, JAC, MID, MD, P1, PN, Z, ZS, DIV, W, Q, Q0, OUT, RELAY, HOME, DOT, ARA, ARB, PART,
    in_send, in_recv, in_local, s_send, s_recv, i_send, i_recv, x_send, x_recv, out_send, out_recv, out_local,
    a_send, a_recv, b_send, b_recv,
):
    slab = lax.axis_index("slab")
    depth = lax.axis_index("depth")
    across, along = block_of(slab, depth)
    has = dict(next=across < 15, prev=across > 0, up=along < 15, down=along > 0)
    opposite = dict(next="prev", prev="next", up="down", down="up")
    to_next = device_of(lax.rem(across + 1, 16), along)
    to_prev = device_of(lax.rem(across + 15, 16), along)
    to_up = device_of(across, lax.rem(along + 1, 16))
    to_down = device_of(across, lax.rem(along + 15, 16))

    my_k = lax.rem(slab, 4)
    my_tile = lax.rem(along, 4)
    goes_to = [device_of(slab // 4, depth * 4 + i) for i in range(4)]
    comes_from = [(across * 4 + k, along // 4) for k in range(4)]

    def is_me(device):
        return (device[0] == slab) & (device[1] == depth)

    core = lax.rem(depth, 2)
    x_me = lax.rem(slab, 4)
    y_me = slab // 16
    same_z = slab - x_me - y_me * 16
    same_xy = y_me * 16 + x_me
    a_me = y_me * 4 + x_me
    b_me = along
    x_at = [lax.rem(x_me + d, 4) for d in range(4)]
    y_at = [lax.rem(y_me + d, 4) for d in range(4)]
    z_at = [lax.rem(along // 2 + d, 8) for d in range(8)]
    z_slab = [same_xy + z // 2 * 4 for z in z_at]
    z_depth = [lax.rem(z, 2) * 2 for z in z_at]
    steps = [(dx, dy) for dx in range(4) for dy in range(4) if dx or dy]
    steps.sort(key=lambda d: -min(d[0], 4 - d[0]) - min(d[1], 4 - d[1]))
    a_peers = [((same_z + y_at[dy] * 16 + x_at[dx], depth), y_at[dy] * 4 + x_at[dx]) for dx, dy in steps]
    steps = [(dz, dc) for dz in range(8) for dc in range(2) if dz or dc]
    steps.sort(key=lambda d: -min(d[0], 8 - d[0]) - 0.5 * d[1])
    cores = (core, 1 - core)
    b_peers = [((z_slab[dz], z_depth[dz] + cores[dc]), z_at[dz] * 2 + cores[dc]) for dz, dc in steps]
    x_line = [(slab - x_me + k, depth) for k in range(4)]
    odd = lax.rem(y_me, 2)
    z_home = [(same_xy + 4 * (k + odd * (3 - 2 * k)), along // 4) for k in range(4)]

    barrier = pltpu.get_barrier_semaphore()

    def greet(device):
        pl.semaphore_signal(barrier, inc=1, device_id=device, device_id_type=MESH_ID)

    zeros = jnp.zeros((4, WIDE, LANES), jnp.float32)
    for name, place in (("prev", 0), ("next", 12)):

        @pl.when(jnp.logical_not(has[name]))
        def _(place=place):
            V[place : place + 4] = zeros
            for j in range(KRYLOV):
                for c in range(4):
                    X[j, c, place : place + 4] = zeros

    zeros = jnp.zeros((WIDE, 4, LANES), jnp.float32)
    for name, place in (("down", 12), ("up", 8)):

        @pl.when(jnp.logical_not(has[name]))
        def _(place=place):
            V[:, place : place + 4] = zeros
            for j in range(KRYLOV):
                for c in range(4):
                    X[j, c, :, place : place + 4] = zeros

    for device in goes_to + comes_from + [peer for peer, _ in a_peers + b_peers]:
        greet(device)
    pl.semaphore_wait(barrier, 38)

    def remote(src, dst, send, recv, peer):
        return pltpu.make_async_remote_copy(
            src_ref=src, dst_ref=dst, send_sem=send, recv_sem=recv, device_id=peer, device_id_type=MESH_ID
        )

    def rows(i):
        return pl.ds(pl.multiple_of(i * EDGE, EDGE), EDGE)

    def fields(i, k):
        return (
            (v_hbm.at[:, rows(i)], RAW.at[4, pl.ds(2 * k, 2)]),
            (f_hbm.at[:, :, rows(i)], RAW.at[0:3, pl.ds(2 * k, 2)]),
            (s_hbm.at[:, rows(i)], RAW.at[3, pl.ds(2 * k, 2)]),
        )

    def give(t, i):
        src, dst = fields(i, my_k)[t]
        return remote(src, dst, in_send.at[t, i], in_recv.at[t, my_k], goes_to[i])

    def take(t, k):
        src, dst = fields(0, k)[t]
        return remote(src, dst, in_send.at[t, 0], in_recv.at[t, k], comes_from[k])

    def keep(t):
        src, dst = fields(my_tile, my_k)[t]
        return pltpu.make_async_copy(src, dst, in_local.at[t])

    home = is_me(device_of(slab // 4, depth * 4 + my_tile))
    for t in range(3):
        pl.when(home)(lambda t=t: keep(t).start())
        for i in range(4):
            pl.when(jnp.logical_not(is_me(goes_to[i])))(lambda t=t, i=i: give(t, i).start())

    def taken(t):
        pl.when(home)(lambda: keep(t).wait())
        for k in range(4):
            pl.when(jnp.logical_not(is_me(comes_from[k])))(lambda k=k: take(t, k).wait_recv())

    def start(copies, *names):
        for name in names:
            pl.when(has[name.split("_")[-1]])(lambda name=name: copies[name]().start())

    def received(copies, *names):
        for name in names:
            pl.when(has[opposite[name.split("_")[-1]]])(lambda name=name: copies[name]().wait_recv())

    def sent(copies, *names):
        for name in names:
            pl.when(has[name.split("_")[-1]])(lambda name=name: copies[name]().wait_send())

    def setup_copy(k, src, dst, peer):
        return lambda: remote(src, dst, s_send.at[k], s_recv.at[k], peer)

    setup = dict(
        up=setup_copy(0, V.at[4:12, 4:8], V.at[4:12, 12:16], to_up),
        down=setup_copy(1, V.at[4:12, 0:4], V.at[4:12, 8:12], to_down),
        next=setup_copy(2, V.at[8:12], V.at[0:4], to_next),
        prev=setup_copy(3, V.at[4:8], V.at[12:16], to_prev),
    )

    def step_copies(j, c):
        def copy(k, src, dst, peer):
            return lambda: remote(
                X.at[(j, c) + src], X.at[(j, c) + dst], i_send.at[j, c, k], i_recv.at[j, c, k], peer
            )

        high, from_high = (slice(9, 12), slice(1, 4)) if c == 3 else (slice(8, 12), slice(0, 4))
        low, from_low = (slice(4, 6), slice(12, 14)) if c == 3 else (slice(4, 8), slice(12, 16))
        own, first, last, above, below = slice(4, 12), slice(0, 4), slice(4, 8), slice(8, 12), slice(12, 16)
        main = slice(0, 8)
        return dict(
            up=copy(0, (own, last), (own, below), to_up),
            down=copy(1, (own, first), (own, above), to_down),
            main_next=copy(2, (high, main), (from_high, main), to_next),
            main_prev=copy(3, (low, main), (from_low, main), to_prev),
            below_next=copy(4, (high, below), (from_high, below), to_next),
            below_prev=copy(5, (low, below), (from_low, below), to_prev),
            above_next=copy(4, (high, above), (from_high, above), to_next),
            above_prev=copy(5, (low, above), (from_low, above), to_prev),
            low_up=copy(6, (from_high, last), (from_high, below), to_up),
            high_up=copy(7, (from_low, last), (from_low, below), to_up),
            low_down=copy(6, (from_high, first), (from_high, above), to_down),
            high_down=copy(7, (from_low, first), (from_low, above), to_down),
        )

    FIRST = ("up", "down", "main_next", "main_prev")
    ROWS_0 = ("low_up", "high_up", "below_next", "below_prev")
    ROWS_1 = ("low_down", "high_down", "above_next", "above_prev")

    def on_core(number, action):
        pl.when(core == number)(action)

    def begin(j, c):
        start(step_copies(j, c), *FIRST)

    def pass_outer(j, c):
        copies = step_copies(j, c)
        received(copies, "up", "down")
        on_core(0, lambda: start(copies, "below_next", "below_prev"))
        on_core(1, lambda: start(copies, "above_next", "above_prev"))

    def pass_inner(j, c):
        copies = step_copies(j, c)
        for name, side, place in (("main_next", "prev", 0), ("main_prev", "next", 1)):
            received(copies, name)

            @pl.when(has[side])
            def _(place=place):
                on_core(0, lambda: start(copies, ROWS_0[place]))
                on_core(1, lambda: start(copies, ROWS_1[place]))

    def take_corners(j, c):
        copies = step_copies(j, c)

        def corners(here, theirs):
            pl.when(has["prev"])(lambda: received(copies, theirs[0]))
            pl.when(has["next"])(lambda: received(copies, theirs[1]))
            received(copies, *here[2:])

        on_core(0, lambda: corners(ROWS_0, ROWS_1))
        on_core(1, lambda: corners(ROWS_1, ROWS_0))

    def all_sent(j, c):
        copies = step_copies(j, c)
        sent(copies, *FIRST)

        def corners(mine):
            pl.when(has["prev"])(lambda: sent(copies, mine[0]))
            pl.when(has["next"])(lambda: sent(copies, mine[1]))
            sent(copies, *mine[2:])

        on_core(0, lambda: corners(ROWS_0))
        on_core(1, lambda: corners(ROWS_1))

    place_in = lax.broadcasted_iota(jnp.int32, (LANES, LANES), 0)
    place_out = lax.broadcasted_iota(jnp.int32, (LANES, LANES), 1)
    split = place_in == jnp.where(place_out < 128, 2 * place_out, 2 * place_out - 255)
    split = split.astype(jnp.float32)
    taken(0)
    moved = permute(RAW[4].reshape(64, LANES), split)
    for n in range(8):
        V[n + OFF, 0:EDGE] = moved[8 * n : 8 * n + 8]
    start(setup, "up")
    start(setup, "down")

    row = lax.broadcasted_iota(jnp.int32, (WIDE, LANES), 0)
    row = along * EDGE + jnp.where(row < 12, row, row - WIDE)
    element_row = ((row >= 0) & (row < 128)).astype(jnp.float32)
    node_row = ((row >= 1) & (row < 128)).astype(jnp.float32)

    def plane_flag(n, low):
        place = across * EDGE + n
        return ((place >= low) & (place < 128)).astype(jnp.float32)

    received(setup, "up")
    received(setup, "down")
    start(setup, "next")
    start(setup, "prev")

    def inverse_plane(n):
        both = VM[n + OFF - 1] + VM[n + OFF]
        both = both + prev_y(both)
        both = both + prev_z(both)
        free = node_row * plane_flag(n, 1)
        INV[n + OFF] = free * 3.0 / jnp.where(free > 0.0, both, 1.0)

    for n in range(8):
        VM[n + OFF] = V[n + OFF] * (element_row * plane_flag(n, 0))
    for n in range(1, 8):
        inverse_plane(n)
    received(setup, "next")
    received(setup, "prev")
    for n in (-4, -3, -2, -1, 8, 9, 10, 11):
        VM[n + OFF] = V[n + OFF] * (element_row * plane_flag(n, 0))
    inverse_plane(0)
    taken(1)
    for c in range(3):
        moved = permute(RAW[c].reshape(64, LANES), split)
        for n in range(8):
            free = (node_row * plane_flag(n, 1))[0:EDGE]
            q = moved[8 * n : 8 * n + 8] * free
            Q0[c, n] = q
            Q[c, n] = q
            X[0, c, n + OFF, 0:EDGE] = q * INV[n + OFF, 0:EDGE]
        begin(0, c)
    taken(2)
    moved = permute(RAW[3].reshape(64, LANES), split)
    for n in range(8):
        p = moved[8 * n : 8 * n + 8]
        Q0[3, n] = p
        Q[3, n] = p
        X[0, 3, n + OFF, 0:EDGE] = p
    begin(0, 3)
    for n in (-3, -2, -1, 8, 9, 10):
        inverse_plane(n)
    for e in range(-3, 10):
        both = INV[e + OFF] + INV[e + OFF + 1]
        both = both + next_y(both)
        both = both + next_z(both)
        there = element_row * plane_flag(e, 0)
        ISC[e + OFF] = there / jnp.where(there > 0.0, 0.1875 * both, 1.0)

    def along_x(j, k, slot):
        return remote(ZS.at[j, :, 2 * k : 2 * k + 2], RELAY.at[j, slot], x_send.at[j, k], x_recv.at[j, slot], x_line[k])

    def x_begin(j):
        for k in range(4):
            pl.when(x_me != k)(lambda k=k: along_x(j, k, x_me).start())
        RELAY[j, x_me] = ZS[j, :, pl.ds(2 * x_me, 2)]

    @pl.loop(0, KRYLOV)
    def _(j):
        for c in range(3):
            pass_outer(j, c)

        def modes_of(n, c):
            return forward_modes(X[j, c, n + OFF])

        def jacobi(n, c, before, after):
            JAC[c, n + OFF] = 2.0 * X[j, c, n + OFF] - INV[n + OFF] * back_to_nodes(before, after)

        def sweep(first, last, c, before, keep_first, keep_last):
            low = modes_of(first, c)
            for e in range(first, last + 1):
                high = modes_of(e + 1, c)
                weighted = weigh(element_modes(low, high), VM[e + OFF])
                after = from_after(weighted)
                if before is not None:
                    jacobi(e, c, before, after)
                elif keep_first is not None:
                    for m in range(4):
                        MID[c, keep_first, m] = after[m]
                before = from_before(weighted)
                low = high
            if keep_last is not None:
                for m in range(4):
                    MID[c, keep_last, m] = before[m]
            return before

        for c in range(3):
            sweep(0, 6, c, None, 0, 1)
        pass_outer(j, 3)
        for c in range(4):
            pass_inner(j, c)

        for c in range(3):
            take_corners(j, c)
            before = sweep(-4, -1, c, None, None, None)
            jacobi(0, c, before, [MID[c, 0, m] for m in range(4)])
            sweep(7, 10, c, [MID[c, 1, m] for m in range(4)], None, None)

        take_corners(j, 3)

        @pl.when(j == 1)
        def _():
            x_begin(0)

        @pl.when(j == 2)
        def _():
            x_begin(1)

        low = None
        for n in range(-3, 11):
            high, own = divergence_halves([JAC[c, n + OFF] for c in range(3)])
            if low is not None:
                e = n - 1
                defect = 0.25 * (high + low) - X[j, 3, e + OFF]
                MD[e + OFF] = defect
                P1[e + OFF] = defect * ISC[e + OFF]
            low = own
        low = None
        for n in range(-2, 10):
            slope = gradient(P1[n + OFF - 1], P1[n + OFF])
            scale = 0.25 * INV[n + OFF]
            high, own = divergence_halves([scale * slope[c] for c in range(3)])
            if low is not None:
                e = n - 1
                PN[e + OFF] = P1[e + OFF] + (MD[e + OFF] - 0.25 * (high + low)) * ISC[e + OFF]
            low = own
        for n in range(-1, 9):
            slope = gradient(PN[n + OFF - 1], PN[n + OFF])
            scale = 0.25 * INV[n + OFF]
            for c in range(3):
                z = JAC[c, n + OFF] - scale * slope[c]
                Z[c, n + OFF] = z
                if 0 <= n < 8:
                    ZS[j, c, n] = z[0:EDGE]
            if 0 <= n < 8:
                ZS[j, 3, n] = PN[n + OFF, 0:EDGE]
        @pl.when(j == 2)
        def _():
            x_begin(2)

        for c in range(3):
            low = forward_modes(Z[c, OFF - 1])
            before = None
            for e in range(-1, 8):
                high = forward_modes(Z[c, e + 1 + OFF])
                modes = element_modes(low, high)
                place = (0, 2, 4)[c]
                if e >= 0:
                    own = modes[place][0:EDGE]
                    DIV[e] = own if c == 0 else DIV[e] + own
                weighted = list(weigh(modes, VM[e + OFF]))
                weighted[place] = weighted[place] + 0.25 * PN[e + OFF]
                after = from_after(weighted)
                if before is not None:
                    free = (node_row * plane_flag(e, 1))[0:EDGE]
                    w = back_to_nodes(before, after)[0:EDGE] * free
                    W[j, c, e] = w
                    q = w - Q[c, e]
                    Q[c, e] = q
                    X[j + 1, c, e + OFF, 0:EDGE] = q * INV[e + OFF, 0:EDGE]
                before = from_before(weighted)
                low = high
            pl.when(j < KRYLOV - 1)(lambda c=c: begin(j + 1, c))
        for e in range(8):
            w = 0.25 * DIV[e]
            W[j, 3, e] = w
            q = w - Q[3, e]
            Q[3, e] = q
            X[j + 1, 3, e + OFF, 0:EDGE] = q

        pl.when(j < KRYLOV - 1)(lambda: begin(j + 1, 3))

        def inner(other):
            total = None
            for n in range(8):
                for c in range(4):
                    term = W[j, c, n] * other(c, n)
                    total = term if total is None else total + term
            return fold(total)

        DOT[j * 4 + 3] = inner(lambda c, n: Q0[c, n])

        @pl.loop(0, j + 1)
        def _(k):
            DOT[j * 4 + k] = inner(lambda c, n: W[k, c, n])

    order = [(0, 0), (1, 0), (2, 0), (1, 1), (2, 1), (2, 2), (0, 3), (1, 3), (2, 3)]
    rows16 = lax.broadcasted_iota(jnp.int32, (16, 128), 0)
    stacked = jnp.zeros((16, 128), jnp.float32)
    for place, (a, b) in enumerate(order):
        line = jnp.sum(DOT[a * 4 + b], axis=0, keepdims=True)
        stacked = jnp.where(rows16 == place, line, stacked)
    folded = stacked + pltpu.roll(stacked, 64, 1)
    left = lax.broadcasted_iota(jnp.int32, (8, 128), 1) < 64
    tile = jnp.where(left, folded[0:8], folded[8:16])

    def reduce(tile, stage, buffer, me, peers, send, recv):
        PART[stage] = tile

        def copy(i, slot):
            return remote(PART.at[stage], buffer.at[slot], send.at[i], recv.at[slot], peers[i][0])

        for i in range(15):
            copy(i, me).start()
        buffer[me] = tile
        for i in reversed(range(15)):
            copy(i, peers[i][1]).wait_recv()
        total = buffer[0]
        for i in range(1, 16):
            total = total + buffer[i]
        for i in range(15):
            copy(i, me).wait_send()
        return total

    tile = reduce(tile, 0, ARA, a_me, a_peers, a_send, a_recv)
    tile = reduce(tile, 1, ARB, b_me, b_peers, b_send, b_recv)
    sums_a = jnp.sum(jnp.where(left, tile, 0.0), axis=1, keepdims=True)
    sums_b = jnp.sum(jnp.where(left, 0.0, tile), axis=1, keepdims=True)
    a00, a10, a20, a11, a21, a22, b0, b1 = [sums_a[i : i + 1] for i in range(8)]
    b2 = sums_b[0:1]
    l00 = jnp.sqrt(a00)
    l10 = a10 / l00
    l20 = a20 / l00
    l11 = jnp.sqrt(a11 - l10 * l10)
    l21 = (a21 - l20 * l10) / l11
    l22 = jnp.sqrt(a22 - l20 * l20 - l21 * l21)
    y0 = b0 / l00
    y1 = (b1 - l10 * y0) / l11
    y2 = (b2 - l20 * y0 - l21 * y1) / l22
    c2 = y2 / l22
    c1 = (y1 - l21 * c2) / l11
    c0 = (y0 - l10 * c1 - l20 * c2) / l00
    join = place_out == jnp.where(place_in < 128, 2 * place_in, 2 * place_in - 255)
    join = join.astype(jnp.float32)
    def back(k):
        return remote(OUT.at[k], HOME.at[:, :, rows(my_tile)], out_send.at[k], out_recv.at[my_tile], z_home[k])

    def arrive(i, holder):
        return remote(OUT.at[0], HOME.at[:, :, EDGE * i : EDGE * i + EDGE], out_send.at[0], out_recv.at[i], holder)

    def b_peer_of(i):
        tile = depth * 4 + i
        return same_xy + tile // 4 * 4, lax.rem(tile // 2, 2) * 2 + lax.rem(tile, 2)

    def stay(k):
        return pltpu.make_async_copy(OUT.at[k], HOME.at[:, :, rows(my_tile)], out_local.at[0])

    for k in range(4):
        for j in range(KRYLOV):
            pl.when(x_me != k)(lambda j=j, k=k: along_x(j, k, k).wait_recv())
        mixed = c0 * RELAY[0, k] + c1 * RELAY[1, k] + c2 * RELAY[2, k]
        OUT[k] = permute(mixed.reshape(64, LANES), join).reshape(4, 2, EDGE, LANES)
        pl.when(is_me(z_home[k]))(lambda k=k: stay(k).start())
        pl.when(jnp.logical_not(is_me(z_home[k])))(lambda k=k: back(k).start())

    sent(setup, *setup)

    @pl.loop(0, KRYLOV)
    def _(j):
        for c in range(4):
            all_sent(j, c)

    for t in range(3):
        for i in range(4):
            pl.when(jnp.logical_not(is_me(goes_to[i])))(lambda t=t, i=i: give(t, i).wait_send())

    for i in range(4):
        holder = b_peer_of(i)
        pl.when(is_me(holder))(lambda: stay(0).wait())
        pl.when(jnp.logical_not(is_me(holder)))(lambda i=i, holder=holder: arrive(i, holder).wait_recv())
    for c in range(3):
        vel_ref[c] = HOME[c]
    pre_ref[...] = HOME[3]
    for k in range(4):
        for j in range(KRYLOV):
            pl.when(x_me != k)(lambda j=j, k=k: along_x(j, k, x_me).wait_send())
        pl.when(jnp.logical_not(is_me(z_home[k])))(lambda k=k: back(k).wait_send())


def body(forcing, source, viscosity):
    f32 = jnp.float32
    vmem = lambda *shape: pltpu.VMEM(shape, f32)
    dma = lambda *shape: pltpu.SemaphoreType.DMA(shape)
    K = KRYLOV
    return pl.pallas_call(
        kernel,
        out_shape=(
            jax.ShapeDtypeStruct((3, 2, 32, LANES), f32),
            jax.ShapeDtypeStruct((2, 32, LANES), f32),
        ),
        in_specs=[pl.BlockSpec(memory_space=pl.ANY)] * 3,
        out_specs=(pl.BlockSpec(memory_space=pltpu.VMEM), pl.BlockSpec(memory_space=pltpu.VMEM)),
        scratch_shapes=[
            vmem(5, EDGE, EDGE, LANES),
            vmem(WIDE, WIDE, LANES),
            vmem(WIDE, WIDE, LANES),
            vmem(K + 1, 4, WIDE, WIDE, LANES),
            vmem(WIDE, WIDE, LANES),
            vmem(WIDE, WIDE, LANES),
            vmem(3, WIDE, WIDE, LANES),
            vmem(3, 2, 4, WIDE, LANES),
            vmem(WIDE, WIDE, LANES),
            vmem(WIDE, WIDE, LANES),
            vmem(WIDE, WIDE, LANES),
            vmem(3, WIDE, WIDE, LANES),
            vmem(K, 4, EDGE, EDGE, LANES),
            vmem(EDGE, EDGE, LANES),
            vmem(K, 4, EDGE, EDGE, LANES),
            vmem(4, EDGE, EDGE, LANES),
            vmem(4, EDGE, EDGE, LANES),
            vmem(4, 4, 2, EDGE, LANES),
            vmem(K, 4, 4, 2, EDGE, LANES),
            vmem(4, 2, 32, LANES),
            vmem(4 * K, 8, 128),
            vmem(16, 8, 128),
            vmem(16, 8, 128),
            vmem(2, 8, 128),
            dma(3, 4),
            dma(3, 4),
            dma(3),
            dma(4),
            dma(4),
            dma(K, 4, 8),
            dma(K, 4, 8),
            dma(K, 4),
            dma(K, 4),
            dma(4),
            dma(4),
            dma(1),
            dma(16),
            dma(16),
            dma(16),
            dma(16),
        ],
        compiler_params=pltpu.CompilerParams(
            collective_id=0, has_side_effects=True, vmem_limit_bytes=60 * 1024 * 1024
        ),
        name="stokes_cycle",
    )(forcing, source, viscosity)


def solution(mesh):
    placed = (P(None, "slab", "depth", None), P("slab", "depth", None), P("slab", "depth", None))
    return jax.shard_map(
        body,
        mesh=mesh,
        in_specs=placed,
        out_specs=(P(None, "slab", "depth", None), P("slab", "depth", None)),
        check_vma=False,
    )
```

```python
import jax
import jax.numpy as jnp
from jax import lax
from jax.experimental import pallas as pl
from jax.experimental.pallas import tpu as pltpu
from jax.sharding import PartitionSpec as P

KRYLOV = 3
EDGE = 8
WIDE = 16
OFF = 4
LANES = 256
MESH_ID = pl.DeviceIdType.MESH


def next_z(x):
    return jnp.concatenate([x[:, 128:], pltpu.roll(x[:, :128], 127, 1)], axis=1)


def prev_z(x):
    return jnp.concatenate([pltpu.roll(x[:, 128:], 1, 1), x[:, :128]], axis=1)


def permute(x, matrix):
    parts = []
    for _ in range(3):
        part = x.astype(jnp.bfloat16)
        x = x - part.astype(jnp.float32)
        parts.append(part)
    count = x.shape[0]
    moved = jnp.dot(jnp.concatenate(parts, axis=0), matrix, preferred_element_type=jnp.float32)
    return moved[0:count] + (moved[count : 2 * count] + moved[2 * count :])


def next_y(x):
    return pltpu.roll(x, WIDE - 1, 0)


def prev_y(x):
    return pltpu.roll(x, 1, 0)


def forward_modes(u):
    ahead = next_z(u)
    zs = ahead + u
    zd = ahead - u
    zs_ahead = next_y(zs)
    zd_ahead = next_y(zd)
    return zs_ahead + zs, zs_ahead - zs, zd_ahead + zd, zd_ahead - zd


def element_modes(low, high):
    return (
        high[0] - low[0],
        high[1] - low[1],
        high[1] + low[1],
        high[2] - low[2],
        high[2] + low[2],
        high[3] - low[3],
        high[3] + low[3],
    )


def weigh(modes, visc):
    v16 = visc * (1.0 / 16.0)
    v24 = visc * (1.0 / 24.0)
    v48 = visc * (1.0 / 48.0)
    return (
        modes[0] * v16,
        modes[1] * v24,
        modes[2] * v16,
        modes[3] * v24,
        modes[4] * v16,
        modes[5] * v48,
        modes[6] * v24,
    )


def from_before(modes):
    return modes[0], modes[2] + modes[1], modes[4] + modes[3], modes[6] + modes[5]


def from_after(modes):
    return modes[0], modes[2] - modes[1], modes[4] - modes[3], modes[6] - modes[5]


def back_to_nodes(before, after):
    ss = before[0] - after[0]
    ds = before[1] + after[1]
    sd = before[2] + after[2]
    dd = before[3] + after[3]
    zs = (ss - ds) + prev_y(ss + ds)
    zd = (sd - dd) + prev_y(sd + dd)
    return (zs - zd) + prev_z(zs + zd)


def divergence_halves(u):
    x_ahead = next_z(u[0])
    y_ahead = next_z(u[1])
    z_ahead = next_z(u[2])
    zs_x = x_ahead + u[0]
    zs_y = y_ahead + u[1]
    zd_z = z_ahead - u[2]
    ss_x = next_y(zs_x) + zs_x
    rest = (zd_z - zs_y) + next_y(zd_z + zs_y)
    return rest + ss_x, rest - ss_x


def gradient(before, after):
    diff = before - after
    both = before + after
    diff_y = diff + prev_y(diff)
    both_back = prev_y(both)
    sum_y = both + both_back
    dif_y = both_back - both
    return (
        diff_y + prev_z(diff_y),
        dif_y + prev_z(dif_y),
        prev_z(sum_y) - sum_y,
    )


def fold(product):
    return product[:, :128] + product[:, 128:]


def block_of(slab, depth):
    x = lax.rem(slab, 4)
    y = slab // 16
    z = lax.rem(slab // 4, 4) * 2 + depth // 2
    odd = lax.rem(y, 2)
    return y * 4 + x + odd * (3 - 2 * x), z * 2 + lax.rem(depth, 2)


def device_of(across, along):
    y = across // 4
    place = lax.rem(across, 4)
    odd = lax.rem(y, 2)
    x = place + odd * (3 - 2 * place)
    z = along // 2
    return y * 16 + (z // 2) * 4 + x, lax.rem(z, 2) * 2 + lax.rem(along, 2)


def kernel(
    f_hbm, s_hbm, v_hbm, vel_ref, pre_ref,
    RAW, V, VM, X, INV, ISC, JAC, MID, MD, P1, PN, Z, ZS, DIV, W, Q, Q0, OUT, RELAY, HOME, DOT, ARA, ARB, PART,
    in_send, in_recv, in_local, s_send, s_recv, i_send, i_recv, x_send, x_recv, out_send, out_recv, out_local,
    a_send, a_recv, b_send, b_recv,
):
    slab = lax.axis_index("slab")
    depth = lax.axis_index("depth")
    across, along = block_of(slab, depth)
    has = dict(next=across < 15, prev=across > 0, up=along < 15, down=along > 0)
    opposite = dict(next="prev", prev="next", up="down", down="up")
    to_next = device_of(lax.rem(across + 1, 16), along)
    to_prev = device_of(lax.rem(across + 15, 16), along)
    to_up = device_of(across, lax.rem(along + 1, 16))
    to_down = device_of(across, lax.rem(along + 15, 16))

    my_k = lax.rem(slab, 4)
    my_tile = lax.rem(along, 4)
    goes_to = [device_of(slab // 4, depth * 4 + i) for i in range(4)]
    comes_from = [(across * 4 + k, along // 4) for k in range(4)]

    def is_me(device):
        return (device[0] == slab) & (device[1] == depth)

    core = lax.rem(depth, 2)
    x_me = lax.rem(slab, 4)
    y_me = slab // 16
    same_z = slab - x_me - y_me * 16
    same_xy = y_me * 16 + x_me
    a_me = y_me * 4 + x_me
    b_me = along
    x_at = [lax.rem(x_me + d, 4) for d in range(4)]
    y_at = [lax.rem(y_me + d, 4) for d in range(4)]
    z_at = [lax.rem(along // 2 + d, 8) for d in range(8)]
    z_slab = [same_xy + z // 2 * 4 for z in z_at]
    z_depth = [lax.rem(z, 2) * 2 for z in z_at]
    steps = [(dx, dy) for dx in range(4) for dy in range(4) if dx or dy]
    steps.sort(key=lambda d: -min(d[0], 4 - d[0]) - min(d[1], 4 - d[1]))
    a_peers = [((same_z + y_at[dy] * 16 + x_at[dx], depth), y_at[dy] * 4 + x_at[dx]) for dx, dy in steps]
    steps = [(dz, dc) for dz in range(8) for dc in range(2) if dz or dc]
    steps.sort(key=lambda d: -min(d[0], 8 - d[0]) - 0.5 * d[1])
    cores = (core, 1 - core)
    b_peers = [((z_slab[dz], z_depth[dz] + cores[dc]), z_at[dz] * 2 + cores[dc]) for dz, dc in steps]
    x_line = [(slab - x_me + k, depth) for k in range(4)]
    odd = lax.rem(y_me, 2)
    z_home = [(same_xy + 4 * (k + odd * (3 - 2 * k)), along // 4) for k in range(4)]

    barrier = pltpu.get_barrier_semaphore()

    def greet(device):
        pl.semaphore_signal(barrier, inc=1, device_id=device, device_id_type=MESH_ID)

    zeros = jnp.zeros((4, WIDE, LANES), jnp.float32)
    for name, place in (("prev", 0), ("next", 12)):

        @pl.when(jnp.logical_not(has[name]))
        def _(place=place):
            V[place : place + 4] = zeros
            for j in range(KRYLOV):
                for c in range(4):
                    X[j, c, place : place + 4] = zeros

    zeros = jnp.zeros((WIDE, 4, LANES), jnp.float32)
    for name, place in (("down", 12), ("up", 8)):

        @pl.when(jnp.logical_not(has[name]))
        def _(place=place):
            V[:, place : place + 4] = zeros
            for j in range(KRYLOV):
                for c in range(4):
                    X[j, c, :, place : place + 4] = zeros

    for device in goes_to + comes_from + [peer for peer, _ in a_peers + b_peers]:
        greet(device)
    pl.semaphore_wait(barrier, 38)

    def remote(src, dst, send, recv, peer):
        return pltpu.make_async_remote_copy(
            src_ref=src, dst_ref=dst, send_sem=send, recv_sem=recv, device_id=peer, device_id_type=MESH_ID
        )

    def rows(i):
        return pl.ds(pl.multiple_of(i * EDGE, EDGE), EDGE)

    def fields(i, k):
        return (
            (v_hbm.at[:, rows(i)], RAW.at[4, pl.ds(2 * k, 2)]),
            (f_hbm.at[:, :, rows(i)], RAW.at[0:3, pl.ds(2 * k, 2)]),
            (s_hbm.at[:, rows(i)], RAW.at[3, pl.ds(2 * k, 2)]),
        )

    def give(t, i):
        src, dst = fields(i, my_k)[t]
        return remote(src, dst, in_send.at[t, i], in_recv.at[t, my_k], goes_to[i])

    def take(t, k):
        src, dst = fields(0, k)[t]
        return remote(src, dst, in_send.at[t, 0], in_recv.at[t, k], comes_from[k])

    def keep(t):
        src, dst = fields(my_tile, my_k)[t]
        return pltpu.make_async_copy(src, dst, in_local.at[t])

    home = is_me(device_of(slab // 4, depth * 4 + my_tile))
    for t in range(3):
        pl.when(home)(lambda t=t: keep(t).start())
        for i in range(4):
            pl.when(jnp.logical_not(is_me(goes_to[i])))(lambda t=t, i=i: give(t, i).start())

    def taken(t):
        pl.when(home)(lambda: keep(t).wait())
        for k in range(4):
            pl.when(jnp.logical_not(is_me(comes_from[k])))(lambda k=k: take(t, k).wait_recv())

    def start(copies, *names):
        for name in names:
            pl.when(has[name.split("_")[-1]])(lambda name=name: copies[name]().start())

    def received(copies, *names):
        for name in names:
            pl.when(has[opposite[name.split("_")[-1]]])(lambda name=name: copies[name]().wait_recv())

    def sent(copies, *names):
        for name in names:
            pl.when(has[name.split("_")[-1]])(lambda name=name: copies[name]().wait_send())

    def setup_copy(k, src, dst, peer):
        return lambda: remote(src, dst, s_send.at[k], s_recv.at[k], peer)

    setup = dict(
        up=setup_copy(0, V.at[4:12, 4:8], V.at[4:12, 12:16], to_up),
        down=setup_copy(1, V.at[4:12, 0:4], V.at[4:12, 8:12], to_down),
        next=setup_copy(2, V.at[8:12], V.at[0:4], to_next),
        prev=setup_copy(3, V.at[4:8], V.at[12:16], to_prev),
    )

    def step_copies(j, c):
        def copy(k, src, dst, peer):
            return lambda: remote(
                X.at[(j, c) + src], X.at[(j, c) + dst], i_send.at[j, c, k], i_recv.at[j, c, k], peer
            )

        high, from_high = (slice(9, 12), slice(1, 4)) if c == 3 else (slice(8, 12), slice(0, 4))
        low, from_low = (slice(4, 6), slice(12, 14)) if c == 3 else (slice(4, 8), slice(12, 16))
        own, first, last, above, below = slice(4, 12), slice(0, 4), slice(4, 8), slice(8, 12), slice(12, 16)
        main = slice(0, 8)
        return dict(
            up=copy(0, (own, last), (own, below), to_up),
            down=copy(1, (own, first), (own, above), to_down),
            main_next=copy(2, (high, main), (from_high, main), to_next),
            main_prev=copy(3, (low, main), (from_low, main), to_prev),
            below_next=copy(4, (high, below), (from_high, below), to_next),
            below_prev=copy(5, (low, below), (from_low, below), to_prev),
            above_next=copy(4, (high, above), (from_high, above), to_next),
            above_prev=copy(5, (low, above), (from_low, above), to_prev),
            low_up=copy(6, (from_high, last), (from_high, below), to_up),
            high_up=copy(7, (from_low, last), (from_low, below), to_up),
            low_down=copy(6, (from_high, first), (from_high, above), to_down),
            high_down=copy(7, (from_low, first), (from_low, above), to_down),
        )

    FIRST = ("up", "down", "main_next", "main_prev")
    ROWS_0 = ("low_up", "high_up", "below_next", "below_prev")
    ROWS_1 = ("low_down", "high_down", "above_next", "above_prev")

    def on_core(number, action):
        pl.when(core == number)(action)

    def begin(j, c):
        start(step_copies(j, c), *FIRST)

    def pass_outer(j, c):
        copies = step_copies(j, c)
        received(copies, "up", "down")
        on_core(0, lambda: start(copies, "below_next", "below_prev"))
        on_core(1, lambda: start(copies, "above_next", "above_prev"))

    def pass_inner(j, c):
        copies = step_copies(j, c)
        for name, side, place in (("main_next", "prev", 0), ("main_prev", "next", 1)):
            received(copies, name)

            @pl.when(has[side])
            def _(place=place):
                on_core(0, lambda: start(copies, ROWS_0[place]))
                on_core(1, lambda: start(copies, ROWS_1[place]))

    def take_corners(j, c):
        copies = step_copies(j, c)

        def corners(here, theirs):
            pl.when(has["prev"])(lambda: received(copies, theirs[0]))
            pl.when(has["next"])(lambda: received(copies, theirs[1]))
            received(copies, *here[2:])

        on_core(0, lambda: corners(ROWS_0, ROWS_1))
        on_core(1, lambda: corners(ROWS_1, ROWS_0))

    def all_sent(j, c):
        copies = step_copies(j, c)
        sent(copies, *FIRST)

        def corners(mine):
            pl.when(has["prev"])(lambda: sent(copies, mine[0]))
            pl.when(has["next"])(lambda: sent(copies, mine[1]))
            sent(copies, *mine[2:])

        on_core(0, lambda: corners(ROWS_0))
        on_core(1, lambda: corners(ROWS_1))

    place_in = lax.broadcasted_iota(jnp.int32, (LANES, LANES), 0)
    place_out = lax.broadcasted_iota(jnp.int32, (LANES, LANES), 1)
    split = place_in == jnp.where(place_out < 128, 2 * place_out, 2 * place_out - 255)
    split = split.astype(jnp.bfloat16)
    taken(0)
    moved = permute(RAW[4].reshape(64, LANES), split)
    for n in range(8):
        V[n + OFF, 0:EDGE] = moved[8 * n : 8 * n + 8]
    start(setup, "up")
    start(setup, "down")

    row = lax.broadcasted_iota(jnp.int32, (WIDE, LANES), 0)
    row = along * EDGE + jnp.where(row < 12, row, row - WIDE)
    element_row = ((row >= 0) & (row < 128)).astype(jnp.float32)
    node_row = ((row >= 1) & (row < 128)).astype(jnp.float32)

    def plane_flag(n, low):
        place = across * EDGE + n
        return ((place >= low) & (place < 128)).astype(jnp.float32)

    received(setup, "up")
    received(setup, "down")
    start(setup, "next")
    start(setup, "prev")

    def inverse_plane(n):
        both = VM[n + OFF - 1] + VM[n + OFF]
        both = both + prev_y(both)
        both = both + prev_z(both)
        free = node_row * plane_flag(n, 1)
        INV[n + OFF] = free * 3.0 / jnp.where(free > 0.0, both, 1.0)

    for n in range(8):
        VM[n + OFF] = V[n + OFF] * (element_row * plane_flag(n, 0))
    for n in range(1, 8):
        inverse_plane(n)
    received(setup, "next")
    received(setup, "prev")
    for n in (-4, -3, -2, -1, 8, 9, 10, 11):
        VM[n + OFF] = V[n + OFF] * (element_row * plane_flag(n, 0))
    inverse_plane(0)
    taken(1)
    moved = permute(RAW[0:3].reshape(192, LANES), split)
    for c in range(3):
        for n in range(8):
            free = (node_row * plane_flag(n, 1))[0:EDGE]
            q = moved[64 * c + 8 * n : 64 * c + 8 * n + 8] * free
            Q0[c, n] = q
            Q[c, n] = q
            X[0, c, n + OFF, 0:EDGE] = q * INV[n + OFF, 0:EDGE]
        begin(0, c)
    taken(2)
    moved = permute(RAW[3].reshape(64, LANES), split)
    for n in range(8):
        p = moved[8 * n : 8 * n + 8]
        Q0[3, n] = p
        Q[3, n] = p
        X[0, 3, n + OFF, 0:EDGE] = p
    begin(0, 3)
    for n in (-3, -2, -1, 8, 9, 10):
        inverse_plane(n)
    for e in range(-3, 10):
        both = INV[e + OFF] + INV[e + OFF + 1]
        both = both + next_y(both)
        both = both + next_z(both)
        there = element_row * plane_flag(e, 0)
        ISC[e + OFF] = there / jnp.where(there > 0.0, 0.1875 * both, 1.0)

    def along_x(j, k, slot):
        return remote(ZS.at[j, :, 2 * k : 2 * k + 2], RELAY.at[j, slot], x_send.at[j, k], x_recv.at[j, slot], x_line[k])

    def x_begin(j):
        for k in range(4):
            pl.when(x_me != k)(lambda k=k: along_x(j, k, x_me).start())
        RELAY[j, x_me] = ZS[j, :, pl.ds(2 * x_me, 2)]

    @pl.loop(0, KRYLOV)
    def _(j):
        for c in range(3):
            pass_outer(j, c)

        def modes_of(n, c):
            return forward_modes(X[j, c, n + OFF])

        def jacobi(n, c, before, after):
            JAC[c, n + OFF] = 2.0 * X[j, c, n + OFF] - INV[n + OFF] * back_to_nodes(before, after)

        def sweep(first, last, c, before, keep_first, keep_last):
            low = modes_of(first, c)
            for e in range(first, last + 1):
                high = modes_of(e + 1, c)
                weighted = weigh(element_modes(low, high), VM[e + OFF])
                after = from_after(weighted)
                if before is not None:
                    jacobi(e, c, before, after)
                elif keep_first is not None:
                    for m in range(4):
                        MID[c, keep_first, m] = after[m]
                before = from_before(weighted)
                low = high
            if keep_last is not None:
                for m in range(4):
                    MID[c, keep_last, m] = before[m]
            return before

        for c in range(3):
            sweep(0, 6, c, None, 0, 1)
        pass_outer(j, 3)
        for c in range(4):
            pass_inner(j, c)

        for c in range(3):
            take_corners(j, c)
            before = sweep(-4, -1, c, None, None, None)
            jacobi(0, c, before, [MID[c, 0, m] for m in range(4)])
            sweep(7, 10, c, [MID[c, 1, m] for m in range(4)], None, None)

        take_corners(j, 3)

        @pl.when(j == 1)
        def _():
            x_begin(0)

        @pl.when(j == 2)
        def _():
            x_begin(1)

        low = None
        for n in range(-3, 11):
            high, own = divergence_halves([JAC[c, n + OFF] for c in range(3)])
            if low is not None:
                e = n - 1
                defect = 0.25 * (high + low) - X[j, 3, e + OFF]
                MD[e + OFF] = defect
                P1[e + OFF] = defect * ISC[e + OFF]
            low = own
        low = None
        for n in range(-2, 10):
            slope = gradient(P1[n + OFF - 1], P1[n + OFF])
            scale = 0.25 * INV[n + OFF]
            high, own = divergence_halves([scale * slope[c] for c in range(3)])
            if low is not None:
                e = n - 1
                PN[e + OFF] = P1[e + OFF] + (MD[e + OFF] - 0.25 * (high + low)) * ISC[e + OFF]
            low = own
        for n in range(-1, 9):
            slope = gradient(PN[n + OFF - 1], PN[n + OFF])
            scale = 0.25 * INV[n + OFF]
            for c in range(3):
                z = JAC[c, n + OFF] - scale * slope[c]
                Z[c, n + OFF] = z
                if 0 <= n < 8:
                    ZS[j, c, n] = z[0:EDGE]
            if 0 <= n < 8:
                ZS[j, 3, n] = PN[n + OFF, 0:EDGE]
        @pl.when(j == 2)
        def _():
            x_begin(2)

        for c in range(3):
            low = forward_modes(Z[c, OFF - 1])
            before = None
            for e in range(-1, 8):
                high = forward_modes(Z[c, e + 1 + OFF])
                modes = element_modes(low, high)
                place = (0, 2, 4)[c]
                if e >= 0:
                    own = modes[place][0:EDGE]
                    DIV[e] = own if c == 0 else DIV[e] + own
                weighted = list(weigh(modes, VM[e + OFF]))
                weighted[place] = weighted[place] + 0.25 * PN[e + OFF]
                after = from_after(weighted)
                if before is not None:
                    free = (node_row * plane_flag(e, 1))[0:EDGE]
                    w = back_to_nodes(before, after)[0:EDGE] * free
                    W[j, c, e] = w
                    q = w - Q[c, e]
                    Q[c, e] = q
                    X[j + 1, c, e + OFF, 0:EDGE] = q * INV[e + OFF, 0:EDGE]
                before = from_before(weighted)
                low = high
            pl.when(j < KRYLOV - 1)(lambda c=c: begin(j + 1, c))
        for e in range(8):
            w = 0.25 * DIV[e]
            W[j, 3, e] = w
            q = w - Q[3, e]
            Q[3, e] = q
            X[j + 1, 3, e + OFF, 0:EDGE] = q

        pl.when(j < KRYLOV - 1)(lambda: begin(j + 1, 3))

        def inner(other):
            total = None
            for n in range(8):
                for c in range(4):
                    term = W[j, c, n] * other(c, n)
                    total = term if total is None else total + term
            return fold(total)

        DOT[j * 4 + 3] = inner(lambda c, n: Q0[c, n])

        @pl.loop(0, j + 1)
        def _(k):
            DOT[j * 4 + k] = inner(lambda c, n: W[k, c, n])

    order = [(0, 0), (1, 0), (2, 0), (1, 1), (2, 1), (2, 2), (0, 3), (1, 3), (2, 3)]
    rows16 = lax.broadcasted_iota(jnp.int32, (16, 128), 0)
    stacked = jnp.zeros((16, 128), jnp.float32)
    for place, (a, b) in enumerate(order):
        line = jnp.sum(DOT[a * 4 + b], axis=0, keepdims=True)
        stacked = jnp.where(rows16 == place, line, stacked)
    folded = stacked + pltpu.roll(stacked, 64, 1)
    left = lax.broadcasted_iota(jnp.int32, (8, 128), 1) < 64
    tile = jnp.where(left, folded[0:8], folded[8:16])

    def reduce(tile, stage, buffer, me, peers, send, recv):
        PART[stage] = tile

        def copy(i, slot):
            return remote(PART.at[stage], buffer.at[slot], send.at[i], recv.at[slot], peers[i][0])

        for i in range(15):
            copy(i, me).start()
        buffer[me] = tile
        for i in reversed(range(15)):
            copy(i, peers[i][1]).wait_recv()
        total = buffer[0]
        for i in range(1, 16):
            total = total + buffer[i]
        for i in range(15):
            copy(i, me).wait_send()
        return total

    tile = reduce(tile, 0, ARB, b_me, b_peers, b_send, b_recv)
    tile = reduce(tile, 1, ARA, a_me, a_peers, a_send, a_recv)
    sums_a = jnp.sum(jnp.where(left, tile, 0.0), axis=1, keepdims=True)
    sums_b = jnp.sum(jnp.where(left, 0.0, tile), axis=1, keepdims=True)
    a00, a10, a20, a11, a21, a22, b0, b1 = [sums_a[i : i + 1] for i in range(8)]
    b2 = sums_b[0:1]
    l00 = jnp.sqrt(a00)
    l10 = a10 / l00
    l20 = a20 / l00
    l11 = jnp.sqrt(a11 - l10 * l10)
    l21 = (a21 - l20 * l10) / l11
    l22 = jnp.sqrt(a22 - l20 * l20 - l21 * l21)
    y0 = b0 / l00
    y1 = (b1 - l10 * y0) / l11
    y2 = (b2 - l20 * y0 - l21 * y1) / l22
    c2 = y2 / l22
    c1 = (y1 - l21 * c2) / l11
    c0 = (y0 - l10 * c1 - l20 * c2) / l00
    join = place_out == jnp.where(place_in < 128, 2 * place_in, 2 * place_in - 255)
    join = join.astype(jnp.bfloat16)
    def back(k):
        return remote(OUT.at[k], HOME.at[:, :, rows(my_tile)], out_send.at[k], out_recv.at[my_tile], z_home[k])

    def arrive(i, holder):
        return remote(OUT.at[0], HOME.at[:, :, EDGE * i : EDGE * i + EDGE], out_send.at[0], out_recv.at[i], holder)

    def b_peer_of(i):
        tile = depth * 4 + i
        return same_xy + tile // 4 * 4, lax.rem(tile // 2, 2) * 2 + lax.rem(tile, 2)

    def stay(k):
        return pltpu.make_async_copy(OUT.at[k], HOME.at[:, :, rows(my_tile)], out_local.at[0])

    for k in range(4):
        for j in range(KRYLOV):
            pl.when(x_me != k)(lambda j=j, k=k: along_x(j, k, k).wait_recv())
    mixed = c0 * RELAY[0] + c1 * RELAY[1] + c2 * RELAY[2]
    OUT[...] = permute(mixed.reshape(256, LANES), join).reshape(4, 4, 2, EDGE, LANES)
    for k in range(4):
        pl.when(is_me(z_home[k]))(lambda k=k: stay(k).start())
        pl.when(jnp.logical_not(is_me(z_home[k])))(lambda k=k: back(k).start())

    sent(setup, *setup)

    @pl.loop(0, KRYLOV)
    def _(j):
        for c in range(4):
            all_sent(j, c)

    for t in range(3):
        for i in range(4):
            pl.when(jnp.logical_not(is_me(goes_to[i])))(lambda t=t, i=i: give(t, i).wait_send())

    for i in range(4):
        holder = b_peer_of(i)
        pl.when(is_me(holder))(lambda: stay(0).wait())
        pl.when(jnp.logical_not(is_me(holder)))(lambda i=i, holder=holder: arrive(i, holder).wait_recv())
    for c in range(3):
        vel_ref[c] = HOME[c]
    pre_ref[...] = HOME[3]
    for k in range(4):
        for j in range(KRYLOV):
            pl.when(x_me != k)(lambda j=j, k=k: along_x(j, k, x_me).wait_send())
        pl.when(jnp.logical_not(is_me(z_home[k])))(lambda k=k: back(k).wait_send())


def body(forcing, source, viscosity):
    f32 = jnp.float32
    vmem = lambda *shape: pltpu.VMEM(shape, f32)
    dma = lambda *shape: pltpu.SemaphoreType.DMA(shape)
    K = KRYLOV
    return pl.pallas_call(
        kernel,
        out_shape=(
            jax.ShapeDtypeStruct((3, 2, 32, LANES), f32),
            jax.ShapeDtypeStruct((2, 32, LANES), f32),
        ),
        in_specs=[pl.BlockSpec(memory_space=pl.ANY)] * 3,
        out_specs=(pl.BlockSpec(memory_space=pltpu.VMEM), pl.BlockSpec(memory_space=pltpu.VMEM)),
        scratch_shapes=[
            vmem(5, EDGE, EDGE, LANES),
            vmem(WIDE, WIDE, LANES),
            vmem(WIDE, WIDE, LANES),
            vmem(K + 1, 4, WIDE, WIDE, LANES),
            vmem(WIDE, WIDE, LANES),
            vmem(WIDE, WIDE, LANES),
            vmem(3, WIDE, WIDE, LANES),
            vmem(3, 2, 4, WIDE, LANES),
            vmem(WIDE, WIDE, LANES),
            vmem(WIDE, WIDE, LANES),
            vmem(WIDE, WIDE, LANES),
            vmem(3, WIDE, WIDE, LANES),
            vmem(K, 4, EDGE, EDGE, LANES),
            vmem(EDGE, EDGE, LANES),
            vmem(K, 4, EDGE, EDGE, LANES),
            vmem(4, EDGE, EDGE, LANES),
            vmem(4, EDGE, EDGE, LANES),
            vmem(4, 4, 2, EDGE, LANES),
            vmem(K, 4, 4, 2, EDGE, LANES),
            vmem(4, 2, 32, LANES),
            vmem(4 * K, 8, 128),
            vmem(16, 8, 128),
            vmem(16, 8, 128),
            vmem(2, 8, 128),
            dma(3, 4),
            dma(3, 4),
            dma(3),
            dma(4),
            dma(4),
            dma(K, 4, 8),
            dma(K, 4, 8),
            dma(K, 4),
            dma(K, 4),
            dma(4),
            dma(4),
            dma(1),
            dma(16),
            dma(16),
            dma(16),
            dma(16),
        ],
        compiler_params=pltpu.CompilerParams(
            collective_id=0, has_side_effects=True, vmem_limit_bytes=60 * 1024 * 1024
        ),
        name="stokes_cycle",
    )(forcing, source, viscosity)


def solution(mesh):
    placed = (P(None, "slab", "depth", None), P("slab", "depth", None), P("slab", "depth", None))
    return jax.shard_map(
        body,
        mesh=mesh,
        in_specs=placed,
        out_specs=(P(None, "slab", "depth", None), P("slab", "depth", None)),
        check_vma=False,
    )
```

```python
import jax
import jax.numpy as jnp
from jax import lax
from jax.experimental import pallas as pl
from jax.experimental.pallas import tpu as pltpu
from jax.sharding import PartitionSpec as P

KRYLOV = 3
EDGE = 8
WIDE = 16
OFF = 4
LANES = 256
MESH_ID = pl.DeviceIdType.MESH


def next_z(x):
    return jnp.concatenate([x[:, 128:], pltpu.roll(x[:, :128], 127, 1)], axis=1)


def prev_z(x):
    return jnp.concatenate([pltpu.roll(x[:, 128:], 1, 1), x[:, :128]], axis=1)


def permute(x, matrix):
    parts = []
    for _ in range(3):
        part = x.astype(jnp.bfloat16)
        x = x - part.astype(jnp.float32)
        parts.append(part)
    count = x.shape[0]
    moved = jnp.dot(jnp.concatenate(parts, axis=0), matrix, preferred_element_type=jnp.float32)
    return moved[0:count] + (moved[count : 2 * count] + moved[2 * count :])


def next_y(x):
    return pltpu.roll(x, WIDE - 1, 0)


def prev_y(x):
    return pltpu.roll(x, 1, 0)


def forward_modes(u):
    ahead = next_z(u)
    zs = ahead + u
    zd = ahead - u
    zs_ahead = next_y(zs)
    zd_ahead = next_y(zd)
    return zs_ahead + zs, zs_ahead - zs, zd_ahead + zd, zd_ahead - zd


def element_modes(low, high):
    return (
        high[0] - low[0],
        high[1] - low[1],
        high[1] + low[1],
        high[2] - low[2],
        high[2] + low[2],
        high[3] - low[3],
        high[3] + low[3],
    )


def weigh(modes, visc):
    v16 = visc * (1.0 / 16.0)
    v24 = visc * (1.0 / 24.0)
    v48 = visc * (1.0 / 48.0)
    return (
        modes[0] * v16,
        modes[1] * v24,
        modes[2] * v16,
        modes[3] * v24,
        modes[4] * v16,
        modes[5] * v48,
        modes[6] * v24,
    )


def from_before(modes):
    return modes[0], modes[2] + modes[1], modes[4] + modes[3], modes[6] + modes[5]


def from_after(modes):
    return modes[0], modes[2] - modes[1], modes[4] - modes[3], modes[6] - modes[5]


def back_to_nodes(before, after):
    ss = before[0] - after[0]
    ds = before[1] + after[1]
    sd = before[2] + after[2]
    dd = before[3] + after[3]
    zs = (ss - ds) + prev_y(ss + ds)
    zd = (sd - dd) + prev_y(sd + dd)
    return (zs - zd) + prev_z(zs + zd)


def divergence_halves(u):
    x_ahead = next_z(u[0])
    y_ahead = next_z(u[1])
    z_ahead = next_z(u[2])
    zs_x = x_ahead + u[0]
    zs_y = y_ahead + u[1]
    zd_z = z_ahead - u[2]
    ss_x = next_y(zs_x) + zs_x
    rest = (zd_z - zs_y) + next_y(zd_z + zs_y)
    return rest + ss_x, rest - ss_x


def gradient(before, after):
    diff = before - after
    both = before + after
    diff_y = diff + prev_y(diff)
    both_back = prev_y(both)
    sum_y = both + both_back
    dif_y = both_back - both
    return (
        diff_y + prev_z(diff_y),
        dif_y + prev_z(dif_y),
        prev_z(sum_y) - sum_y,
    )


def fold(product):
    return product[:, :128] + product[:, 128:]


def block_of(slab, depth):
    x = lax.rem(slab, 4)
    y = slab // 16
    z = lax.rem(slab // 4, 4) * 2 + depth // 2
    odd = lax.rem(y, 2)
    return y * 4 + x + odd * (3 - 2 * x), z * 2 + lax.rem(depth, 2)


def device_of(across, along):
    y = across // 4
    place = lax.rem(across, 4)
    odd = lax.rem(y, 2)
    x = place + odd * (3 - 2 * place)
    z = along // 2
    return y * 16 + (z // 2) * 4 + x, lax.rem(z, 2) * 2 + lax.rem(along, 2)


def kernel(
    f_hbm, s_hbm, v_hbm, vel_ref, pre_ref,
    RAW, V, VM, X, INV, ISC, JAC, MID, MD, P1, PN, Z, ZS, DIV, W, Q, Q0, OUT, RELAY, HOME, DOT, ARA, ARB, PART,
    in_send, in_recv, in_local, s_send, s_recv, i_send, i_recv, x_send, x_recv, out_send, out_recv, out_local,
    a_send, a_recv, b_send, b_recv,
):
    slab = lax.axis_index("slab")
    depth = lax.axis_index("depth")
    across, along = block_of(slab, depth)
    has = dict(next=across < 15, prev=across > 0, up=along < 15, down=along > 0)
    opposite = dict(next="prev", prev="next", up="down", down="up")
    to_next = device_of(lax.rem(across + 1, 16), along)
    to_prev = device_of(lax.rem(across + 15, 16), along)
    to_up = device_of(across, lax.rem(along + 1, 16))
    to_down = device_of(across, lax.rem(along + 15, 16))

    my_k = lax.rem(slab, 4)
    my_tile = lax.rem(along, 4)
    goes_to = [device_of(slab // 4, depth * 4 + i) for i in range(4)]
    comes_from = [(across * 4 + k, along // 4) for k in range(4)]

    def is_me(device):
        return (device[0] == slab) & (device[1] == depth)

    core = lax.rem(depth, 2)
    x_me = lax.rem(slab, 4)
    y_me = slab // 16
    same_z = slab - x_me - y_me * 16
    same_xy = y_me * 16 + x_me
    a_me = y_me * 4 + x_me
    b_me = along
    x_at = [lax.rem(x_me + d, 4) for d in range(4)]
    y_at = [lax.rem(y_me + d, 4) for d in range(4)]
    z_at = [lax.rem(along // 2 + d, 8) for d in range(8)]
    z_slab = [same_xy + z // 2 * 4 for z in z_at]
    z_depth = [lax.rem(z, 2) * 2 for z in z_at]
    steps = [(dx, dy) for dx in range(4) for dy in range(4) if dx or dy]
    steps.sort(key=lambda d: -min(d[0], 4 - d[0]) - min(d[1], 4 - d[1]))
    a_peers = [((same_z + y_at[dy] * 16 + x_at[dx], depth), y_at[dy] * 4 + x_at[dx]) for dx, dy in steps]
    steps = [(dz, dc) for dz in range(8) for dc in range(2) if dz or dc]
    steps.sort(key=lambda d: -min(d[0], 8 - d[0]) - 0.5 * d[1])
    cores = (core, 1 - core)
    b_peers = [((z_slab[dz], z_depth[dz] + cores[dc]), z_at[dz] * 2 + cores[dc]) for dz, dc in steps]
    x_line = [(slab - x_me + k, depth) for k in range(4)]
    odd = lax.rem(y_me, 2)
    z_home = [(same_xy + 4 * (k + odd * (3 - 2 * k)), along // 4) for k in range(4)]

    barrier = pltpu.get_barrier_semaphore()

    def greet(device):
        pl.semaphore_signal(barrier, inc=1, device_id=device, device_id_type=MESH_ID)

    zeros = jnp.zeros((4, WIDE, LANES), jnp.float32)
    for name, place in (("prev", 0), ("next", 12)):

        @pl.when(jnp.logical_not(has[name]))
        def _(place=place):
            V[place : place + 4] = zeros
            for j in range(KRYLOV):
                for c in range(4):
                    X[j, c, place : place + 4] = zeros

    zeros = jnp.zeros((WIDE, 4, LANES), jnp.float32)
    for name, place in (("down", 12), ("up", 8)):

        @pl.when(jnp.logical_not(has[name]))
        def _(place=place):
            V[:, place : place + 4] = zeros
            for j in range(KRYLOV):
                for c in range(4):
                    X[j, c, :, place : place + 4] = zeros

    for device in goes_to + comes_from + [peer for peer, _ in a_peers + b_peers]:
        greet(device)
    pl.semaphore_wait(barrier, 38)

    def remote(src, dst, send, recv, peer):
        return pltpu.make_async_remote_copy(
            src_ref=src, dst_ref=dst, send_sem=send, recv_sem=recv, device_id=peer, device_id_type=MESH_ID
        )

    def rows(i):
        return pl.ds(pl.multiple_of(i * EDGE, EDGE), EDGE)

    def fields(t, i, k):
        place = RAW.at[t, pl.ds(2 * k, 2)]
        if t < 3:
            return f_hbm.at[t, :, rows(i)], place
        return (s_hbm if t == 3 else v_hbm).at[:, rows(i)], place

    def give(t, i):
        src, dst = fields(t, i, my_k)
        return remote(src, dst, in_send.at[t, i], in_recv.at[t, my_k], goes_to[i])

    def take(t, k):
        src, dst = fields(t, 0, k)
        return remote(src, dst, in_send.at[t, 0], in_recv.at[t, k], comes_from[k])

    def keep(t):
        src, dst = fields(t, my_tile, my_k)
        return pltpu.make_async_copy(src, dst, in_local.at[t])

    home = is_me(device_of(slab // 4, depth * 4 + my_tile))
    for t in (4, 0, 1, 2, 3):
        pl.when(home)(lambda t=t: keep(t).start())
        for i in range(4):
            pl.when(jnp.logical_not(is_me(goes_to[i])))(lambda t=t, i=i: give(t, i).start())

    def taken(t):
        pl.when(home)(lambda: keep(t).wait())
        for k in range(4):
            pl.when(jnp.logical_not(is_me(comes_from[k])))(lambda k=k: take(t, k).wait_recv())

    def start(copies, *names):
        for name in names:
            pl.when(has[name.split("_")[-1]])(lambda name=name: copies[name]().start())

    def received(copies, *names):
        for name in names:
            pl.when(has[opposite[name.split("_")[-1]]])(lambda name=name: copies[name]().wait_recv())

    def sent(copies, *names):
        for name in names:
            pl.when(has[name.split("_")[-1]])(lambda name=name: copies[name]().wait_send())

    def setup_copy(k, src, dst, peer):
        return lambda: remote(src, dst, s_send.at[k], s_recv.at[k], peer)

    setup = dict(
        up=setup_copy(0, V.at[4:12, 4:8], V.at[4:12, 12:16], to_up),
        down=setup_copy(1, V.at[4:12, 0:4], V.at[4:12, 8:12], to_down),
        near_next=setup_copy(2, V.at[11], V.at[3], to_next),
        far_next=setup_copy(4, V.at[8:11], V.at[0:3], to_next),
        near_prev=setup_copy(3, V.at[4:8], V.at[12:16], to_prev),
    )

    def step_copies(j, c):
        def copy(k, src, dst, peer):
            return lambda: remote(
                X.at[(j, c) + src], X.at[(j, c) + dst], i_send.at[j, c, k], i_recv.at[j, c, k], peer
            )

        high, from_high = (slice(9, 12), slice(1, 4)) if c == 3 else (slice(8, 12), slice(0, 4))
        low, from_low = (slice(4, 6), slice(12, 14)) if c == 3 else (slice(4, 8), slice(12, 16))
        own, first, last, above, below = slice(4, 12), slice(0, 4), slice(4, 8), slice(8, 12), slice(12, 16)
        main = slice(0, 8)
        return dict(
            up=copy(0, (own, last), (own, below), to_up),
            down=copy(1, (own, first), (own, above), to_down),
            main_next=copy(2, (high, main), (from_high, main), to_next),
            main_prev=copy(3, (low, main), (from_low, main), to_prev),
            below_next=copy(4, (high, below), (from_high, below), to_next),
            below_prev=copy(5, (low, below), (from_low, below), to_prev),
            above_next=copy(4, (high, above), (from_high, above), to_next),
            above_prev=copy(5, (low, above), (from_low, above), to_prev),
            low_up=copy(6, (from_high, last), (from_high, below), to_up),
            high_up=copy(7, (from_low, last), (from_low, below), to_up),
            low_down=copy(6, (from_high, first), (from_high, above), to_down),
            high_down=copy(7, (from_low, first), (from_low, above), to_down),
        )

    FIRST = ("up", "down", "main_next", "main_prev")
    ROWS_0 = ("low_up", "high_up", "below_next", "below_prev")
    ROWS_1 = ("low_down", "high_down", "above_next", "above_prev")

    def on_core(number, action):
        pl.when(core == number)(action)

    def begin(j, c):
        start(step_copies(j, c), *FIRST)

    def pass_outer(j, c):
        copies = step_copies(j, c)
        received(copies, "up", "down")
        on_core(0, lambda: start(copies, "below_next", "below_prev"))
        on_core(1, lambda: start(copies, "above_next", "above_prev"))

    def pass_inner(j, c):
        copies = step_copies(j, c)
        for name, side, place in (("main_next", "prev", 0), ("main_prev", "next", 1)):
            received(copies, name)

            @pl.when(has[side])
            def _(place=place):
                on_core(0, lambda: start(copies, ROWS_0[place]))
                on_core(1, lambda: start(copies, ROWS_1[place]))

    def take_corners(j, c):
        copies = step_copies(j, c)

        def corners(here, theirs):
            pl.when(has["prev"])(lambda: received(copies, theirs[0]))
            pl.when(has["next"])(lambda: received(copies, theirs[1]))
            received(copies, *here[2:])

        on_core(0, lambda: corners(ROWS_0, ROWS_1))
        on_core(1, lambda: corners(ROWS_1, ROWS_0))

    def all_sent(j, c):
        copies = step_copies(j, c)
        sent(copies, *FIRST)

        def corners(mine):
            pl.when(has["prev"])(lambda: sent(copies, mine[0]))
            pl.when(has["next"])(lambda: sent(copies, mine[1]))
            sent(copies, *mine[2:])

        on_core(0, lambda: corners(ROWS_0))
        on_core(1, lambda: corners(ROWS_1))

    place_in = lax.broadcasted_iota(jnp.int32, (LANES, LANES), 0)
    place_out = lax.broadcasted_iota(jnp.int32, (LANES, LANES), 1)
    split = place_in == jnp.where(place_out < 128, 2 * place_out, 2 * place_out - 255)
    split = split.astype(jnp.bfloat16)
    taken(4)
    moved = permute(RAW[4].reshape(64, LANES), split)
    for n in range(8):
        V[n + OFF, 0:EDGE] = moved[8 * n : 8 * n + 8]
    start(setup, "up")
    start(setup, "down")

    row = lax.broadcasted_iota(jnp.int32, (WIDE, LANES), 0)
    row = along * EDGE + jnp.where(row < 12, row, row - WIDE)
    element_row = ((row >= 0) & (row < 128)).astype(jnp.float32)
    node_row = ((row >= 1) & (row < 128)).astype(jnp.float32)

    def plane_flag(n, low):
        place = across * EDGE + n
        return ((place >= low) & (place < 128)).astype(jnp.float32)

    received(setup, "up")
    received(setup, "down")
    start(setup, "near_next", "far_next", "near_prev")

    def inverse_plane(n):
        both = VM[n + OFF - 1] + VM[n + OFF]
        both = both + prev_y(both)
        both = both + prev_z(both)
        free = node_row * plane_flag(n, 1)
        INV[n + OFF] = free * 3.0 / jnp.where(free > 0.0, both, 1.0)

    for n in range(8):
        VM[n + OFF] = V[n + OFF] * (element_row * plane_flag(n, 0))
    for n in range(1, 8):
        inverse_plane(n)
    received(setup, "near_next")
    VM[OFF - 1] = V[OFF - 1] * (element_row * plane_flag(-1, 0))
    inverse_plane(0)
    for t in range(4):
        taken(t)
        moved = permute(RAW[t].reshape(64, LANES), split)
        for n in range(8):
            q = moved[8 * n : 8 * n + 8]
            if t < 3:
                q = q * (node_row * plane_flag(n, 1))[0:EDGE]
            Q0[t, n] = q
            Q[t, n] = q
            X[0, t, n + OFF, 0:EDGE] = q * INV[n + OFF, 0:EDGE] if t < 3 else q
        begin(0, t)
    received(setup, "far_next", "near_prev")
    for n in (-4, -3, -2, 8, 9, 10, 11):
        VM[n + OFF] = V[n + OFF] * (element_row * plane_flag(n, 0))
    for n in (-3, -2, -1, 8, 9, 10):
        inverse_plane(n)
    for e in range(-3, 10):
        both = INV[e + OFF] + INV[e + OFF + 1]
        both = both + next_y(both)
        both = both + next_z(both)
        there = element_row * plane_flag(e, 0)
        ISC[e + OFF] = there / jnp.where(there > 0.0, 0.1875 * both, 1.0)

    def along_x(j, k, slot):
        return remote(ZS.at[j, :, 2 * k : 2 * k + 2], RELAY.at[j, slot], x_send.at[j, k], x_recv.at[j, slot], x_line[k])

    def x_begin(j):
        for k in range(4):
            pl.when(x_me != k)(lambda k=k: along_x(j, k, x_me).start())
        RELAY[j, x_me] = ZS[j, :, pl.ds(2 * x_me, 2)]

    @pl.loop(0, KRYLOV)
    def _(j):
        for c in range(3):
            pass_outer(j, c)

        def modes_of(n, c):
            return forward_modes(X[j, c, n + OFF])

        def jacobi(n, c, before, after):
            JAC[c, n + OFF] = 2.0 * X[j, c, n + OFF] - INV[n + OFF] * back_to_nodes(before, after)

        def sweep(first, last, c, before, keep_first, keep_last):
            low = modes_of(first, c)
            for e in range(first, last + 1):
                high = modes_of(e + 1, c)
                weighted = weigh(element_modes(low, high), VM[e + OFF])
                after = from_after(weighted)
                if before is not None:
                    jacobi(e, c, before, after)
                elif keep_first is not None:
                    for m in range(4):
                        MID[c, keep_first, m] = after[m]
                before = from_before(weighted)
                low = high
            if keep_last is not None:
                for m in range(4):
                    MID[c, keep_last, m] = before[m]
            return before

        for c in range(3):
            sweep(0, 6, c, None, 0, 1)
        pass_outer(j, 3)
        for c in range(4):
            pass_inner(j, c)

        for c in range(3):
            take_corners(j, c)
            before = sweep(-4, -1, c, None, None, None)
            jacobi(0, c, before, [MID[c, 0, m] for m in range(4)])
            sweep(7, 10, c, [MID[c, 1, m] for m in range(4)], None, None)

        take_corners(j, 3)

        @pl.when(j == 1)
        def _():
            x_begin(0)

        @pl.when(j == 2)
        def _():
            x_begin(1)

        low = None
        for n in range(-3, 11):
            high, own = divergence_halves([JAC[c, n + OFF] for c in range(3)])
            if low is not None:
                e = n - 1
                defect = 0.25 * (high + low) - X[j, 3, e + OFF]
                MD[e + OFF] = defect
                P1[e + OFF] = defect * ISC[e + OFF]
            low = own
        low = None
        for n in range(-2, 10):
            slope = gradient(P1[n + OFF - 1], P1[n + OFF])
            scale = 0.25 * INV[n + OFF]
            high, own = divergence_halves([scale * slope[c] for c in range(3)])
            if low is not None:
                e = n - 1
                PN[e + OFF] = P1[e + OFF] + (MD[e + OFF] - 0.25 * (high + low)) * ISC[e + OFF]
            low = own
        for n in range(-1, 9):
            slope = gradient(PN[n + OFF - 1], PN[n + OFF])
            scale = 0.25 * INV[n + OFF]
            for c in range(3):
                z = JAC[c, n + OFF] - scale * slope[c]
                Z[c, n + OFF] = z
                if 0 <= n < 8:
                    ZS[j, c, n] = z[0:EDGE]
            if 0 <= n < 8:
                ZS[j, 3, n] = PN[n + OFF, 0:EDGE]
        @pl.when(j == 2)
        def _():
            x_begin(2)

        for c in range(3):
            low = forward_modes(Z[c, OFF - 1])
            before = None
            for e in range(-1, 8):
                high = forward_modes(Z[c, e + 1 + OFF])
                modes = element_modes(low, high)
                place = (0, 2, 4)[c]
                if e >= 0:
                    own = modes[place][0:EDGE]
                    DIV[e] = own if c == 0 else DIV[e] + own
                weighted = list(weigh(modes, VM[e + OFF]))
                weighted[place] = weighted[place] + 0.25 * PN[e + OFF]
                after = from_after(weighted)
                if before is not None:
                    free = (node_row * plane_flag(e, 1))[0:EDGE]
                    w = back_to_nodes(before, after)[0:EDGE] * free
                    W[j, c, e] = w
                    q = w - Q[c, e]
                    Q[c, e] = q
                    X[j + 1, c, e + OFF, 0:EDGE] = q * INV[e + OFF, 0:EDGE]
                before = from_before(weighted)
                low = high
            pl.when(j < KRYLOV - 1)(lambda c=c: begin(j + 1, c))
        for e in range(8):
            w = 0.25 * DIV[e]
            W[j, 3, e] = w
            q = w - Q[3, e]
            Q[3, e] = q
            X[j + 1, 3, e + OFF, 0:EDGE] = q

        pl.when(j < KRYLOV - 1)(lambda: begin(j + 1, 3))

        def inner(other):
            total = None
            for n in range(8):
                for c in range(4):
                    term = W[j, c, n] * other(c, n)
                    total = term if total is None else total + term
            return fold(total)

        DOT[j * 4 + 3] = inner(lambda c, n: Q0[c, n])

        @pl.loop(0, j + 1)
        def _(k):
            DOT[j * 4 + k] = inner(lambda c, n: W[k, c, n])

    order = [(0, 0), (1, 0), (2, 0), (1, 1), (2, 1), (2, 2), (0, 3), (1, 3), (2, 3)]
    rows16 = lax.broadcasted_iota(jnp.int32, (16, 128), 0)
    stacked = jnp.zeros((16, 128), jnp.float32)
    for place, (a, b) in enumerate(order):
        line = jnp.sum(DOT[a * 4 + b], axis=0, keepdims=True)
        stacked = jnp.where(rows16 == place, line, stacked)
    folded = stacked + pltpu.roll(stacked, 64, 1)
    left = lax.broadcasted_iota(jnp.int32, (8, 128), 1) < 64
    tile = jnp.where(left, folded[0:8], folded[8:16])

    def reduce(tile, stage, buffer, me, peers, send, recv, meanwhile):
        PART[stage] = tile

        def copy(i, slot):
            return remote(PART.at[stage], buffer.at[slot], send.at[i], recv.at[slot], peers[i][0])

        for i in range(15):
            copy(i, me).start()
        buffer[me] = tile
        meanwhile()
        for i in reversed(range(15)):
            copy(i, peers[i][1]).wait_recv()
        total = buffer[0]
        for i in range(1, 16):
            total = total + buffer[i]
        for i in range(15):
            copy(i, me).wait_send()
        return total

    join = place_out == jnp.where(place_in < 128, 2 * place_in, 2 * place_in - 255)
    join = join.astype(jnp.bfloat16)

    def x_taken(j):
        for k in range(4):
            pl.when(x_me != k)(lambda k=k: along_x(j, k, k).wait_recv())
        RELAY[j] = permute(RELAY[j].reshape(256, LANES), join).reshape(4, 4, 2, EDGE, LANES)

    def x_taken_early():
        x_taken(0)
        x_taken(1)

    tile = reduce(tile, 0, ARB, b_me, b_peers, b_send, b_recv, x_taken_early)
    tile = reduce(tile, 1, ARA, a_me, a_peers, a_send, a_recv, lambda: x_taken(2))
    sums_a = jnp.sum(jnp.where(left, tile, 0.0), axis=1, keepdims=True)
    sums_b = jnp.sum(jnp.where(left, 0.0, tile), axis=1, keepdims=True)
    a00, a10, a20, a11, a21, a22, b0, b1 = [sums_a[i : i + 1] for i in range(8)]
    b2 = sums_b[0:1]
    l00 = jnp.sqrt(a00)
    l10 = a10 / l00
    l20 = a20 / l00
    l11 = jnp.sqrt(a11 - l10 * l10)
    l21 = (a21 - l20 * l10) / l11
    l22 = jnp.sqrt(a22 - l20 * l20 - l21 * l21)
    y0 = b0 / l00
    y1 = (b1 - l10 * y0) / l11
    y2 = (b2 - l20 * y0 - l21 * y1) / l22
    c2 = y2 / l22
    c1 = (y1 - l21 * c2) / l11
    c0 = (y0 - l10 * c1 - l20 * c2) / l00
    def back(k):
        return remote(OUT.at[k], HOME.at[:, :, rows(my_tile)], out_send.at[k], out_recv.at[my_tile], z_home[k])

    def arrive(i, holder):
        return remote(OUT.at[0], HOME.at[:, :, EDGE * i : EDGE * i + EDGE], out_send.at[0], out_recv.at[i], holder)

    def b_peer_of(i):
        tile = depth * 4 + i
        return same_xy + tile // 4 * 4, lax.rem(tile // 2, 2) * 2 + lax.rem(tile, 2)

    def stay(k):
        return pltpu.make_async_copy(OUT.at[k], HOME.at[:, :, rows(my_tile)], out_local.at[0])

    for k in range(4):
        OUT[k] = c0 * RELAY[0, k] + c1 * RELAY[1, k] + c2 * RELAY[2, k]
        pl.when(is_me(z_home[k]))(lambda k=k: stay(k).start())
        pl.when(jnp.logical_not(is_me(z_home[k])))(lambda k=k: back(k).start())

    sent(setup, *setup)

    @pl.loop(0, KRYLOV)
    def _(j):
        for c in range(4):
            all_sent(j, c)

    for t in range(5):
        for i in range(4):
            pl.when(jnp.logical_not(is_me(goes_to[i])))(lambda t=t, i=i: give(t, i).wait_send())

    for i in range(4):
        holder = b_peer_of(i)
        pl.when(is_me(holder))(lambda: stay(0).wait())
        pl.when(jnp.logical_not(is_me(holder)))(lambda i=i, holder=holder: arrive(i, holder).wait_recv())
    for c in range(3):
        vel_ref[c] = HOME[c]
    pre_ref[...] = HOME[3]
    for k in range(4):
        for j in range(KRYLOV):
            pl.when(x_me != k)(lambda j=j, k=k: along_x(j, k, x_me).wait_send())
        pl.when(jnp.logical_not(is_me(z_home[k])))(lambda k=k: back(k).wait_send())


def body(forcing, source, viscosity):
    f32 = jnp.float32
    vmem = lambda *shape: pltpu.VMEM(shape, f32)
    dma = lambda *shape: pltpu.SemaphoreType.DMA(shape)
    K = KRYLOV
    return pl.pallas_call(
        kernel,
        out_shape=(
            jax.ShapeDtypeStruct((3, 2, 32, LANES), f32),
            jax.ShapeDtypeStruct((2, 32, LANES), f32),
        ),
        in_specs=[pl.BlockSpec(memory_space=pl.ANY)] * 3,
        out_specs=(pl.BlockSpec(memory_space=pltpu.VMEM), pl.BlockSpec(memory_space=pltpu.VMEM)),
        scratch_shapes=[
            vmem(5, EDGE, EDGE, LANES),
            vmem(WIDE, WIDE, LANES),
            vmem(WIDE, WIDE, LANES),
            vmem(K + 1, 4, WIDE, WIDE, LANES),
            vmem(WIDE, WIDE, LANES),
            vmem(WIDE, WIDE, LANES),
            vmem(3, WIDE, WIDE, LANES),
            vmem(3, 2, 4, WIDE, LANES),
            vmem(WIDE, WIDE, LANES),
            vmem(WIDE, WIDE, LANES),
            vmem(WIDE, WIDE, LANES),
            vmem(3, WIDE, WIDE, LANES),
            vmem(K, 4, EDGE, EDGE, LANES),
            vmem(EDGE, EDGE, LANES),
            vmem(K, 4, EDGE, EDGE, LANES),
            vmem(4, EDGE, EDGE, LANES),
            vmem(4, EDGE, EDGE, LANES),
            vmem(4, 4, 2, EDGE, LANES),
            vmem(K, 4, 4, 2, EDGE, LANES),
            vmem(4, 2, 32, LANES),
            vmem(4 * K, 8, 128),
            vmem(16, 8, 128),
            vmem(16, 8, 128),
            vmem(2, 8, 128),
            dma(5, 4),
            dma(5, 4),
            dma(5),
            dma(6),
            dma(6),
            dma(K, 4, 8),
            dma(K, 4, 8),
            dma(K, 4),
            dma(K, 4),
            dma(4),
            dma(4),
            dma(1),
            dma(16),
            dma(16),
            dma(16),
            dma(16),
        ],
        compiler_params=pltpu.CompilerParams(
            collective_id=0, has_side_effects=True, vmem_limit_bytes=60 * 1024 * 1024
        ),
        name="stokes_cycle",
    )(forcing, source, viscosity)


def solution(mesh):
    placed = (P(None, "slab", "depth", None), P("slab", "depth", None), P("slab", "depth", None))
    return jax.shard_map(
        body,
        mesh=mesh,
        in_specs=placed,
        out_specs=(P(None, "slab", "depth", None), P("slab", "depth", None)),
        check_vma=False,
    )
```

```python
import jax
import jax.numpy as jnp
from jax import lax
from jax.experimental import pallas as pl
from jax.experimental.pallas import tpu as pltpu
from jax.sharding import PartitionSpec as P

KRYLOV = 3
EDGE = 8
WIDE = 16
OFF = 4
LANES = 256
MESH_ID = pl.DeviceIdType.MESH


def next_z(x):
    return jnp.concatenate([x[:, 128:], pltpu.roll(x[:, :128], 127, 1)], axis=1)


def prev_z(x):
    return jnp.concatenate([pltpu.roll(x[:, 128:], 1, 1), x[:, :128]], axis=1)


def permute(x, matrix):
    parts = []
    for _ in range(3):
        part = x.astype(jnp.bfloat16)
        x = x - part.astype(jnp.float32)
        parts.append(part)
    count = x.shape[0]
    moved = jnp.dot(jnp.concatenate(parts, axis=0), matrix, preferred_element_type=jnp.float32)
    return moved[0:count] + (moved[count : 2 * count] + moved[2 * count :])


def next_y(x):
    return pltpu.roll(x, WIDE - 1, 0)


def prev_y(x):
    return pltpu.roll(x, 1, 0)


def forward_modes(u):
    ahead = next_z(u)
    zs = ahead + u
    zd = ahead - u
    zs_ahead = next_y(zs)
    zd_ahead = next_y(zd)
    return zs_ahead + zs, zs_ahead - zs, zd_ahead + zd, zd_ahead - zd


def element_modes(low, high):
    return (
        high[0] - low[0],
        high[1] - low[1],
        high[1] + low[1],
        high[2] - low[2],
        high[2] + low[2],
        high[3] - low[3],
        high[3] + low[3],
    )


def weigh(modes, visc):
    v16 = visc * (1.0 / 16.0)
    v24 = visc * (1.0 / 24.0)
    v48 = visc * (1.0 / 48.0)
    return (
        modes[0] * v16,
        modes[1] * v24,
        modes[2] * v16,
        modes[3] * v24,
        modes[4] * v16,
        modes[5] * v48,
        modes[6] * v24,
    )


def from_before(modes):
    return modes[0], modes[2] + modes[1], modes[4] + modes[3], modes[6] + modes[5]


def from_after(modes):
    return modes[0], modes[2] - modes[1], modes[4] - modes[3], modes[6] - modes[5]


def back_to_nodes(before, after):
    ss = before[0] - after[0]
    ds = before[1] + after[1]
    sd = before[2] + after[2]
    dd = before[3] + after[3]
    zs = (ss - ds) + prev_y(ss + ds)
    zd = (sd - dd) + prev_y(sd + dd)
    return (zs - zd) + prev_z(zs + zd)


def divergence_halves(u):
    x_ahead = next_z(u[0])
    y_ahead = next_z(u[1])
    z_ahead = next_z(u[2])
    zs_x = x_ahead + u[0]
    zs_y = y_ahead + u[1]
    zd_z = z_ahead - u[2]
    ss_x = next_y(zs_x) + zs_x
    rest = (zd_z - zs_y) + next_y(zd_z + zs_y)
    return rest + ss_x, rest - ss_x


def gradient(before, after):
    diff = before - after
    both = before + after
    diff_y = diff + prev_y(diff)
    both_back = prev_y(both)
    sum_y = both + both_back
    dif_y = both_back - both
    return (
        diff_y + prev_z(diff_y),
        dif_y + prev_z(dif_y),
        prev_z(sum_y) - sum_y,
    )


def fold(product):
    return product[:, :128] + product[:, 128:]


def block_of(slab, depth):
    x = lax.rem(slab, 4)
    y = slab // 16
    z = lax.rem(slab // 4, 4) * 2 + depth // 2
    odd = lax.rem(y, 2)
    across = y * 4 + x + odd * (3 - 2 * x)
    return across, z * 2 + lax.rem(depth + across, 2)


def device_of(across, along):
    y = across // 4
    place = lax.rem(across, 4)
    odd = lax.rem(y, 2)
    x = place + odd * (3 - 2 * place)
    z = along // 2
    return y * 16 + (z // 2) * 4 + x, lax.rem(z, 2) * 2 + lax.rem(along + across, 2)


def kernel(
    f_hbm, s_hbm, v_hbm, vel_ref, pre_ref,
    RAW, V, VM, X, INV, ISC, JAC, MID, JP, JM, CP, CM, MD, P1, PN, Z, ZS, DIV, W, Q, Q0, OUT, RELAY, HOME, DOT, ARA, ARB, PART,
    in_send, in_recv, in_local, s_send, s_recv, i_send, i_recv, x_send, x_recv, out_send, out_recv, out_local,
    a_send, a_recv, b_send, b_recv,
):
    slab = lax.axis_index("slab")
    depth = lax.axis_index("depth")
    across, along = block_of(slab, depth)
    has = dict(next=across < 15, prev=across > 0, up=along < 15, down=along > 0)
    opposite = dict(next="prev", prev="next", up="down", down="up")
    to_next = device_of(lax.rem(across + 1, 16), along)
    to_prev = device_of(lax.rem(across + 15, 16), along)
    to_up = device_of(across, lax.rem(along + 1, 16))
    to_down = device_of(across, lax.rem(along + 15, 16))

    my_k = lax.rem(slab, 4)
    my_tile = lax.rem(along, 4)
    goes_to = [device_of(slab // 4, depth * 4 + i) for i in range(4)]
    comes_from = [(across * 4 + k, along // 4) for k in range(4)]

    def is_me(device):
        return (device[0] == slab) & (device[1] == depth)

    core = lax.rem(depth, 2)
    side = lax.rem(along, 2)
    x_me = lax.rem(slab, 4)
    y_me = slab // 16
    same_z = slab - x_me - y_me * 16
    same_xy = y_me * 16 + x_me
    a_me = y_me * 4 + x_me
    b_me = along // 2 * 2 + core
    x_at = [lax.rem(x_me + d, 4) for d in range(4)]
    y_at = [lax.rem(y_me + d, 4) for d in range(4)]
    z_at = [lax.rem(along // 2 + d, 8) for d in range(8)]
    z_slab = [same_xy + z // 2 * 4 for z in z_at]
    z_depth = [lax.rem(z, 2) * 2 for z in z_at]
    steps = [(dx, dy) for dx in range(4) for dy in range(4) if dx or dy]
    steps.sort(key=lambda d: -min(d[0], 4 - d[0]) - min(d[1], 4 - d[1]))
    a_peers = [((same_z + y_at[dy] * 16 + x_at[dx], depth), y_at[dy] * 4 + x_at[dx]) for dx, dy in steps]
    steps = [(dz, dc) for dz in range(8) for dc in range(2) if dz or dc]
    steps.sort(key=lambda d: -min(d[0], 8 - d[0]) - 0.5 * d[1])
    cores = (core, 1 - core)
    b_peers = [((z_slab[dz], z_depth[dz] + cores[dc]), z_at[dz] * 2 + cores[dc]) for dz, dc in steps]
    odd = lax.rem(y_me, 2)
    x_line = [(slab - x_me + k, depth - core + side) for k in range(4)]
    x_from = [(slab - x_me + k, depth - core + lax.rem(core + k + odd, 2)) for k in range(4)]
    passes = along // 2 * 2 + core
    z_tile = lax.rem(passes, 4)
    z_home = [(same_xy + 4 * (k + odd * (3 - 2 * k)), passes // 4) for k in range(4)]

    barrier = pltpu.get_barrier_semaphore()

    def greet(device):
        pl.semaphore_signal(barrier, inc=1, device_id=device, device_id_type=MESH_ID)

    zeros = jnp.zeros((4, WIDE, LANES), jnp.float32)
    for name, place in (("prev", 0), ("next", 12)):

        @pl.when(jnp.logical_not(has[name]))
        def _(place=place):
            V[place : place + 4] = zeros
            for j in range(KRYLOV):
                for c in range(4):
                    X[j, c, place : place + 4] = zeros

    zeros = jnp.zeros((WIDE, 4, LANES), jnp.float32)
    for name, place in (("down", 12), ("up", 8)):

        @pl.when(jnp.logical_not(has[name]))
        def _(place=place):
            V[:, place : place + 4] = zeros
            for j in range(KRYLOV):
                for c in range(4):
                    X[j, c, :, place : place + 4] = zeros

    for device in goes_to + comes_from + x_line + x_from + [to_next, to_prev] + [peer for peer, _ in a_peers + b_peers]:
        greet(device)
    pl.semaphore_wait(barrier, 48)

    def remote(src, dst, send, recv, peer):
        return pltpu.make_async_remote_copy(
            src_ref=src, dst_ref=dst, send_sem=send, recv_sem=recv, device_id=peer, device_id_type=MESH_ID
        )

    def rows(i):
        return pl.ds(pl.multiple_of(i * EDGE, EDGE), EDGE)

    def fields(t, i, k):
        place = RAW.at[t, pl.ds(2 * k, 2)]
        if t < 3:
            return f_hbm.at[t, :, rows(i)], place
        return (s_hbm if t == 3 else v_hbm).at[:, rows(i)], place

    def give(t, i):
        src, dst = fields(t, i, my_k)
        return remote(src, dst, in_send.at[t, i], in_recv.at[t, my_k], goes_to[i])

    def take(t, k):
        src, dst = fields(t, 0, k)
        return remote(src, dst, in_send.at[t, 0], in_recv.at[t, k], comes_from[k])

    def keep(t):
        src, dst = fields(t, my_tile, my_k)
        return pltpu.make_async_copy(src, dst, in_local.at[t])

    home = is_me(device_of(slab // 4, depth * 4 + my_tile))
    for t in (4, 0, 1, 2, 3):
        pl.when(home)(lambda t=t: keep(t).start())
        for i in range(4):
            pl.when(jnp.logical_not(is_me(goes_to[i])))(lambda t=t, i=i: give(t, i).start())

    def taken(t):
        pl.when(home)(lambda: keep(t).wait())
        for k in range(4):
            pl.when(jnp.logical_not(is_me(comes_from[k])))(lambda k=k: take(t, k).wait_recv())

    def start(copies, *names):
        for name in names:
            pl.when(has[name.split("_")[-1]])(lambda name=name: copies[name]().start())

    def received(copies, *names):
        for name in names:
            pl.when(has[opposite[name.split("_")[-1]]])(lambda name=name: copies[name]().wait_recv())

    def sent(copies, *names):
        for name in names:
            pl.when(has[name.split("_")[-1]])(lambda name=name: copies[name]().wait_send())

    def setup_copy(k, src, dst, peer):
        return lambda: remote(src, dst, s_send.at[k], s_recv.at[k], peer)

    setup = dict(
        up=setup_copy(0, V.at[4:12, 4:8], V.at[4:12, 12:16], to_up),
        down=setup_copy(1, V.at[4:12, 0:4], V.at[4:12, 8:12], to_down),
        near_next=setup_copy(2, V.at[11], V.at[3], to_next),
        far_next=setup_copy(4, V.at[8:11], V.at[0:3], to_next),
        near_prev=setup_copy(3, V.at[4:8], V.at[12:16], to_prev),
    )

    def step_copies(j, c):
        def copy(k, src, dst, peer):
            return lambda: remote(
                X.at[(j, c) + src], X.at[(j, c) + dst], i_send.at[j, c, k], i_recv.at[j, c, k], peer
            )

        high, from_high = (slice(9, 12), slice(1, 4)) if c == 3 else (slice(8, 12), slice(0, 4))
        low, from_low = (slice(4, 6), slice(12, 14)) if c == 3 else (slice(4, 8), slice(12, 16))
        own, first, last, above, below = slice(4, 12), slice(0, 4), slice(4, 8), slice(8, 12), slice(12, 16)
        main = slice(0, 8)
        return dict(
            up=copy(0, (own, last), (own, below), to_up),
            down=copy(1, (own, first), (own, above), to_down),
            main_next=copy(2, (high, main), (from_high, main), to_next),
            main_prev=copy(3, (low, main), (from_low, main), to_prev),
            below_next=copy(4, (high, below), (from_high, below), to_next),
            below_prev=copy(5, (low, below), (from_low, below), to_prev),
            above_next=copy(4, (high, above), (from_high, above), to_next),
            above_prev=copy(5, (low, above), (from_low, above), to_prev),
            low_up=copy(6, (from_high, last), (from_high, below), to_up),
            high_up=copy(7, (from_low, last), (from_low, below), to_up),
            low_down=copy(6, (from_high, first), (from_high, above), to_down),
            high_down=copy(7, (from_low, first), (from_low, above), to_down),
        )

    FIRST = ("up", "down", "main_next", "main_prev")
    ROWS_0 = ("low_up", "high_up", "below_next", "below_prev")
    ROWS_1 = ("low_down", "high_down", "above_next", "above_prev")

    def on_core(number, action):
        pl.when(side == number)(action)

    def begin(j, c):
        start(step_copies(j, c), *FIRST)

    def pass_outer(j, c):
        copies = step_copies(j, c)
        received(copies, "up", "down")
        on_core(0, lambda: start(copies, "below_next", "below_prev"))
        on_core(1, lambda: start(copies, "above_next", "above_prev"))

    def pass_inner(j, c):
        copies = step_copies(j, c)
        for name, side, place in (("main_next", "prev", 0), ("main_prev", "next", 1)):
            received(copies, name)

            @pl.when(has[side])
            def _(place=place):
                on_core(0, lambda: start(copies, ROWS_0[place]))
                on_core(1, lambda: start(copies, ROWS_1[place]))

    def take_corners(j, c):
        copies = step_copies(j, c)

        def corners(here, theirs):
            pl.when(has["prev"])(lambda: received(copies, theirs[0]))
            pl.when(has["next"])(lambda: received(copies, theirs[1]))
            received(copies, *here[2:])

        on_core(0, lambda: corners(ROWS_0, ROWS_1))
        on_core(1, lambda: corners(ROWS_1, ROWS_0))

    def all_sent(j, c):
        copies = step_copies(j, c)
        sent(copies, *FIRST)

        def corners(mine):
            pl.when(has["prev"])(lambda: sent(copies, mine[0]))
            pl.when(has["next"])(lambda: sent(copies, mine[1]))
            sent(copies, *mine[2:])

        on_core(0, lambda: corners(ROWS_0))
        on_core(1, lambda: corners(ROWS_1))

    place_in = lax.broadcasted_iota(jnp.int32, (LANES, LANES), 0)
    place_out = lax.broadcasted_iota(jnp.int32, (LANES, LANES), 1)
    split = place_in == jnp.where(place_out < 128, 2 * place_out, 2 * place_out - 255)
    split = split.astype(jnp.bfloat16)
    taken(4)
    moved = permute(RAW[4].reshape(64, LANES), split)
    for n in range(8):
        V[n + OFF, 0:EDGE] = moved[8 * n : 8 * n + 8]
    start(setup, "up")
    start(setup, "down")

    row = lax.broadcasted_iota(jnp.int32, (WIDE, LANES), 0)
    row = along * EDGE + jnp.where(row < 12, row, row - WIDE)
    element_row = ((row >= 0) & (row < 128)).astype(jnp.float32)
    node_row = ((row >= 1) & (row < 128)).astype(jnp.float32)

    def plane_flag(n, low):
        place = across * EDGE + n
        return ((place >= low) & (place < 128)).astype(jnp.float32)

    received(setup, "up")
    received(setup, "down")
    start(setup, "near_next", "far_next", "near_prev")

    def inverse_plane(n):
        both = VM[n + OFF - 1] + VM[n + OFF]
        both = both + prev_y(both)
        both = both + prev_z(both)
        free = node_row * plane_flag(n, 1)
        INV[n + OFF] = free * 3.0 / jnp.where(free > 0.0, both, 1.0)

    for n in range(8):
        VM[n + OFF] = V[n + OFF] * (element_row * plane_flag(n, 0))
    for n in range(1, 8):
        inverse_plane(n)
    received(setup, "near_next")
    VM[OFF - 1] = V[OFF - 1] * (element_row * plane_flag(-1, 0))
    inverse_plane(0)
    for t in range(4):
        taken(t)
        moved = permute(RAW[t].reshape(64, LANES), split)
        for n in range(8):
            q = moved[8 * n : 8 * n + 8]
            if t < 3:
                q = q * (node_row * plane_flag(n, 1))[0:EDGE]
            Q0[t, n] = q
            Q[t, n] = q
            X[0, t, n + OFF, 0:EDGE] = q * INV[n + OFF, 0:EDGE] if t < 3 else q
        begin(0, t)
    received(setup, "far_next", "near_prev")
    for n in (-4, -3, -2, 8, 9, 10, 11):
        VM[n + OFF] = V[n + OFF] * (element_row * plane_flag(n, 0))
    for n in (-3, -2, -1, 8, 9, 10):
        inverse_plane(n)
    for e in range(-3, 10):
        both = INV[e + OFF] + INV[e + OFF + 1]
        both = both + next_y(both)
        both = both + next_z(both)
        there = element_row * plane_flag(e, 0)
        ISC[e + OFF] = there / jnp.where(there > 0.0, 0.1875 * both, 1.0)

    def along_x(j, k, slot, peer):
        return remote(ZS.at[j, :, 2 * k : 2 * k + 2], RELAY.at[j, slot], x_send.at[j, k], x_recv.at[j, slot], peer)

    def x_begin(j):
        for k in range(4):
            pl.when(jnp.logical_not(is_me(x_line[k])))(lambda k=k: along_x(j, k, x_me, x_line[k]).start())

        @pl.when(side == core)
        def _():
            RELAY[j, x_me] = ZS[j, :, pl.ds(2 * x_me, 2)]


    @pl.loop(0, KRYLOV)
    def _(j):
        for c in range(3):
            pass_outer(j, c)

        def modes_of(n, c):
            return forward_modes(X[j, c, n + OFF])

        def jacobi(n, c, before, after):
            JAC[c, n + OFF] = 2.0 * X[j, c, n + OFF] - INV[n + OFF] * back_to_nodes(before, after)

        def sweep(first, last, c, before, keep_first, keep_last):
            low = modes_of(first, c)
            for e in range(first, last + 1):
                high = modes_of(e + 1, c)
                weighted = weigh(element_modes(low, high), VM[e + OFF])
                after = from_after(weighted)
                if before is not None:
                    jacobi(e, c, before, after)
                elif keep_first is not None:
                    for m in range(4):
                        MID[c, keep_first, m] = after[m]
                before = from_before(weighted)
                low = high
            if keep_last is not None:
                for m in range(4):
                    MID[c, keep_last, m] = before[m]
            return before

        def halves_of(planes):
            for n in planes:
                JP[n + OFF], JM[n + OFF] = divergence_halves([JAC[c, n + OFF] for c in range(3)])

        def first_pressures(planes):
            for e in planes:
                defect = 0.25 * (JP[e + OFF + 1] + JM[e + OFF]) - X[j, 3, e + OFF]
                MD[e + OFF] = defect
                P1[e + OFF] = defect * ISC[e + OFF]

        def corrections(planes):
            for n in planes:
                slope = gradient(P1[n + OFF - 1], P1[n + OFF])
                scale = 0.25 * INV[n + OFF]
                CP[n + OFF], CM[n + OFF] = divergence_halves([scale * slope[c] for c in range(3)])

        def next_pressures(planes):
            for e in planes:
                change = MD[e + OFF] - 0.25 * (CP[e + OFF + 1] + CM[e + OFF])
                PN[e + OFF] = P1[e + OFF] + change * ISC[e + OFF]

        def z_planes(planes):
            for n in planes:
                slope = gradient(PN[n + OFF - 1], PN[n + OFF])
                scale = 0.25 * INV[n + OFF]
                for c in range(3):
                    z = JAC[c, n + OFF] - scale * slope[c]
                    Z[c, n + OFF] = z
                    if 0 <= n < 8:
                        ZS[j, c, n] = z[0:EDGE]
                if 0 <= n < 8:
                    ZS[j, 3, n] = PN[n + OFF, 0:EDGE]

        for c in range(3):
            sweep(0, 6, c, None, 0, 1)
        pass_outer(j, 3)
        halves_of(range(1, 7))
        for c in range(4):
            pass_inner(j, c)
        first_pressures(range(1, 6))
        corrections(range(2, 6))
        next_pressures(range(2, 5))
        z_planes((3, 4))

        for c in range(3):
            take_corners(j, c)
            before = sweep(-4, -1, c, None, None, None)
            jacobi(0, c, before, [MID[c, 0, m] for m in range(4)])
            sweep(7, 10, c, [MID[c, 1, m] for m in range(4)], None, None)

        halves_of((-3, -2, -1, 0, 7, 8, 9, 10))
        take_corners(j, 3)

        @pl.when(j == 1)
        def _():
            x_begin(0)

        @pl.when(j == 2)
        def _():
            x_begin(1)

        first_pressures((*range(-3, 1), *range(6, 10)))
        corrections((-2, -1, 0, 1, 6, 7, 8, 9))
        next_pressures((-2, -1, 0, 1, 5, 6, 7, 8))
        z_planes((-1, 0, 1, 2, 5, 6, 7, 8))
        @pl.when(j == 2)
        def _():
            x_begin(2)

        for c in range(3):
            low = forward_modes(Z[c, OFF - 1])
            before = None
            for e in range(-1, 8):
                high = forward_modes(Z[c, e + 1 + OFF])
                modes = element_modes(low, high)
                place = (0, 2, 4)[c]
                if e >= 0:
                    own = modes[place][0:EDGE]
                    DIV[e] = own if c == 0 else DIV[e] + own
                weighted = list(weigh(modes, VM[e + OFF]))
                weighted[place] = weighted[place] + 0.25 * PN[e + OFF]
                after = from_after(weighted)
                if before is not None:
                    free = (node_row * plane_flag(e, 1))[0:EDGE]
                    w = back_to_nodes(before, after)[0:EDGE] * free
                    W[j, c, e] = w
                    q = w - Q[c, e]
                    Q[c, e] = q
                    X[j + 1, c, e + OFF, 0:EDGE] = q * INV[e + OFF, 0:EDGE]
                before = from_before(weighted)
                low = high
            pl.when(j < KRYLOV - 1)(lambda c=c: begin(j + 1, c))
        for e in range(8):
            w = 0.25 * DIV[e]
            W[j, 3, e] = w
            q = w - Q[3, e]
            Q[3, e] = q
            X[j + 1, 3, e + OFF, 0:EDGE] = q

        pl.when(j < KRYLOV - 1)(lambda: begin(j + 1, 3))

        def inner(other):
            total = None
            for n in range(8):
                for c in range(4):
                    term = W[j, c, n] * other(c, n)
                    total = term if total is None else total + term
            return fold(total)

        DOT[j * 4 + 3] = inner(lambda c, n: Q0[c, n])

        @pl.loop(0, j + 1)
        def _(k):
            DOT[j * 4 + k] = inner(lambda c, n: W[k, c, n])

    order = [(0, 0), (1, 0), (2, 0), (1, 1), (2, 1), (2, 2), (0, 3), (1, 3), (2, 3)]
    rows16 = lax.broadcasted_iota(jnp.int32, (16, 128), 0)
    stacked = jnp.zeros((16, 128), jnp.float32)
    for place, (a, b) in enumerate(order):
        line = jnp.sum(DOT[a * 4 + b], axis=0, keepdims=True)
        stacked = jnp.where(rows16 == place, line, stacked)
    folded = stacked + pltpu.roll(stacked, 64, 1)
    left = lax.broadcasted_iota(jnp.int32, (8, 128), 1) < 64
    tile = jnp.where(left, folded[0:8], folded[8:16])

    def reduce(tile, stage, buffer, me, peers, send, recv, meanwhile):
        PART[stage] = tile

        def copy(i, slot):
            return remote(PART.at[stage], buffer.at[slot], send.at[i], recv.at[slot], peers[i][0])

        for i in range(15):
            copy(i, me).start()
        buffer[me] = tile
        meanwhile()
        for i in reversed(range(15)):
            copy(i, peers[i][1]).wait_recv()
        total = buffer[0]
        for i in range(1, 16):
            total = total + buffer[i]
        for i in range(15):
            copy(i, me).wait_send()
        return total

    join = place_out == jnp.where(place_in < 128, 2 * place_in, 2 * place_in - 255)
    join = join.astype(jnp.bfloat16)

    def x_taken(j):
        for k in range(4):
            pl.when(jnp.logical_not(is_me(x_from[k])))(lambda k=k: along_x(j, k, k, x_from[k]).wait_recv())
        RELAY[j] = permute(RELAY[j].reshape(256, LANES), join).reshape(4, 4, 2, EDGE, LANES)

    def x_taken_early():
        x_taken(0)
        x_taken(1)

    tile = reduce(tile, 0, ARB, b_me, b_peers, b_send, b_recv, x_taken_early)
    tile = reduce(tile, 1, ARA, a_me, a_peers, a_send, a_recv, lambda: x_taken(2))
    sums_a = jnp.sum(jnp.where(left, tile, 0.0), axis=1, keepdims=True)
    sums_b = jnp.sum(jnp.where(left, 0.0, tile), axis=1, keepdims=True)
    a00, a10, a20, a11, a21, a22, b0, b1 = [sums_a[i : i + 1] for i in range(8)]
    b2 = sums_b[0:1]
    r0 = 1.0 / jnp.sqrt(a00)
    l10 = a10 * r0
    l20 = a20 * r0
    r1 = 1.0 / jnp.sqrt(a11 - l10 * l10)
    l21 = (a21 - l20 * l10) * r1
    r2 = 1.0 / jnp.sqrt(a22 - l20 * l20 - l21 * l21)
    y0 = b0 * r0
    y1 = (b1 - l10 * y0) * r1
    y2 = (b2 - l20 * y0 - l21 * y1) * r2
    c2 = y2 * r2
    c1 = (y1 - l21 * c2) * r1
    c0 = (y0 - l10 * c1 - l20 * c2) * r0
    def back(k):
        return remote(OUT.at[k], HOME.at[:, :, rows(z_tile)], out_send.at[k], out_recv.at[z_tile], z_home[k])

    def arrive(i, holder):
        return remote(OUT.at[0], HOME.at[:, :, EDGE * i : EDGE * i + EDGE], out_send.at[0], out_recv.at[i], holder)

    def b_peer_of(i):
        tile = depth * 4 + i
        return same_xy + tile // 4 * 4, lax.rem(tile // 2, 2) * 2 + lax.rem(tile, 2)

    def stay(k):
        return pltpu.make_async_copy(OUT.at[k], HOME.at[:, :, rows(z_tile)], out_local.at[0])

    for k in range(4):
        OUT[k] = c0 * RELAY[0, k] + c1 * RELAY[1, k] + c2 * RELAY[2, k]
        pl.when(is_me(z_home[k]))(lambda k=k: stay(k).start())
        pl.when(jnp.logical_not(is_me(z_home[k])))(lambda k=k: back(k).start())

    sent(setup, *setup)

    @pl.loop(0, KRYLOV)
    def _(j):
        for c in range(4):
            all_sent(j, c)

    for t in range(5):
        for i in range(4):
            pl.when(jnp.logical_not(is_me(goes_to[i])))(lambda t=t, i=i: give(t, i).wait_send())

    for i in range(4):
        holder = b_peer_of(i)
        pl.when(is_me(holder))(lambda: stay(0).wait())
        pl.when(jnp.logical_not(is_me(holder)))(lambda i=i, holder=holder: arrive(i, holder).wait_recv())
    for c in range(3):
        vel_ref[c] = HOME[c]
    pre_ref[...] = HOME[3]
    for k in range(4):
        for j in range(KRYLOV):
            pl.when(jnp.logical_not(is_me(x_line[k])))(
                lambda j=j, k=k: along_x(j, k, x_me, x_line[k]).wait_send()
            )
        pl.when(jnp.logical_not(is_me(z_home[k])))(lambda k=k: back(k).wait_send())


def body(forcing, source, viscosity):
    f32 = jnp.float32
    vmem = lambda *shape: pltpu.VMEM(shape, f32)
    dma = lambda *shape: pltpu.SemaphoreType.DMA(shape)
    K = KRYLOV
    return pl.pallas_call(
        kernel,
        out_shape=(
            jax.ShapeDtypeStruct((3, 2, 32, LANES), f32),
            jax.ShapeDtypeStruct((2, 32, LANES), f32),
        ),
        in_specs=[pl.BlockSpec(memory_space=pl.ANY)] * 3,
        out_specs=(pl.BlockSpec(memory_space=pltpu.VMEM), pl.BlockSpec(memory_space=pltpu.VMEM)),
        scratch_shapes=[
            vmem(5, EDGE, EDGE, LANES),
            vmem(WIDE, WIDE, LANES),
            vmem(WIDE, WIDE, LANES),
            vmem(K + 1, 4, WIDE, WIDE, LANES),
            vmem(WIDE, WIDE, LANES),
            vmem(WIDE, WIDE, LANES),
            vmem(3, WIDE, WIDE, LANES),
            vmem(3, 2, 4, WIDE, LANES),
            vmem(WIDE, WIDE, LANES),
            vmem(WIDE, WIDE, LANES),
            vmem(WIDE, WIDE, LANES),
            vmem(WIDE, WIDE, LANES),
            vmem(WIDE, WIDE, LANES),
            vmem(WIDE, WIDE, LANES),
            vmem(WIDE, WIDE, LANES),
            vmem(3, WIDE, WIDE, LANES),
            vmem(K, 4, EDGE, EDGE, LANES),
            vmem(EDGE, EDGE, LANES),
            vmem(K, 4, EDGE, EDGE, LANES),
            vmem(4, EDGE, EDGE, LANES),
            vmem(4, EDGE, EDGE, LANES),
            vmem(4, 4, 2, EDGE, LANES),
            vmem(K, 4, 4, 2, EDGE, LANES),
            vmem(4, 2, 32, LANES),
            vmem(4 * K, 8, 128),
            vmem(16, 8, 128),
            vmem(16, 8, 128),
            vmem(2, 8, 128),
            dma(5, 4),
            dma(5, 4),
            dma(5),
            dma(6),
            dma(6),
            dma(K, 4, 8),
            dma(K, 4, 8),
            dma(K, 4),
            dma(K, 4),
            dma(4),
            dma(4),
            dma(1),
            dma(16),
            dma(16),
            dma(16),
            dma(16),
        ],
        compiler_params=pltpu.CompilerParams(
            collective_id=0, has_side_effects=True, vmem_limit_bytes=60 * 1024 * 1024
        ),
        name="stokes_cycle",
    )(forcing, source, viscosity)


def solution(mesh):
    placed = (P(None, "slab", "depth", None), P("slab", "depth", None), P("slab", "depth", None))
    return jax.shard_map(
        body,
        mesh=mesh,
        in_specs=placed,
        out_specs=(P(None, "slab", "depth", None), P("slab", "depth", None)),
        check_vma=False,
    )
```

```python
import jax
import jax.numpy as jnp
from jax import lax
from jax.experimental import pallas as pl
from jax.experimental.pallas import tpu as pltpu
from jax.sharding import PartitionSpec as P

KRYLOV = 3
EDGE = 8
WIDE = 16
OFF = 4
LANES = 256
MESH_ID = pl.DeviceIdType.MESH


def next_z(x):
    return jnp.concatenate([x[:, 128:], pltpu.roll(x[:, :128], 127, 1)], axis=1)


def prev_z(x):
    return jnp.concatenate([pltpu.roll(x[:, 128:], 1, 1), x[:, :128]], axis=1)


def permute(x, matrix):
    parts = []
    for _ in range(3):
        part = x.astype(jnp.bfloat16)
        x = x - part.astype(jnp.float32)
        parts.append(part)
    count = x.shape[0]
    moved = jnp.dot(jnp.concatenate(parts, axis=0), matrix, preferred_element_type=jnp.float32)
    return moved[0:count] + (moved[count : 2 * count] + moved[2 * count :])


def next_y(x):
    return pltpu.roll(x, WIDE - 1, 0)


def prev_y(x):
    return pltpu.roll(x, 1, 0)


def forward_modes(u):
    ahead = next_z(u)
    zs = ahead + u
    zd = ahead - u
    zs_ahead = next_y(zs)
    zd_ahead = next_y(zd)
    return zs_ahead + zs, zs_ahead - zs, zd_ahead + zd, zd_ahead - zd


def element_modes(low, high):
    return (
        high[0] - low[0],
        high[1] - low[1],
        high[1] + low[1],
        high[2] - low[2],
        high[2] + low[2],
        high[3] - low[3],
        high[3] + low[3],
    )


def weigh(modes, visc):
    v16 = visc * (1.0 / 16.0)
    v24 = visc * (1.0 / 24.0)
    v48 = visc * (1.0 / 48.0)
    return (
        modes[0] * v16,
        modes[1] * v24,
        modes[2] * v16,
        modes[3] * v24,
        modes[4] * v16,
        modes[5] * v48,
        modes[6] * v24,
    )


def from_before(modes):
    return modes[0], modes[2] + modes[1], modes[4] + modes[3], modes[6] + modes[5]


def from_after(modes):
    return modes[0], modes[2] - modes[1], modes[4] - modes[3], modes[6] - modes[5]


def back_to_nodes(before, after):
    ss = before[0] - after[0]
    ds = before[1] + after[1]
    sd = before[2] + after[2]
    dd = before[3] + after[3]
    zs = (ss - ds) + prev_y(ss + ds)
    zd = (sd - dd) + prev_y(sd + dd)
    return (zs - zd) + prev_z(zs + zd)


def divergence_halves(u):
    x_ahead = next_z(u[0])
    y_ahead = next_z(u[1])
    z_ahead = next_z(u[2])
    zs_x = x_ahead + u[0]
    zs_y = y_ahead + u[1]
    zd_z = z_ahead - u[2]
    ss_x = next_y(zs_x) + zs_x
    rest = (zd_z - zs_y) + next_y(zd_z + zs_y)
    return rest + ss_x, rest - ss_x


def gradient(before, after):
    diff = before - after
    both = before + after
    diff_y = diff + prev_y(diff)
    both_back = prev_y(both)
    sum_y = both + both_back
    dif_y = both_back - both
    return (
        diff_y + prev_z(diff_y),
        dif_y + prev_z(dif_y),
        prev_z(sum_y) - sum_y,
    )


def fold(product):
    return product[:, :128] + product[:, 128:]


def block_of(slab, depth):
    x = lax.rem(slab, 4)
    y = slab // 16
    z = lax.rem(slab // 4, 4) * 2 + depth // 2
    odd = lax.rem(y, 2)
    across = y * 4 + x + odd * (3 - 2 * x)
    return across, z * 2 + lax.rem(depth + across, 2)


def device_of(across, along):
    y = across // 4
    place = lax.rem(across, 4)
    odd = lax.rem(y, 2)
    x = place + odd * (3 - 2 * place)
    z = along // 2
    return y * 16 + (z // 2) * 4 + x, lax.rem(z, 2) * 2 + lax.rem(along + across, 2)


def kernel(
    f_hbm, s_hbm, v_hbm, vel_ref, pre_ref,
    RAW, V, VM, X, INV, ISC, JAC, MID, JP, JM, CP, CM, MD, P1, PN, Z, ZS, DIV, W, Q, Q0, OUT, RELAY, HOME, DOT, ARA, ARB, PART,
    in_send, in_recv, in_local, s_send, s_recv, i_send, i_recv, x_send, x_recv, out_send, out_recv, out_local,
    a_send, a_recv, b_send, b_recv,
):
    slab = lax.axis_index("slab")
    depth = lax.axis_index("depth")
    across, along = block_of(slab, depth)
    has = dict(next=across < 15, prev=across > 0, up=along < 15, down=along > 0)
    opposite = dict(next="prev", prev="next", up="down", down="up")
    to_next = device_of(lax.rem(across + 1, 16), along)
    to_prev = device_of(lax.rem(across + 15, 16), along)
    to_up = device_of(across, lax.rem(along + 1, 16))
    to_down = device_of(across, lax.rem(along + 15, 16))

    my_k = lax.rem(slab, 4)
    my_tile = lax.rem(along, 4)
    goes_to = [device_of(slab // 4, depth * 4 + i) for i in range(4)]
    comes_from = [(across * 4 + k, along // 4) for k in range(4)]

    def is_me(device):
        return (device[0] == slab) & (device[1] == depth)

    core = lax.rem(depth, 2)
    side = lax.rem(along, 2)
    x_me = lax.rem(slab, 4)
    y_me = slab // 16
    same_z = slab - x_me - y_me * 16
    same_xy = y_me * 16 + x_me
    a_me = y_me * 4 + x_me
    b_me = along // 2 * 2 + core
    x_at = [lax.rem(x_me + d, 4) for d in range(4)]
    y_at = [lax.rem(y_me + d, 4) for d in range(4)]
    z_at = [lax.rem(along // 2 + d, 8) for d in range(8)]
    z_slab = [same_xy + z // 2 * 4 for z in z_at]
    z_depth = [lax.rem(z, 2) * 2 for z in z_at]
    steps = [(dx, dy) for dx in range(4) for dy in range(4) if dx or dy]
    steps.sort(key=lambda d: -min(d[0], 4 - d[0]) - min(d[1], 4 - d[1]))
    a_peers = [((same_z + y_at[dy] * 16 + x_at[dx], depth), y_at[dy] * 4 + x_at[dx]) for dx, dy in steps]
    steps = [(dz, dc) for dz in range(8) for dc in range(2) if dz or dc]
    steps.sort(key=lambda d: -min(d[0], 8 - d[0]) - 0.5 * d[1])
    cores = (core, 1 - core)
    b_peers = [((z_slab[dz], z_depth[dz] + cores[dc]), z_at[dz] * 2 + cores[dc]) for dz, dc in steps]
    odd = lax.rem(y_me, 2)
    x_line = [(slab - x_me + k, depth) for k in range(4)]
    z_home = [(same_xy + 4 * (k + odd * (3 - 2 * k)), along // 4) for k in range(4)]
    z_tile = [lax.rem(along // 2 * 2 + lax.rem(core + k + odd, 2), 4) for k in range(4)]

    barrier = pltpu.get_barrier_semaphore()

    def greet(device):
        pl.semaphore_signal(barrier, inc=1, device_id=device, device_id_type=MESH_ID)

    zeros = jnp.zeros((4, WIDE, LANES), jnp.float32)
    for name, place in (("prev", 0), ("next", 12)):

        @pl.when(jnp.logical_not(has[name]))
        def _(place=place):
            V[place : place + 4] = zeros
            for j in range(KRYLOV):
                for c in range(4):
                    X[j, c, place : place + 4] = zeros

    zeros = jnp.zeros((WIDE, 4, LANES), jnp.float32)
    for name, place in (("down", 12), ("up", 8)):

        @pl.when(jnp.logical_not(has[name]))
        def _(place=place):
            V[:, place : place + 4] = zeros
            for j in range(KRYLOV):
                for c in range(4):
                    X[j, c, :, place : place + 4] = zeros

    for device in goes_to + comes_from + [to_next, to_prev] + [peer for peer, _ in a_peers + b_peers]:
        greet(device)
    pl.semaphore_wait(barrier, 40)

    def remote(src, dst, send, recv, peer):
        return pltpu.make_async_remote_copy(
            src_ref=src, dst_ref=dst, send_sem=send, recv_sem=recv, device_id=peer, device_id_type=MESH_ID
        )

    def rows(i):
        return pl.ds(pl.multiple_of(i * EDGE, EDGE), EDGE)

    def fields(t, i, k):
        place = RAW.at[t, pl.ds(2 * k, 2)]
        if t < 3:
            return f_hbm.at[t, :, rows(i)], place
        return (s_hbm if t == 3 else v_hbm).at[:, rows(i)], place

    def give(t, i):
        src, dst = fields(t, i, my_k)
        return remote(src, dst, in_send.at[t, i], in_recv.at[t, my_k], goes_to[i])

    def take(t, k):
        src, dst = fields(t, 0, k)
        return remote(src, dst, in_send.at[t, 0], in_recv.at[t, k], comes_from[k])

    def keep(t):
        src, dst = fields(t, my_tile, my_k)
        return pltpu.make_async_copy(src, dst, in_local.at[t])

    home = is_me(device_of(slab // 4, depth * 4 + my_tile))
    for t in (4, 0, 1, 2, 3):
        pl.when(home)(lambda t=t: keep(t).start())
        for i in range(4):
            pl.when(jnp.logical_not(is_me(goes_to[i])))(lambda t=t, i=i: give(t, i).start())

    def taken(t):
        pl.when(home)(lambda: keep(t).wait())
        for k in range(4):
            pl.when(jnp.logical_not(is_me(comes_from[k])))(lambda k=k: take(t, k).wait_recv())

    def start(copies, *names):
        for name in names:
            pl.when(has[name.split("_")[-1]])(lambda name=name: copies[name]().start())

    def received(copies, *names):
        for name in names:
            pl.when(has[opposite[name.split("_")[-1]]])(lambda name=name: copies[name]().wait_recv())

    def sent(copies, *names):
        for name in names:
            pl.when(has[name.split("_")[-1]])(lambda name=name: copies[name]().wait_send())

    def setup_copy(k, src, dst, peer):
        return lambda: remote(src, dst, s_send.at[k], s_recv.at[k], peer)

    setup = dict(
        up=setup_copy(0, V.at[4:12, 4:8], V.at[4:12, 12:16], to_up),
        down=setup_copy(1, V.at[4:12, 0:4], V.at[4:12, 8:12], to_down),
        near_next=setup_copy(2, V.at[11], V.at[3], to_next),
        far_next=setup_copy(4, V.at[8:11], V.at[0:3], to_next),
        near_prev=setup_copy(3, V.at[4:8], V.at[12:16], to_prev),
    )

    def step_copies(j, c):
        def copy(k, src, dst, peer):
            return lambda: remote(
                X.at[(j, c) + src], X.at[(j, c) + dst], i_send.at[j, c, k], i_recv.at[j, c, k], peer
            )

        high, from_high = (slice(9, 12), slice(1, 4)) if c == 3 else (slice(8, 12), slice(0, 4))
        low, from_low = (slice(4, 6), slice(12, 14)) if c == 3 else (slice(4, 8), slice(12, 16))
        own, first, last, above, below = slice(4, 12), slice(0, 4), slice(4, 8), slice(8, 12), slice(12, 16)
        main = slice(0, 8)
        return dict(
            up=copy(0, (own, last), (own, below), to_up),
            down=copy(1, (own, first), (own, above), to_down),
            main_next=copy(2, (high, main), (from_high, main), to_next),
            main_prev=copy(3, (low, main), (from_low, main), to_prev),
            below_next=copy(4, (high, below), (from_high, below), to_next),
            below_prev=copy(5, (low, below), (from_low, below), to_prev),
            above_next=copy(4, (high, above), (from_high, above), to_next),
            above_prev=copy(5, (low, above), (from_low, above), to_prev),
            low_up=copy(6, (from_high, last), (from_high, below), to_up),
            high_up=copy(7, (from_low, last), (from_low, below), to_up),
            low_down=copy(6, (from_high, first), (from_high, above), to_down),
            high_down=copy(7, (from_low, first), (from_low, above), to_down),
        )

    FIRST = ("up", "down", "main_next", "main_prev")
    ROWS_0 = ("low_up", "high_up", "below_next", "below_prev")
    ROWS_1 = ("low_down", "high_down", "above_next", "above_prev")

    def on_core(number, action):
        pl.when(side == number)(action)

    def begin(j, c):
        start(step_copies(j, c), *FIRST)

    def pass_outer(j, c):
        copies = step_copies(j, c)
        received(copies, "up", "down")
        on_core(0, lambda: start(copies, "below_next", "below_prev"))
        on_core(1, lambda: start(copies, "above_next", "above_prev"))

    def pass_inner(j, c):
        copies = step_copies(j, c)
        for name, side, place in (("main_next", "prev", 0), ("main_prev", "next", 1)):
            received(copies, name)

            @pl.when(has[side])
            def _(place=place):
                on_core(0, lambda: start(copies, ROWS_0[place]))
                on_core(1, lambda: start(copies, ROWS_1[place]))

    def take_corners(j, c):
        copies = step_copies(j, c)

        def corners(here, theirs):
            pl.when(has["prev"])(lambda: received(copies, theirs[0]))
            pl.when(has["next"])(lambda: received(copies, theirs[1]))
            received(copies, *here[2:])

        on_core(0, lambda: corners(ROWS_0, ROWS_1))
        on_core(1, lambda: corners(ROWS_1, ROWS_0))

    def all_sent(j, c):
        copies = step_copies(j, c)
        sent(copies, *FIRST)

        def corners(mine):
            pl.when(has["prev"])(lambda: sent(copies, mine[0]))
            pl.when(has["next"])(lambda: sent(copies, mine[1]))
            sent(copies, *mine[2:])

        on_core(0, lambda: corners(ROWS_0))
        on_core(1, lambda: corners(ROWS_1))

    place_in = lax.broadcasted_iota(jnp.int32, (LANES, LANES), 0)
    place_out = lax.broadcasted_iota(jnp.int32, (LANES, LANES), 1)
    split = place_in == jnp.where(place_out < 128, 2 * place_out, 2 * place_out - 255)
    split = split.astype(jnp.bfloat16)
    taken(4)
    moved = permute(RAW[4].reshape(64, LANES), split)
    for n in range(8):
        V[n + OFF, 0:EDGE] = moved[8 * n : 8 * n + 8]
    start(setup, "up")
    start(setup, "down")

    row = lax.broadcasted_iota(jnp.int32, (WIDE, LANES), 0)
    row = along * EDGE + jnp.where(row < 12, row, row - WIDE)
    element_row = ((row >= 0) & (row < 128)).astype(jnp.float32)
    node_row = ((row >= 1) & (row < 128)).astype(jnp.float32)

    def plane_flag(n, low):
        place = across * EDGE + n
        return ((place >= low) & (place < 128)).astype(jnp.float32)

    received(setup, "up")
    received(setup, "down")
    start(setup, "near_next", "far_next", "near_prev")

    def inverse_plane(n):
        both = VM[n + OFF - 1] + VM[n + OFF]
        both = both + prev_y(both)
        both = both + prev_z(both)
        free = node_row * plane_flag(n, 1)
        INV[n + OFF] = free * 3.0 / jnp.where(free > 0.0, both, 1.0)

    for n in range(8):
        VM[n + OFF] = V[n + OFF] * (element_row * plane_flag(n, 0))
    for n in range(1, 8):
        inverse_plane(n)
    received(setup, "near_next")
    VM[OFF - 1] = V[OFF - 1] * (element_row * plane_flag(-1, 0))
    inverse_plane(0)
    for t in range(4):
        taken(t)
        moved = permute(RAW[t].reshape(64, LANES), split)
        for n in range(8):
            q = moved[8 * n : 8 * n + 8]
            if t < 3:
                q = q * (node_row * plane_flag(n, 1))[0:EDGE]
            Q0[t, n] = q
            Q[t, n] = q
            X[0, t, n + OFF, 0:EDGE] = q * INV[n + OFF, 0:EDGE] if t < 3 else q
        begin(0, t)
    received(setup, "far_next", "near_prev")
    for n in (-4, -3, -2, 8, 9, 10, 11):
        VM[n + OFF] = V[n + OFF] * (element_row * plane_flag(n, 0))
    for n in (-3, -2, -1, 8, 9, 10):
        inverse_plane(n)
    for e in range(-3, 10):
        both = INV[e + OFF] + INV[e + OFF + 1]
        both = both + next_y(both)
        both = both + next_z(both)
        there = element_row * plane_flag(e, 0)
        ISC[e + OFF] = there / jnp.where(there > 0.0, 0.1875 * both, 1.0)

    def along_x(j, k, slot):
        return remote(ZS.at[j, :, 2 * k : 2 * k + 2], RELAY.at[j, slot], x_send.at[j, k], x_recv.at[j, slot], x_line[k])

    def x_begin(j):
        for k in range(4):
            pl.when(x_me != k)(lambda k=k: along_x(j, k, x_me).start())
        RELAY[j, x_me] = ZS[j, :, pl.ds(2 * x_me, 2)]

    @pl.loop(0, KRYLOV)
    def _(j):
        for c in range(3):
            pass_outer(j, c)

        def modes_of(n, c):
            return forward_modes(X[j, c, n + OFF])

        def jacobi(n, c, before, after):
            JAC[c, n + OFF] = 2.0 * X[j, c, n + OFF] - INV[n + OFF] * back_to_nodes(before, after)

        def sweep(first, last, c, before, keep_first, keep_last):
            low = modes_of(first, c)
            for e in range(first, last + 1):
                high = modes_of(e + 1, c)
                weighted = weigh(element_modes(low, high), VM[e + OFF])
                after = from_after(weighted)
                if before is not None:
                    jacobi(e, c, before, after)
                elif keep_first is not None:
                    for m in range(4):
                        MID[c, keep_first, m] = after[m]
                before = from_before(weighted)
                low = high
            if keep_last is not None:
                for m in range(4):
                    MID[c, keep_last, m] = before[m]
            return before

        def halves_of(planes):
            for n in planes:
                JP[n + OFF], JM[n + OFF] = divergence_halves([JAC[c, n + OFF] for c in range(3)])

        def first_pressures(planes):
            for e in planes:
                defect = 0.25 * (JP[e + OFF + 1] + JM[e + OFF]) - X[j, 3, e + OFF]
                MD[e + OFF] = defect
                P1[e + OFF] = defect * ISC[e + OFF]

        def corrections(planes):
            for n in planes:
                slope = gradient(P1[n + OFF - 1], P1[n + OFF])
                scale = 0.25 * INV[n + OFF]
                CP[n + OFF], CM[n + OFF] = divergence_halves([scale * slope[c] for c in range(3)])

        def next_pressures(planes):
            for e in planes:
                change = MD[e + OFF] - 0.25 * (CP[e + OFF + 1] + CM[e + OFF])
                PN[e + OFF] = P1[e + OFF] + change * ISC[e + OFF]

        def z_planes(planes):
            for n in planes:
                slope = gradient(PN[n + OFF - 1], PN[n + OFF])
                scale = 0.25 * INV[n + OFF]
                for c in range(3):
                    z = JAC[c, n + OFF] - scale * slope[c]
                    Z[c, n + OFF] = z
                    if 0 <= n < 8:
                        ZS[j, c, n] = z[0:EDGE]
                if 0 <= n < 8:
                    ZS[j, 3, n] = PN[n + OFF, 0:EDGE]

        for c in range(3):
            sweep(0, 6, c, None, 0, 1)
        pass_outer(j, 3)
        halves_of(range(1, 7))
        for c in range(4):
            pass_inner(j, c)
        first_pressures(range(1, 6))
        corrections(range(2, 6))
        next_pressures(range(2, 5))
        z_planes((3, 4))

        for c in range(3):
            take_corners(j, c)
            before = sweep(-4, -1, c, None, None, None)
            jacobi(0, c, before, [MID[c, 0, m] for m in range(4)])
            sweep(7, 10, c, [MID[c, 1, m] for m in range(4)], None, None)

        halves_of((-3, -2, -1, 0, 7, 8, 9, 10))
        take_corners(j, 3)

        @pl.when(j == 1)
        def _():
            x_begin(0)

        @pl.when(j == 2)
        def _():
            x_begin(1)

        first_pressures((*range(-3, 1), *range(6, 10)))
        corrections((-2, -1, 0, 1, 6, 7, 8, 9))
        next_pressures((-2, -1, 0, 1, 5, 6, 7, 8))
        z_planes((-1, 0, 1, 2, 5, 6, 7, 8))
        @pl.when(j == 2)
        def _():
            x_begin(2)

        for c in range(3):
            low = forward_modes(Z[c, OFF - 1])
            before = None
            for e in range(-1, 8):
                high = forward_modes(Z[c, e + 1 + OFF])
                modes = element_modes(low, high)
                place = (0, 2, 4)[c]
                if e >= 0:
                    own = modes[place][0:EDGE]
                    DIV[e] = own if c == 0 else DIV[e] + own
                weighted = list(weigh(modes, VM[e + OFF]))
                weighted[place] = weighted[place] + 0.25 * PN[e + OFF]
                after = from_after(weighted)
                if before is not None:
                    free = (node_row * plane_flag(e, 1))[0:EDGE]
                    w = back_to_nodes(before, after)[0:EDGE] * free
                    W[j, c, e] = w
                    q = w - Q[c, e]
                    Q[c, e] = q
                    X[j + 1, c, e + OFF, 0:EDGE] = q * INV[e + OFF, 0:EDGE]
                before = from_before(weighted)
                low = high
            pl.when(j < KRYLOV - 1)(lambda c=c: begin(j + 1, c))
        for e in range(8):
            w = 0.25 * DIV[e]
            W[j, 3, e] = w
            q = w - Q[3, e]
            Q[3, e] = q
            X[j + 1, 3, e + OFF, 0:EDGE] = q

        pl.when(j < KRYLOV - 1)(lambda: begin(j + 1, 3))

        def inner(other):
            total = None
            for n in range(8):
                for c in range(4):
                    term = W[j, c, n] * other(c, n)
                    total = term if total is None else total + term
            return fold(total)

        DOT[j * 4 + 3] = inner(lambda c, n: Q0[c, n])

        @pl.loop(0, j + 1)
        def _(k):
            DOT[j * 4 + k] = inner(lambda c, n: W[k, c, n])

    order = [(0, 0), (1, 0), (2, 0), (1, 1), (2, 1), (2, 2), (0, 3), (1, 3), (2, 3)]
    rows16 = lax.broadcasted_iota(jnp.int32, (16, 128), 0)
    stacked = jnp.zeros((16, 128), jnp.float32)
    for place, (a, b) in enumerate(order):
        line = jnp.sum(DOT[a * 4 + b], axis=0, keepdims=True)
        stacked = jnp.where(rows16 == place, line, stacked)
    folded = stacked + pltpu.roll(stacked, 64, 1)
    left = lax.broadcasted_iota(jnp.int32, (8, 128), 1) < 64
    tile = jnp.where(left, folded[0:8], folded[8:16])

    def reduce(tile, stage, buffer, me, peers, send, recv, meanwhile):
        PART[stage] = tile

        def copy(i, slot):
            return remote(PART.at[stage], buffer.at[slot], send.at[i], recv.at[slot], peers[i][0])

        for i in range(15):
            copy(i, me).start()
        buffer[me] = tile
        meanwhile()
        for i in reversed(range(15)):
            copy(i, peers[i][1]).wait_recv()
        total = buffer[0]
        for i in range(1, 16):
            total = total + buffer[i]
        for i in range(15):
            copy(i, me).wait_send()
        return total

    join = place_out == jnp.where(place_in < 128, 2 * place_in, 2 * place_in - 255)
    join = join.astype(jnp.bfloat16)

    def x_taken(j):
        for k in range(4):
            pl.when(x_me != k)(lambda k=k: along_x(j, k, k).wait_recv())
        RELAY[j] = permute(RELAY[j].reshape(256, LANES), join).reshape(4, 4, 2, EDGE, LANES)

    def x_taken_early():
        x_taken(0)
        x_taken(1)

    tile = reduce(tile, 0, ARB, b_me, b_peers, b_send, b_recv, x_taken_early)
    tile = reduce(tile, 1, ARA, a_me, a_peers, a_send, a_recv, lambda: x_taken(2))
    sums_a = jnp.sum(jnp.where(left, tile, 0.0), axis=1, keepdims=True)
    sums_b = jnp.sum(jnp.where(left, 0.0, tile), axis=1, keepdims=True)
    a00, a10, a20, a11, a21, a22, b0, b1 = [sums_a[i : i + 1] for i in range(8)]
    b2 = sums_b[0:1]
    r0 = 1.0 / jnp.sqrt(a00)
    l10 = a10 * r0
    l20 = a20 * r0
    r1 = 1.0 / jnp.sqrt(a11 - l10 * l10)
    l21 = (a21 - l20 * l10) * r1
    r2 = 1.0 / jnp.sqrt(a22 - l20 * l20 - l21 * l21)
    y0 = b0 * r0
    y1 = (b1 - l10 * y0) * r1
    y2 = (b2 - l20 * y0 - l21 * y1) * r2
    c2 = y2 * r2
    c1 = (y1 - l21 * c2) * r1
    c0 = (y0 - l10 * c1 - l20 * c2) * r0
    def back(k):
        return remote(OUT.at[k], HOME.at[:, :, rows(z_tile[k])], out_send.at[k], out_recv.at[z_tile[k]], z_home[k])

    def arrive(i, holder):
        return remote(OUT.at[0], HOME.at[:, :, EDGE * i : EDGE * i + EDGE], out_send.at[0], out_recv.at[i], holder)

    def b_peer_of(i):
        tile = depth * 4 + i
        return same_xy + tile // 4 * 4, lax.rem(tile // 2, 2) * 2 + lax.rem(slab // 4 + i, 2)

    def stay(k):
        return pltpu.make_async_copy(OUT.at[k], HOME.at[:, :, rows(z_tile[k])], out_local.at[0])

    for k in range(4):
        OUT[k] = c0 * RELAY[0, k] + c1 * RELAY[1, k] + c2 * RELAY[2, k]
        pl.when(is_me(z_home[k]))(lambda k=k: stay(k).start())
        pl.when(jnp.logical_not(is_me(z_home[k])))(lambda k=k: back(k).start())

    sent(setup, *setup)

    @pl.loop(0, KRYLOV)
    def _(j):
        for c in range(4):
            all_sent(j, c)

    for t in range(5):
        for i in range(4):
            pl.when(jnp.logical_not(is_me(goes_to[i])))(lambda t=t, i=i: give(t, i).wait_send())

    for i in range(4):
        holder = b_peer_of(i)
        pl.when(is_me(holder))(lambda: stay(0).wait())
        pl.when(jnp.logical_not(is_me(holder)))(lambda i=i, holder=holder: arrive(i, holder).wait_recv())
    for c in range(3):
        vel_ref[c] = HOME[c]
    pre_ref[...] = HOME[3]
    for k in range(4):
        for j in range(KRYLOV):
            pl.when(x_me != k)(lambda j=j, k=k: along_x(j, k, x_me).wait_send())
        pl.when(jnp.logical_not(is_me(z_home[k])))(lambda k=k: back(k).wait_send())


def body(forcing, source, viscosity):
    f32 = jnp.float32
    vmem = lambda *shape: pltpu.VMEM(shape, f32)
    dma = lambda *shape: pltpu.SemaphoreType.DMA(shape)
    K = KRYLOV
    return pl.pallas_call(
        kernel,
        out_shape=(
            jax.ShapeDtypeStruct((3, 2, 32, LANES), f32),
            jax.ShapeDtypeStruct((2, 32, LANES), f32),
        ),
        in_specs=[pl.BlockSpec(memory_space=pl.ANY)] * 3,
        out_specs=(pl.BlockSpec(memory_space=pltpu.VMEM), pl.BlockSpec(memory_space=pltpu.VMEM)),
        scratch_shapes=[
            vmem(5, EDGE, EDGE, LANES),
            vmem(WIDE, WIDE, LANES),
            vmem(WIDE, WIDE, LANES),
            vmem(K + 1, 4, WIDE, WIDE, LANES),
            vmem(WIDE, WIDE, LANES),
            vmem(WIDE, WIDE, LANES),
            vmem(3, WIDE, WIDE, LANES),
            vmem(3, 2, 4, WIDE, LANES),
            vmem(WIDE, WIDE, LANES),
            vmem(WIDE, WIDE, LANES),
            vmem(WIDE, WIDE, LANES),
            vmem(WIDE, WIDE, LANES),
            vmem(WIDE, WIDE, LANES),
            vmem(WIDE, WIDE, LANES),
            vmem(WIDE, WIDE, LANES),
            vmem(3, WIDE, WIDE, LANES),
            vmem(K, 4, EDGE, EDGE, LANES),
            vmem(EDGE, EDGE, LANES),
            vmem(K, 4, EDGE, EDGE, LANES),
            vmem(4, EDGE, EDGE, LANES),
            vmem(4, EDGE, EDGE, LANES),
            vmem(4, 4, 2, EDGE, LANES),
            vmem(K, 4, 4, 2, EDGE, LANES),
            vmem(4, 2, 32, LANES),
            vmem(4 * K, 8, 128),
            vmem(16, 8, 128),
            vmem(16, 8, 128),
            vmem(2, 8, 128),
            dma(5, 4),
            dma(5, 4),
            dma(5),
            dma(6),
            dma(6),
            dma(K, 4, 8),
            dma(K, 4, 8),
            dma(K, 4),
            dma(K, 4),
            dma(4),
            dma(4),
            dma(1),
            dma(16),
            dma(16),
            dma(16),
            dma(16),
        ],
        compiler_params=pltpu.CompilerParams(
            collective_id=0, has_side_effects=True, vmem_limit_bytes=60 * 1024 * 1024
        ),
        name="stokes_cycle",
    )(forcing, source, viscosity)


def solution(mesh):
    placed = (P(None, "slab", "depth", None), P("slab", "depth", None), P("slab", "depth", None))
    return jax.shard_map(
        body,
        mesh=mesh,
        in_specs=placed,
        out_specs=(P(None, "slab", "depth", None), P("slab", "depth", None)),
        check_vma=False,
    )
```

```python
import jax
import jax.numpy as jnp
from jax import lax
from jax.experimental import pallas as pl
from jax.experimental.pallas import tpu as pltpu
from jax.sharding import PartitionSpec as P

KRYLOV = 3
EDGE = 8
WIDE = 16
OFF = 4
LANES = 256
MESH_ID = pl.DeviceIdType.MESH


def next_z(x):
    return jnp.concatenate([x[:, 128:], pltpu.roll(x[:, :128], 127, 1)], axis=1)


def prev_z(x):
    return jnp.concatenate([pltpu.roll(x[:, 128:], 1, 1), x[:, :128]], axis=1)


def permute(x, matrix):
    parts = []
    for _ in range(3):
        part = x.astype(jnp.bfloat16)
        x = x - part.astype(jnp.float32)
        parts.append(part)
    count = x.shape[0]
    moved = jnp.dot(jnp.concatenate(parts, axis=0), matrix, preferred_element_type=jnp.float32)
    return moved[0:count] + (moved[count : 2 * count] + moved[2 * count :])


def next_y(x):
    return pltpu.roll(x, WIDE - 1, 0)


def prev_y(x):
    return pltpu.roll(x, 1, 0)


def forward_modes(u):
    ahead = next_z(u)
    zs = ahead + u
    zd = ahead - u
    zs_ahead = next_y(zs)
    zd_ahead = next_y(zd)
    return zs_ahead + zs, zs_ahead - zs, zd_ahead + zd, zd_ahead - zd


def element_modes(low, high):
    return (
        high[0] - low[0],
        high[1] - low[1],
        high[1] + low[1],
        high[2] - low[2],
        high[2] + low[2],
        high[3] - low[3],
        high[3] + low[3],
    )


def weigh(modes, visc):
    v16 = visc * (1.0 / 16.0)
    v24 = visc * (1.0 / 24.0)
    v48 = visc * (1.0 / 48.0)
    return (
        modes[0] * v16,
        modes[1] * v24,
        modes[2] * v16,
        modes[3] * v24,
        modes[4] * v16,
        modes[5] * v48,
        modes[6] * v24,
    )


def from_before(modes):
    return modes[0], modes[2] + modes[1], modes[4] + modes[3], modes[6] + modes[5]


def from_after(modes):
    return modes[0], modes[2] - modes[1], modes[4] - modes[3], modes[6] - modes[5]


def back_to_nodes(before, after):
    ss = before[0] - after[0]
    ds = before[1] + after[1]
    sd = before[2] + after[2]
    dd = before[3] + after[3]
    zs = (ss - ds) + prev_y(ss + ds)
    zd = (sd - dd) + prev_y(sd + dd)
    return (zs - zd) + prev_z(zs + zd)


def divergence_halves(u):
    x_ahead = next_z(u[0])
    y_ahead = next_z(u[1])
    z_ahead = next_z(u[2])
    zs_x = x_ahead + u[0]
    zs_y = y_ahead + u[1]
    zd_z = z_ahead - u[2]
    ss_x = next_y(zs_x) + zs_x
    rest = (zd_z - zs_y) + next_y(zd_z + zs_y)
    return rest + ss_x, rest - ss_x


def gradient(before, after):
    diff = before - after
    both = before + after
    diff_y = diff + prev_y(diff)
    both_back = prev_y(both)
    sum_y = both + both_back
    dif_y = both_back - both
    return (
        diff_y + prev_z(diff_y),
        dif_y + prev_z(dif_y),
        prev_z(sum_y) - sum_y,
    )


def fold(product):
    return product[:, :128] + product[:, 128:]


def block_of(slab, depth):
    x = lax.rem(slab, 4)
    y = slab // 16
    z = lax.rem(slab // 4, 4) * 2 + depth // 2
    odd = lax.rem(y, 2)
    return y * 4 + x + odd * (3 - 2 * x), z * 2 + lax.rem(depth, 2)


def device_of(across, along):
    y = across // 4
    place = lax.rem(across, 4)
    odd = lax.rem(y, 2)
    x = place + odd * (3 - 2 * place)
    z = along // 2
    return y * 16 + (z // 2) * 4 + x, lax.rem(z, 2) * 2 + lax.rem(along, 2)


def kernel(
    f_hbm, s_hbm, v_hbm, vel_ref, pre_ref,
    RAW, V, VM, X, INV, ISC, JAC, MID, JP, JM, CP, CM, MD, P1, PN, Z, ZS, DIV, W, Q, Q0, OUT, RELAY, HOME, DOT, ARA, ARB, PART,
    in_send, in_recv, in_local, s_send, s_recv, i_send, i_recv, x_send, x_recv, out_send, out_recv, out_local,
    a_send, a_recv, b_send, b_recv,
):
    slab = lax.axis_index("slab")
    depth = lax.axis_index("depth")
    across, along = block_of(slab, depth)
    has = dict(next=across < 15, prev=across > 0, up=along < 15, down=along > 0)
    opposite = dict(next="prev", prev="next", up="down", down="up")
    to_next = device_of(lax.rem(across + 1, 16), along)
    to_prev = device_of(lax.rem(across + 15, 16), along)
    to_up = device_of(across, lax.rem(along + 1, 16))
    to_down = device_of(across, lax.rem(along + 15, 16))

    my_k = lax.rem(slab, 4)
    my_tile = lax.rem(along, 4)
    goes_to = [device_of(slab // 4, depth * 4 + i) for i in range(4)]
    comes_from = [(across * 4 + k, along // 4) for k in range(4)]

    def is_me(device):
        return (device[0] == slab) & (device[1] == depth)

    core = lax.rem(depth, 2)
    x_me = lax.rem(slab, 4)
    y_me = slab // 16
    same_z = slab - x_me - y_me * 16
    same_xy = y_me * 16 + x_me
    a_me = y_me * 4 + x_me
    b_me = along
    x_at = [lax.rem(x_me + d, 4) for d in range(4)]
    y_at = [lax.rem(y_me + d, 4) for d in range(4)]
    z_at = [lax.rem(along // 2 + d, 8) for d in range(8)]
    z_slab = [same_xy + z // 2 * 4 for z in z_at]
    z_depth = [lax.rem(z, 2) * 2 for z in z_at]
    steps = [(dx, dy) for dx in range(4) for dy in range(4) if dx or dy]
    steps.sort(key=lambda d: -min(d[0], 4 - d[0]) - min(d[1], 4 - d[1]))
    a_peers = [((same_z + y_at[dy] * 16 + x_at[dx], depth), y_at[dy] * 4 + x_at[dx]) for dx, dy in steps]
    steps = [(dz, dc) for dz in range(8) for dc in range(2) if dz or dc]
    steps.sort(key=lambda d: -min(d[0], 8 - d[0]) - 0.5 * d[1])
    cores = (core, 1 - core)
    b_peers = [((z_slab[dz], z_depth[dz] + cores[dc]), z_at[dz] * 2 + cores[dc]) for dz, dc in steps]
    x_line = [(slab - x_me + k, depth) for k in range(4)]
    odd = lax.rem(y_me, 2)
    z_home = [(same_xy + 4 * (k + odd * (3 - 2 * k)), along // 4) for k in range(4)]

    barrier = pltpu.get_barrier_semaphore()

    def greet(device):
        pl.semaphore_signal(barrier, inc=1, device_id=device, device_id_type=MESH_ID)

    zeros = jnp.zeros((4, WIDE, LANES), jnp.float32)
    for name, place in (("prev", 0), ("next", 12)):

        @pl.when(jnp.logical_not(has[name]))
        def _(place=place):
            V[place : place + 4] = zeros
            for j in range(KRYLOV):
                for c in range(4):
                    X[j, c, place : place + 4] = zeros

    zeros = jnp.zeros((WIDE, 4, LANES), jnp.float32)
    for name, place in (("down", 12), ("up", 8)):

        @pl.when(jnp.logical_not(has[name]))
        def _(place=place):
            V[:, place : place + 4] = zeros
            for j in range(KRYLOV):
                for c in range(4):
                    X[j, c, :, place : place + 4] = zeros

    for device in goes_to + comes_from + [peer for peer, _ in a_peers + b_peers]:
        greet(device)
    pl.semaphore_wait(barrier, 38)

    def remote(src, dst, send, recv, peer):
        return pltpu.make_async_remote_copy(
            src_ref=src, dst_ref=dst, send_sem=send, recv_sem=recv, device_id=peer, device_id_type=MESH_ID
        )

    def rows(i):
        return pl.ds(pl.multiple_of(i * EDGE, EDGE), EDGE)

    def fields(t, i, k):
        place = RAW.at[t, pl.ds(2 * k, 2)]
        if t < 3:
            return f_hbm.at[t, :, rows(i)], place
        return (s_hbm if t == 3 else v_hbm).at[:, rows(i)], place

    def give(t, i):
        src, dst = fields(t, i, my_k)
        return remote(src, dst, in_send.at[t, i], in_recv.at[t, my_k], goes_to[i])

    def take(t, k):
        src, dst = fields(t, 0, k)
        return remote(src, dst, in_send.at[t, 0], in_recv.at[t, k], comes_from[k])

    def keep(t):
        src, dst = fields(t, my_tile, my_k)
        return pltpu.make_async_copy(src, dst, in_local.at[t])

    home = is_me(device_of(slab // 4, depth * 4 + my_tile))
    for t in (4, 0, 1, 2, 3):
        pl.when(home)(lambda t=t: keep(t).start())
        for i in range(4):
            pl.when(jnp.logical_not(is_me(goes_to[i])))(lambda t=t, i=i: give(t, i).start())

    def taken(t):
        pl.when(home)(lambda: keep(t).wait())
        for k in range(4):
            pl.when(jnp.logical_not(is_me(comes_from[k])))(lambda k=k: take(t, k).wait_recv())

    def start(copies, *names):
        for name in names:
            pl.when(has[name.split("_")[-1]])(lambda name=name: copies[name]().start())

    def received(copies, *names):
        for name in names:
            pl.when(has[opposite[name.split("_")[-1]]])(lambda name=name: copies[name]().wait_recv())

    def sent(copies, *names):
        for name in names:
            pl.when(has[name.split("_")[-1]])(lambda name=name: copies[name]().wait_send())

    def setup_copy(k, src, dst, peer):
        return lambda: remote(src, dst, s_send.at[k], s_recv.at[k], peer)

    setup = dict(
        up=setup_copy(0, V.at[4:12, 4:8], V.at[4:12, 12:16], to_up),
        down=setup_copy(1, V.at[4:12, 0:4], V.at[4:12, 8:12], to_down),
        near_next=setup_copy(2, V.at[11], V.at[3], to_next),
        far_next=setup_copy(4, V.at[8:11], V.at[0:3], to_next),
        near_prev=setup_copy(3, V.at[4:8], V.at[12:16], to_prev),
    )

    def step_copies(j, c):
        def copy(k, src, dst, peer):
            return lambda: remote(
                X.at[(j, c) + src], X.at[(j, c) + dst], i_send.at[j, c, k], i_recv.at[j, c, k], peer
            )

        high, from_high = (slice(9, 12), slice(1, 4)) if c == 3 else (slice(8, 12), slice(0, 4))
        low, from_low = (slice(4, 6), slice(12, 14)) if c == 3 else (slice(4, 8), slice(12, 16))
        own, first, last, above, below = slice(4, 12), slice(0, 4), slice(4, 8), slice(8, 12), slice(12, 16)
        main = slice(0, 8)
        return dict(
            up=copy(0, (own, last), (own, below), to_up),
            down=copy(1, (own, first), (own, above), to_down),
            main_next=copy(2, (high, main), (from_high, main), to_next),
            main_prev=copy(3, (low, main), (from_low, main), to_prev),
            below_next=copy(4, (high, below), (from_high, below), to_next),
            below_prev=copy(5, (low, below), (from_low, below), to_prev),
            above_next=copy(4, (high, above), (from_high, above), to_next),
            above_prev=copy(5, (low, above), (from_low, above), to_prev),
            low_up=copy(6, (from_high, last), (from_high, below), to_up),
            high_up=copy(7, (from_low, last), (from_low, below), to_up),
            low_down=copy(6, (from_high, first), (from_high, above), to_down),
            high_down=copy(7, (from_low, first), (from_low, above), to_down),
        )

    FIRST = ("up", "down", "main_next", "main_prev")
    ROWS_0 = ("low_up", "high_up", "below_next", "below_prev")
    ROWS_1 = ("low_down", "high_down", "above_next", "above_prev")

    def on_core(number, action):
        pl.when(core == number)(action)

    def begin(j, c):
        start(step_copies(j, c), *FIRST)

    def pass_outer(j, c):
        copies = step_copies(j, c)
        received(copies, "up", "down")
        on_core(0, lambda: start(copies, "below_next", "below_prev"))
        on_core(1, lambda: start(copies, "above_next", "above_prev"))

    def pass_inner(j, c):
        copies = step_copies(j, c)
        for name, side, place in (("main_next", "prev", 0), ("main_prev", "next", 1)):
            received(copies, name)

            @pl.when(has[side])
            def _(place=place):
                on_core(0, lambda: start(copies, ROWS_0[place]))
                on_core(1, lambda: start(copies, ROWS_1[place]))

    def take_corners(j, c):
        copies = step_copies(j, c)

        def corners(here, theirs):
            pl.when(has["prev"])(lambda: received(copies, theirs[0]))
            pl.when(has["next"])(lambda: received(copies, theirs[1]))
            received(copies, *here[2:])

        on_core(0, lambda: corners(ROWS_0, ROWS_1))
        on_core(1, lambda: corners(ROWS_1, ROWS_0))

    def all_sent(j, c):
        copies = step_copies(j, c)
        sent(copies, *FIRST)

        def corners(mine):
            pl.when(has["prev"])(lambda: sent(copies, mine[0]))
            pl.when(has["next"])(lambda: sent(copies, mine[1]))
            sent(copies, *mine[2:])

        on_core(0, lambda: corners(ROWS_0))
        on_core(1, lambda: corners(ROWS_1))

    place_in = lax.broadcasted_iota(jnp.int32, (LANES, LANES), 0)
    place_out = lax.broadcasted_iota(jnp.int32, (LANES, LANES), 1)
    split = place_in == jnp.where(place_out < 128, 2 * place_out, 2 * place_out - 255)
    split = split.astype(jnp.bfloat16)
    taken(4)
    moved = permute(RAW[4].reshape(64, LANES), split)
    for n in range(8):
        V[n + OFF, 0:EDGE] = moved[8 * n : 8 * n + 8]
    start(setup, "up")
    start(setup, "down")

    row = lax.broadcasted_iota(jnp.int32, (WIDE, LANES), 0)
    row = along * EDGE + jnp.where(row < 12, row, row - WIDE)
    element_row = ((row >= 0) & (row < 128)).astype(jnp.float32)
    node_row = ((row >= 1) & (row < 128)).astype(jnp.float32)

    def plane_flag(n, low):
        place = across * EDGE + n
        return ((place >= low) & (place < 128)).astype(jnp.float32)

    received(setup, "up")
    received(setup, "down")
    start(setup, "near_next", "far_next", "near_prev")

    def inverse_plane(n):
        both = VM[n + OFF - 1] + VM[n + OFF]
        both = both + prev_y(both)
        both = both + prev_z(both)
        free = node_row * plane_flag(n, 1)
        INV[n + OFF] = free * 3.0 / jnp.where(free > 0.0, both, 1.0)

    for n in range(8):
        VM[n + OFF] = V[n + OFF] * (element_row * plane_flag(n, 0))
    for n in range(1, 8):
        inverse_plane(n)
    received(setup, "near_next")
    VM[OFF - 1] = V[OFF - 1] * (element_row * plane_flag(-1, 0))
    inverse_plane(0)
    for t in range(4):
        taken(t)
        moved = permute(RAW[t].reshape(64, LANES), split)
        for n in range(8):
            q = moved[8 * n : 8 * n + 8]
            if t < 3:
                q = q * (node_row * plane_flag(n, 1))[0:EDGE]
            Q0[t, n] = q
            Q[t, n] = q
            X[0, t, n + OFF, 0:EDGE] = q * INV[n + OFF, 0:EDGE] if t < 3 else q
        begin(0, t)
    received(setup, "far_next", "near_prev")
    for n in (-4, -3, -2, 8, 9, 10, 11):
        VM[n + OFF] = V[n + OFF] * (element_row * plane_flag(n, 0))
    for n in (-3, -2, -1, 8, 9, 10):
        inverse_plane(n)
    for e in range(-3, 10):
        both = INV[e + OFF] + INV[e + OFF + 1]
        both = both + next_y(both)
        both = both + next_z(both)
        there = element_row * plane_flag(e, 0)
        ISC[e + OFF] = there / jnp.where(there > 0.0, 0.1875 * both, 1.0)

    def along_x(j, k, slot):
        return remote(ZS.at[j, :, 2 * k : 2 * k + 2], RELAY.at[j, slot], x_send.at[j, k], x_recv.at[j, slot], x_line[k])

    def x_begin(j):
        for k in range(4):
            pl.when(x_me != k)(lambda k=k: along_x(j, k, x_me).start())
        RELAY[j, x_me] = ZS[j, :, pl.ds(2 * x_me, 2)]

    @pl.loop(0, KRYLOV)
    def _(j):
        for c in range(3):
            pass_outer(j, c)

        def modes_of(n, c):
            return forward_modes(X[j, c, n + OFF])

        def jacobi(n, c, before, after):
            JAC[c, n + OFF] = 2.0 * X[j, c, n + OFF] - INV[n + OFF] * back_to_nodes(before, after)

        def sweep(first, last, c, before, keep_first, keep_last):
            low = modes_of(first, c)
            for e in range(first, last + 1):
                high = modes_of(e + 1, c)
                weighted = weigh(element_modes(low, high), VM[e + OFF])
                after = from_after(weighted)
                if before is not None:
                    jacobi(e, c, before, after)
                elif keep_first is not None:
                    for m in range(4):
                        MID[c, keep_first, m] = after[m]
                before = from_before(weighted)
                low = high
            if keep_last is not None:
                for m in range(4):
                    MID[c, keep_last, m] = before[m]
            return before

        def halves_of(planes):
            for n in planes:
                JP[n + OFF], JM[n + OFF] = divergence_halves([JAC[c, n + OFF] for c in range(3)])

        def first_pressures(planes):
            for e in planes:
                defect = 0.25 * (JP[e + OFF + 1] + JM[e + OFF]) - X[j, 3, e + OFF]
                MD[e + OFF] = defect
                P1[e + OFF] = defect * ISC[e + OFF]

        def corrections(planes):
            for n in planes:
                slope = gradient(P1[n + OFF - 1], P1[n + OFF])
                scale = 0.25 * INV[n + OFF]
                CP[n + OFF], CM[n + OFF] = divergence_halves([scale * slope[c] for c in range(3)])

        def next_pressures(planes):
            for e in planes:
                change = MD[e + OFF] - 0.25 * (CP[e + OFF + 1] + CM[e + OFF])
                PN[e + OFF] = P1[e + OFF] + change * ISC[e + OFF]

        def z_planes(planes):
            for n in planes:
                slope = gradient(PN[n + OFF - 1], PN[n + OFF])
                scale = 0.25 * INV[n + OFF]
                for c in range(3):
                    z = JAC[c, n + OFF] - scale * slope[c]
                    Z[c, n + OFF] = z
                    if 0 <= n < 8:
                        ZS[j, c, n] = z[0:EDGE]
                if 0 <= n < 8:
                    ZS[j, 3, n] = PN[n + OFF, 0:EDGE]

        for c in range(3):
            sweep(0, 6, c, None, 0, 1)
        pass_outer(j, 3)
        halves_of(range(1, 7))
        for c in range(4):
            pass_inner(j, c)
        first_pressures(range(1, 6))
        corrections(range(2, 6))
        next_pressures(range(2, 5))
        z_planes((3, 4))

        for c in range(3):
            take_corners(j, c)
            before = sweep(-4, -1, c, None, None, None)
            jacobi(0, c, before, [MID[c, 0, m] for m in range(4)])
            sweep(7, 10, c, [MID[c, 1, m] for m in range(4)], None, None)

        halves_of((-3, -2, -1, 0, 7, 8, 9, 10))
        take_corners(j, 3)

        @pl.when(j == 1)
        def _():
            x_begin(0)

        @pl.when(j == 2)
        def _():
            x_begin(1)

        first_pressures((*range(-3, 1), *range(6, 10)))
        corrections((-2, -1, 0, 1, 6, 7, 8, 9))
        next_pressures((-2, -1, 0, 1, 5, 6, 7, 8))
        z_planes((-1, 0, 1, 2, 5, 6, 7, 8))
        @pl.when(j == 2)
        def _():
            x_begin(2)

        for c in range(3):
            low = forward_modes(Z[c, OFF - 1])
            before = None
            for e in range(-1, 8):
                high = forward_modes(Z[c, e + 1 + OFF])
                modes = element_modes(low, high)
                place = (0, 2, 4)[c]
                if e >= 0:
                    own = modes[place][0:EDGE]
                    DIV[e] = own if c == 0 else DIV[e] + own
                weighted = list(weigh(modes, VM[e + OFF]))
                weighted[place] = weighted[place] + 0.25 * PN[e + OFF]
                after = from_after(weighted)
                if before is not None:
                    free = (node_row * plane_flag(e, 1))[0:EDGE]
                    w = back_to_nodes(before, after)[0:EDGE] * free
                    W[j, c, e] = w
                    q = w - Q[c, e]
                    Q[c, e] = q
                    X[j + 1, c, e + OFF, 0:EDGE] = q * INV[e + OFF, 0:EDGE]
                before = from_before(weighted)
                low = high
            pl.when(j < KRYLOV - 1)(lambda c=c: begin(j + 1, c))
        for e in range(8):
            w = 0.25 * DIV[e]
            W[j, 3, e] = w
            q = w - Q[3, e]
            Q[3, e] = q
            X[j + 1, 3, e + OFF, 0:EDGE] = q

        pl.when(j < KRYLOV - 1)(lambda: begin(j + 1, 3))

        def inner(other):
            total = None
            for n in range(8):
                for c in range(4):
                    term = W[j, c, n] * other(c, n)
                    total = term if total is None else total + term
            return fold(total)

        DOT[j * 4 + 3] = inner(lambda c, n: Q0[c, n])

        @pl.loop(0, j + 1)
        def _(k):
            DOT[j * 4 + k] = inner(lambda c, n: W[k, c, n])

    order = [(0, 0), (1, 0), (2, 0), (1, 1), (2, 1), (2, 2), (0, 3), (1, 3), (2, 3)]
    rows16 = lax.broadcasted_iota(jnp.int32, (16, 128), 0)
    stacked = jnp.zeros((16, 128), jnp.float32)
    for place, (a, b) in enumerate(order):
        line = jnp.sum(DOT[a * 4 + b], axis=0, keepdims=True)
        stacked = jnp.where(rows16 == place, line, stacked)
    folded = stacked + pltpu.roll(stacked, 64, 1)
    left = lax.broadcasted_iota(jnp.int32, (8, 128), 1) < 64
    tile = jnp.where(left, folded[0:8], folded[8:16])

    def reduce(tile, stage, buffer, me, peers, send, recv, meanwhile):
        PART[stage] = tile

        def copy(i, slot):
            return remote(PART.at[stage], buffer.at[slot], send.at[i], recv.at[slot], peers[i][0])

        for i in range(15):
            copy(i, me).start()
        buffer[me] = tile
        meanwhile()
        for i in reversed(range(15)):
            copy(i, peers[i][1]).wait_recv()
        total = buffer[0]
        for i in range(1, 16):
            total = total + buffer[i]
        for i in range(15):
            copy(i, me).wait_send()
        return total

    join = place_out == jnp.where(place_in < 128, 2 * place_in, 2 * place_in - 255)
    join = join.astype(jnp.bfloat16)

    def x_taken(j):
        for k in range(4):
            pl.when(x_me != k)(lambda k=k: along_x(j, k, k).wait_recv())
        RELAY[j] = permute(RELAY[j].reshape(256, LANES), join).reshape(4, 4, 2, EDGE, LANES)

    def x_taken_early():
        x_taken(0)
        x_taken(1)

    tile = reduce(tile, 0, ARB, b_me, b_peers, b_send, b_recv, x_taken_early)
    tile = reduce(tile, 1, ARA, a_me, a_peers, a_send, a_recv, lambda: x_taken(2))
    sums_a = jnp.sum(jnp.where(left, tile, 0.0), axis=1, keepdims=True)
    sums_b = jnp.sum(jnp.where(left, 0.0, tile), axis=1, keepdims=True)
    a00, a10, a20, a11, a21, a22, b0, b1 = [sums_a[i : i + 1] for i in range(8)]
    b2 = sums_b[0:1]
    r0 = 1.0 / jnp.sqrt(a00)
    l10 = a10 * r0
    l20 = a20 * r0
    r1 = 1.0 / jnp.sqrt(a11 - l10 * l10)
    l21 = (a21 - l20 * l10) * r1
    r2 = 1.0 / jnp.sqrt(a22 - l20 * l20 - l21 * l21)
    y0 = b0 * r0
    y1 = (b1 - l10 * y0) * r1
    y2 = (b2 - l20 * y0 - l21 * y1) * r2
    c2 = y2 * r2
    c1 = (y1 - l21 * c2) * r1
    c0 = (y0 - l10 * c1 - l20 * c2) * r0
    def back(k):
        return remote(OUT.at[k], HOME.at[:, :, rows(my_tile)], out_send.at[k], out_recv.at[my_tile], z_home[k])

    def arrive(i, holder):
        return remote(OUT.at[0], HOME.at[:, :, EDGE * i : EDGE * i + EDGE], out_send.at[0], out_recv.at[i], holder)

    def b_peer_of(i):
        tile = depth * 4 + i
        return same_xy + tile // 4 * 4, lax.rem(tile // 2, 2) * 2 + lax.rem(tile, 2)

    def stay(k):
        return pltpu.make_async_copy(OUT.at[k], HOME.at[:, :, rows(my_tile)], out_local.at[0])

    for k in range(4):
        OUT[k] = c0 * RELAY[0, k] + c1 * RELAY[1, k] + c2 * RELAY[2, k]
        pl.when(is_me(z_home[k]))(lambda k=k: stay(k).start())
        pl.when(jnp.logical_not(is_me(z_home[k])))(lambda k=k: back(k).start())

    sent(setup, *setup)

    @pl.loop(0, KRYLOV)
    def _(j):
        for c in range(4):
            all_sent(j, c)

    for t in range(5):
        for i in range(4):
            pl.when(jnp.logical_not(is_me(goes_to[i])))(lambda t=t, i=i: give(t, i).wait_send())

    for i in range(4):
        holder = b_peer_of(i)
        pl.when(is_me(holder))(lambda: stay(0).wait())
        pl.when(jnp.logical_not(is_me(holder)))(lambda i=i, holder=holder: arrive(i, holder).wait_recv())
    for c in range(3):
        vel_ref[c] = HOME[c]
    pre_ref[...] = HOME[3]
    for k in range(4):
        for j in range(KRYLOV):
            pl.when(x_me != k)(lambda j=j, k=k: along_x(j, k, x_me).wait_send())
        pl.when(jnp.logical_not(is_me(z_home[k])))(lambda k=k: back(k).wait_send())


def body(forcing, source, viscosity):
    f32 = jnp.float32
    vmem = lambda *shape: pltpu.VMEM(shape, f32)
    dma = lambda *shape: pltpu.SemaphoreType.DMA(shape)
    K = KRYLOV
    return pl.pallas_call(
        kernel,
        out_shape=(
            jax.ShapeDtypeStruct((3, 2, 32, LANES), f32),
            jax.ShapeDtypeStruct((2, 32, LANES), f32),
        ),
        in_specs=[pl.BlockSpec(memory_space=pl.ANY)] * 3,
        out_specs=(pl.BlockSpec(memory_space=pltpu.VMEM), pl.BlockSpec(memory_space=pltpu.VMEM)),
        scratch_shapes=[
            vmem(5, EDGE, EDGE, LANES),
            vmem(WIDE, WIDE, LANES),
            vmem(WIDE, WIDE, LANES),
            vmem(K + 1, 4, WIDE, WIDE, LANES),
            vmem(WIDE, WIDE, LANES),
            vmem(WIDE, WIDE, LANES),
            vmem(3, WIDE, WIDE, LANES),
            vmem(3, 2, 4, WIDE, LANES),
            vmem(WIDE, WIDE, LANES),
            vmem(WIDE, WIDE, LANES),
            vmem(WIDE, WIDE, LANES),
            vmem(WIDE, WIDE, LANES),
            vmem(WIDE, WIDE, LANES),
            vmem(WIDE, WIDE, LANES),
            vmem(WIDE, WIDE, LANES),
            vmem(3, WIDE, WIDE, LANES),
            vmem(K, 4, EDGE, EDGE, LANES),
            vmem(EDGE, EDGE, LANES),
            vmem(K, 4, EDGE, EDGE, LANES),
            vmem(4, EDGE, EDGE, LANES),
            vmem(4, EDGE, EDGE, LANES),
            vmem(4, 4, 2, EDGE, LANES),
            vmem(K, 4, 4, 2, EDGE, LANES),
            vmem(4, 2, 32, LANES),
            vmem(4 * K, 8, 128),
            vmem(16, 8, 128),
            vmem(16, 8, 128),
            vmem(2, 8, 128),
            dma(5, 4),
            dma(5, 4),
            dma(5),
            dma(6),
            dma(6),
            dma(K, 4, 8),
            dma(K, 4, 8),
            dma(K, 4),
            dma(K, 4),
            dma(4),
            dma(4),
            dma(1),
            dma(16),
            dma(16),
            dma(16),
            dma(16),
        ],
        compiler_params=pltpu.CompilerParams(
            collective_id=0, has_side_effects=True, vmem_limit_bytes=54784 * 1024
        ),
        name="stokes_cycle",
    )(forcing, source, viscosity)


def solution(mesh):
    placed = (P(None, "slab", "depth", None), P("slab", "depth", None), P("slab", "depth", None))
    return jax.shard_map(
        body,
        mesh=mesh,
        in_specs=placed,
        out_specs=(P(None, "slab", "depth", None), P("slab", "depth", None)),
        check_vma=False,
    )
```

```python
import jax
import jax.numpy as jnp
from jax import lax
from jax.experimental import pallas as pl
from jax.experimental.pallas import tpu as pltpu
from jax.sharding import PartitionSpec as P

KRYLOV = 3
EDGE = 8
WIDE = 16
OFF = 4
LANES = 256
MESH_ID = pl.DeviceIdType.MESH


def next_z(x):
    return jnp.concatenate([x[:, 128:], pltpu.roll(x[:, :128], 127, 1)], axis=1)


def prev_z(x):
    return jnp.concatenate([pltpu.roll(x[:, 128:], 1, 1), x[:, :128]], axis=1)


def permute(x, matrix):
    parts = []
    for _ in range(3):
        part = x.astype(jnp.bfloat16)
        x = x - part.astype(jnp.float32)
        parts.append(part)
    count = x.shape[0]
    moved = jnp.dot(jnp.concatenate(parts, axis=0), matrix, preferred_element_type=jnp.float32)
    return moved[0:count] + (moved[count : 2 * count] + moved[2 * count :])


def next_y(x):
    return pltpu.roll(x, WIDE - 1, 0)


def prev_y(x):
    return pltpu.roll(x, 1, 0)


def forward_modes(u):
    ahead = next_z(u)
    zs = ahead + u
    zd = ahead - u
    zs_ahead = next_y(zs)
    zd_ahead = next_y(zd)
    return zs_ahead + zs, zs_ahead - zs, zd_ahead + zd, zd_ahead - zd


def element_modes(low, high):
    return (
        high[0] - low[0],
        high[1] - low[1],
        high[1] + low[1],
        high[2] - low[2],
        high[2] + low[2],
        high[3] - low[3],
        high[3] + low[3],
    )


def weigh(modes, visc):
    v16 = visc * (1.0 / 16.0)
    v24 = visc * (1.0 / 24.0)
    v48 = visc * (1.0 / 48.0)
    return (
        modes[0] * v16,
        modes[1] * v24,
        modes[2] * v16,
        modes[3] * v24,
        modes[4] * v16,
        modes[5] * v48,
        modes[6] * v24,
    )


def from_before(modes):
    return modes[0], modes[2] + modes[1], modes[4] + modes[3], modes[6] + modes[5]


def from_after(modes):
    return modes[0], modes[2] - modes[1], modes[4] - modes[3], modes[6] - modes[5]


def back_to_nodes(before, after):
    ss = before[0] - after[0]
    ds = before[1] + after[1]
    sd = before[2] + after[2]
    dd = before[3] + after[3]
    zs = (ss - ds) + prev_y(ss + ds)
    zd = (sd - dd) + prev_y(sd + dd)
    return (zs - zd) + prev_z(zs + zd)


def divergence_halves(u):
    x_ahead = next_z(u[0])
    y_ahead = next_z(u[1])
    z_ahead = next_z(u[2])
    zs_x = x_ahead + u[0]
    zs_y = y_ahead + u[1]
    zd_z = z_ahead - u[2]
    ss_x = next_y(zs_x) + zs_x
    rest = (zd_z - zs_y) + next_y(zd_z + zs_y)
    return rest + ss_x, rest - ss_x


def gradient(before, after):
    diff = before - after
    both = before + after
    diff_y = diff + prev_y(diff)
    both_back = prev_y(both)
    sum_y = both + both_back
    dif_y = both_back - both
    return (
        diff_y + prev_z(diff_y),
        dif_y + prev_z(dif_y),
        prev_z(sum_y) - sum_y,
    )


def fold(product):
    return product[:, :128] + product[:, 128:]


def block_of(slab, depth):
    x = lax.rem(slab, 4)
    y = slab // 16
    z = lax.rem(slab // 4, 4) * 2 + depth // 2
    odd = lax.rem(y, 2)
    return y * 4 + x + odd * (3 - 2 * x), z * 2 + lax.rem(depth, 2)


def device_of(across, along):
    y = across // 4
    place = lax.rem(across, 4)
    odd = lax.rem(y, 2)
    x = place + odd * (3 - 2 * place)
    z = along // 2
    return y * 16 + (z // 2) * 4 + x, lax.rem(z, 2) * 2 + lax.rem(along, 2)


def kernel(
    f_hbm, s_hbm, v_hbm, vel_ref, pre_ref,
    RAW, V, VM, X, INV, ISC, JAC, MID, JP, JM, CP, CM, MD, P1, PN, Z, ZS, DIV, W, Q, Q0, OUT, RELAY, HOME, DOT, ARA, ARB, PART,
    in_send, in_recv, in_local, s_send, s_recv, i_send, i_recv, x_send, x_recv, out_send, out_recv, out_local,
    a_send, a_recv, b_send, b_recv,
):
    slab = lax.axis_index("slab")
    depth = lax.axis_index("depth")
    across, along = block_of(slab, depth)
    has = dict(next=across < 15, prev=across > 0, up=along < 15, down=along > 0)
    opposite = dict(next="prev", prev="next", up="down", down="up")
    to_next = device_of(lax.rem(across + 1, 16), along)
    to_prev = device_of(lax.rem(across + 15, 16), along)
    to_up = device_of(across, lax.rem(along + 1, 16))
    to_down = device_of(across, lax.rem(along + 15, 16))

    my_k = lax.rem(slab, 4)
    my_tile = lax.rem(along, 4)
    goes_to = [device_of(slab // 4, depth * 4 + i) for i in range(4)]
    comes_from = [(across * 4 + k, along // 4) for k in range(4)]

    def is_me(device):
        return (device[0] == slab) & (device[1] == depth)

    core = lax.rem(depth, 2)
    x_me = lax.rem(slab, 4)
    y_me = slab // 16
    same_z = slab - x_me - y_me * 16
    same_xy = y_me * 16 + x_me
    a_me = y_me * 4 + x_me
    b_me = along
    x_at = [lax.rem(x_me + d, 4) for d in range(4)]
    y_at = [lax.rem(y_me + d, 4) for d in range(4)]
    z_at = [lax.rem(along // 2 + d, 8) for d in range(8)]
    z_slab = [same_xy + z // 2 * 4 for z in z_at]
    z_depth = [lax.rem(z, 2) * 2 for z in z_at]
    steps = [(dx, dy) for dx in range(4) for dy in range(4) if dx or dy]
    steps.sort(key=lambda d: -min(d[0], 4 - d[0]) - min(d[1], 4 - d[1]))
    a_peers = [((same_z + y_at[dy] * 16 + x_at[dx], depth), y_at[dy] * 4 + x_at[dx]) for dx, dy in steps]
    steps = [(dz, dc) for dz in range(8) for dc in range(2) if dz or dc]
    steps.sort(key=lambda d: -min(d[0], 8 - d[0]) - 0.5 * d[1])
    cores = (core, 1 - core)
    b_peers = [((z_slab[dz], z_depth[dz] + cores[dc]), z_at[dz] * 2 + cores[dc]) for dz, dc in steps]
    x_line = [(slab - x_me + k, depth) for k in range(4)]
    odd = lax.rem(y_me, 2)
    z_home = [(same_xy + 4 * (k + odd * (3 - 2 * k)), along // 4) for k in range(4)]

    barrier = pltpu.get_barrier_semaphore()

    def greet(device):
        pl.semaphore_signal(barrier, inc=1, device_id=device, device_id_type=MESH_ID)

    zeros = jnp.zeros((4, WIDE, LANES), jnp.float32)
    for name, place in (("prev", 0), ("next", 12)):

        @pl.when(jnp.logical_not(has[name]))
        def _(place=place):
            V[place : place + 4] = zeros
            for j in range(KRYLOV):
                for c in range(4):
                    X[j, c, place : place + 4] = zeros

    zeros = jnp.zeros((WIDE, 4, LANES), jnp.float32)
    for name, place in (("down", 12), ("up", 8)):

        @pl.when(jnp.logical_not(has[name]))
        def _(place=place):
            V[:, place : place + 4] = zeros
            for j in range(KRYLOV):
                for c in range(4):
                    X[j, c, :, place : place + 4] = zeros

    for device in goes_to + comes_from + [peer for peer, _ in a_peers + b_peers]:
        greet(device)
    pl.semaphore_wait(barrier, 38)

    def remote(src, dst, send, recv, peer):
        return pltpu.make_async_remote_copy(
            src_ref=src, dst_ref=dst, send_sem=send, recv_sem=recv, device_id=peer, device_id_type=MESH_ID
        )

    def rows(i):
        return pl.ds(pl.multiple_of(i * EDGE, EDGE), EDGE)

    def fields(t, i, k):
        place = RAW.at[t, pl.ds(2 * k, 2)]
        if t < 3:
            return f_hbm.at[t, :, rows(i)], place
        return (s_hbm if t == 3 else v_hbm).at[:, rows(i)], place

    def give(t, i):
        src, dst = fields(t, i, my_k)
        return remote(src, dst, in_send.at[t, i], in_recv.at[t, my_k], goes_to[i])

    def take(t, k):
        src, dst = fields(t, 0, k)
        return remote(src, dst, in_send.at[t, 0], in_recv.at[t, k], comes_from[k])

    def keep(t):
        src, dst = fields(t, my_tile, my_k)
        return pltpu.make_async_copy(src, dst, in_local.at[t])

    home = is_me(device_of(slab // 4, depth * 4 + my_tile))
    for t in (4, 0, 1, 2, 3):
        pl.when(home)(lambda t=t: keep(t).start())
        for i in range(4):
            pl.when(jnp.logical_not(is_me(goes_to[i])))(lambda t=t, i=i: give(t, i).start())

    def taken(t):
        pl.when(home)(lambda: keep(t).wait())
        for k in range(4):
            pl.when(jnp.logical_not(is_me(comes_from[k])))(lambda k=k: take(t, k).wait_recv())

    def start(copies, *names):
        for name in names:
            pl.when(has[name.split("_")[-1]])(lambda name=name: copies[name]().start())

    def received(copies, *names):
        for name in names:
            pl.when(has[opposite[name.split("_")[-1]]])(lambda name=name: copies[name]().wait_recv())

    def sent(copies, *names):
        for name in names:
            pl.when(has[name.split("_")[-1]])(lambda name=name: copies[name]().wait_send())

    def setup_copy(k, src, dst, peer):
        return lambda: remote(src, dst, s_send.at[k], s_recv.at[k], peer)

    setup = dict(
        up=setup_copy(0, V.at[4:12, 4:8], V.at[4:12, 12:16], to_up),
        down=setup_copy(1, V.at[4:12, 0:4], V.at[4:12, 8:12], to_down),
        near_next=setup_copy(2, V.at[11], V.at[3], to_next),
        far_next=setup_copy(4, V.at[8:11], V.at[0:3], to_next),
        near_prev=setup_copy(3, V.at[4:8], V.at[12:16], to_prev),
    )

    def step_copies(j, c):
        def copy(k, src, dst, peer):
            return lambda: remote(
                X.at[(j, c) + src], X.at[(j, c) + dst], i_send.at[j, c, k], i_recv.at[j, c, k], peer
            )

        high, from_high = (slice(9, 12), slice(1, 4)) if c == 3 else (slice(8, 12), slice(0, 4))
        low, from_low = (slice(4, 6), slice(12, 14)) if c == 3 else (slice(4, 8), slice(12, 16))
        own, first, last, above, below = slice(4, 12), slice(0, 4), slice(4, 8), slice(8, 12), slice(12, 16)
        main = slice(0, 8)
        return dict(
            up=copy(0, (own, last), (own, below), to_up),
            down=copy(1, (own, first), (own, above), to_down),
            main_next=copy(2, (high, main), (from_high, main), to_next),
            main_prev=copy(3, (low, main), (from_low, main), to_prev),
            below_next=copy(4, (high, below), (from_high, below), to_next),
            below_prev=copy(5, (low, below), (from_low, below), to_prev),
            above_next=copy(4, (high, above), (from_high, above), to_next),
            above_prev=copy(5, (low, above), (from_low, above), to_prev),
            low_up=copy(6, (from_high, last), (from_high, below), to_up),
            high_up=copy(7, (from_low, last), (from_low, below), to_up),
            low_down=copy(6, (from_high, first), (from_high, above), to_down),
            high_down=copy(7, (from_low, first), (from_low, above), to_down),
        )

    FIRST = ("up", "down", "main_next", "main_prev")
    ROWS_0 = ("low_up", "high_up", "below_next", "below_prev")
    ROWS_1 = ("low_down", "high_down", "above_next", "above_prev")

    def on_core(number, action):
        pl.when(core == number)(action)

    def begin(j, c):
        start(step_copies(j, c), *FIRST)

    def pass_outer(j, c):
        copies = step_copies(j, c)
        received(copies, "up", "down")
        on_core(0, lambda: start(copies, "below_next", "below_prev"))
        on_core(1, lambda: start(copies, "above_next", "above_prev"))

    def pass_inner(j, c):
        copies = step_copies(j, c)
        for name, side, place in (("main_next", "prev", 0), ("main_prev", "next", 1)):
            received(copies, name)

            @pl.when(has[side])
            def _(place=place):
                on_core(0, lambda: start(copies, ROWS_0[place]))
                on_core(1, lambda: start(copies, ROWS_1[place]))

    def take_corners(j, c):
        copies = step_copies(j, c)

        def corners(here, theirs):
            pl.when(has["prev"])(lambda: received(copies, theirs[0]))
            pl.when(has["next"])(lambda: received(copies, theirs[1]))
            received(copies, *here[2:])

        on_core(0, lambda: corners(ROWS_0, ROWS_1))
        on_core(1, lambda: corners(ROWS_1, ROWS_0))

    def all_sent(j, c):
        copies = step_copies(j, c)
        sent(copies, *FIRST)

        def corners(mine):
            pl.when(has["prev"])(lambda: sent(copies, mine[0]))
            pl.when(has["next"])(lambda: sent(copies, mine[1]))
            sent(copies, *mine[2:])

        on_core(0, lambda: corners(ROWS_0))
        on_core(1, lambda: corners(ROWS_1))

    place_in = lax.broadcasted_iota(jnp.int32, (LANES, LANES), 0)
    place_out = lax.broadcasted_iota(jnp.int32, (LANES, LANES), 1)
    split = place_in == jnp.where(place_out < 128, 2 * place_out, 2 * place_out - 255)
    split = split.astype(jnp.bfloat16)
    taken(4)
    moved = permute(RAW[4].reshape(64, LANES), split)
    for n in range(8):
        V[n + OFF, 0:EDGE] = moved[8 * n : 8 * n + 8]
    start(setup, "up")
    start(setup, "down")

    row = lax.broadcasted_iota(jnp.int32, (WIDE, LANES), 0)
    row = along * EDGE + jnp.where(row < 12, row, row - WIDE)
    element_row = ((row >= 0) & (row < 128)).astype(jnp.float32)
    node_row = ((row >= 1) & (row < 128)).astype(jnp.float32)

    def plane_flag(n, low):
        place = across * EDGE + n
        return ((place >= low) & (place < 128)).astype(jnp.float32)

    received(setup, "up")
    received(setup, "down")
    start(setup, "near_next", "far_next", "near_prev")

    def inverse_plane(n):
        both = VM[n + OFF - 1] + VM[n + OFF]
        both = both + prev_y(both)
        both = both + prev_z(both)
        free = node_row * plane_flag(n, 1)
        INV[n + OFF] = free * 3.0 / jnp.where(free > 0.0, both, 1.0)

    for n in range(8):
        VM[n + OFF] = V[n + OFF] * (element_row * plane_flag(n, 0))
    for n in range(1, 8):
        inverse_plane(n)
    for t in range(3):
        taken(t)
    moved_f = permute(RAW[0:3].reshape(192, LANES), split)
    received(setup, "near_next")
    VM[OFF - 1] = V[OFF - 1] * (element_row * plane_flag(-1, 0))
    inverse_plane(0)
    for t in range(4):
        if t < 3:
            moved = moved_f[64 * t : 64 * t + 64]
        else:
            taken(t)
            moved = permute(RAW[t].reshape(64, LANES), split)
        for n in range(8):
            q = moved[8 * n : 8 * n + 8]
            if t < 3:
                q = q * (node_row * plane_flag(n, 1))[0:EDGE]
            Q0[t, n] = q
            Q[t, n] = q
            X[0, t, n + OFF, 0:EDGE] = q * INV[n + OFF, 0:EDGE] if t < 3 else q
        begin(0, t)
    received(setup, "far_next", "near_prev")
    for n in (-4, -3, -2, 8, 9, 10, 11):
        VM[n + OFF] = V[n + OFF] * (element_row * plane_flag(n, 0))
    for n in (-3, -2, -1, 8, 9, 10):
        inverse_plane(n)
    for e in range(-3, 10):
        both = INV[e + OFF] + INV[e + OFF + 1]
        both = both + next_y(both)
        both = both + next_z(both)
        there = element_row * plane_flag(e, 0)
        ISC[e + OFF] = there / jnp.where(there > 0.0, 0.1875 * both, 1.0)

    def along_x(j, k, slot):
        return remote(ZS.at[j, :, 2 * k : 2 * k + 2], RELAY.at[j, slot], x_send.at[j, k], x_recv.at[j, slot], x_line[k])

    def x_begin(j):
        for k in range(4):
            pl.when(x_me != k)(lambda k=k: along_x(j, k, x_me).start())
        RELAY[j, x_me] = ZS[j, :, pl.ds(2 * x_me, 2)]

    @pl.loop(0, KRYLOV)
    def _(j):
        for c in range(3):
            pass_outer(j, c)

        def modes_of(n, c):
            return forward_modes(X[j, c, n + OFF])

        def jacobi(n, c, before, after):
            JAC[c, n + OFF] = 2.0 * X[j, c, n + OFF] - INV[n + OFF] * back_to_nodes(before, after)

        def sweep(first, last, c, before, keep_first, keep_last):
            low = modes_of(first, c)
            for e in range(first, last + 1):
                high = modes_of(e + 1, c)
                weighted = weigh(element_modes(low, high), VM[e + OFF])
                after = from_after(weighted)
                if before is not None:
                    jacobi(e, c, before, after)
                elif keep_first is not None:
                    for m in range(4):
                        MID[c, keep_first, m] = after[m]
                before = from_before(weighted)
                low = high
            if keep_last is not None:
                for m in range(4):
                    MID[c, keep_last, m] = before[m]
            return before

        def halves_of(planes):
            for n in planes:
                JP[n + OFF], JM[n + OFF] = divergence_halves([JAC[c, n + OFF] for c in range(3)])

        def first_pressures(planes):
            for e in planes:
                defect = 0.25 * (JP[e + OFF + 1] + JM[e + OFF]) - X[j, 3, e + OFF]
                MD[e + OFF] = defect
                P1[e + OFF] = defect * ISC[e + OFF]

        def corrections(planes):
            for n in planes:
                slope = gradient(P1[n + OFF - 1], P1[n + OFF])
                scale = 0.25 * INV[n + OFF]
                CP[n + OFF], CM[n + OFF] = divergence_halves([scale * slope[c] for c in range(3)])

        def next_pressures(planes):
            for e in planes:
                change = MD[e + OFF] - 0.25 * (CP[e + OFF + 1] + CM[e + OFF])
                PN[e + OFF] = P1[e + OFF] + change * ISC[e + OFF]

        def z_planes(planes):
            for n in planes:
                slope = gradient(PN[n + OFF - 1], PN[n + OFF])
                scale = 0.25 * INV[n + OFF]
                for c in range(3):
                    z = JAC[c, n + OFF] - scale * slope[c]
                    Z[c, n + OFF] = z
                    if 0 <= n < 8:
                        ZS[j, c, n] = z[0:EDGE]
                if 0 <= n < 8:
                    ZS[j, 3, n] = PN[n + OFF, 0:EDGE]

        for c in range(3):
            sweep(0, 6, c, None, 0, 1)
        pass_outer(j, 3)
        halves_of(range(1, 7))
        for c in range(4):
            pass_inner(j, c)
        first_pressures(range(1, 6))
        corrections(range(2, 6))
        next_pressures(range(2, 5))
        z_planes((3, 4))

        for c in range(3):
            take_corners(j, c)
            before = sweep(-4, -1, c, None, None, None)
            jacobi(0, c, before, [MID[c, 0, m] for m in range(4)])
            sweep(7, 10, c, [MID[c, 1, m] for m in range(4)], None, None)

        halves_of((-3, -2, -1, 0, 7, 8, 9, 10))
        take_corners(j, 3)

        @pl.when(j == 1)
        def _():
            x_begin(0)

        @pl.when(j == 2)
        def _():
            x_begin(1)

        first_pressures((*range(-3, 1), *range(6, 10)))
        corrections((-2, -1, 0, 1, 6, 7, 8, 9))
        next_pressures((-2, -1, 0, 1, 5, 6, 7, 8))
        z_planes((-1, 0, 1, 2, 5, 6, 7, 8))
        @pl.when(j == 2)
        def _():
            x_begin(2)

        for c in range(3):
            low = forward_modes(Z[c, OFF - 1])
            before = None
            for e in range(-1, 8):
                high = forward_modes(Z[c, e + 1 + OFF])
                modes = element_modes(low, high)
                place = (0, 2, 4)[c]
                if e >= 0:
                    own = modes[place][0:EDGE]
                    DIV[e] = own if c == 0 else DIV[e] + own
                weighted = list(weigh(modes, VM[e + OFF]))
                weighted[place] = weighted[place] + 0.25 * PN[e + OFF]
                after = from_after(weighted)
                if before is not None:
                    free = (node_row * plane_flag(e, 1))[0:EDGE]
                    w = back_to_nodes(before, after)[0:EDGE] * free
                    W[j, c, e] = w
                    q = w - Q[c, e]
                    Q[c, e] = q
                    X[j + 1, c, e + OFF, 0:EDGE] = q * INV[e + OFF, 0:EDGE]
                before = from_before(weighted)
                low = high
            pl.when(j < KRYLOV - 1)(lambda c=c: begin(j + 1, c))
        for e in range(8):
            w = 0.25 * DIV[e]
            W[j, 3, e] = w
            q = w - Q[3, e]
            Q[3, e] = q
            X[j + 1, 3, e + OFF, 0:EDGE] = q

        pl.when(j < KRYLOV - 1)(lambda: begin(j + 1, 3))

        def inner(other):
            total = None
            for n in range(8):
                for c in range(4):
                    term = W[j, c, n] * other(c, n)
                    total = term if total is None else total + term
            return fold(total)

        DOT[j * 4 + 3] = inner(lambda c, n: Q0[c, n])

        @pl.loop(0, j + 1)
        def _(k):
            DOT[j * 4 + k] = inner(lambda c, n: W[k, c, n])

    order = [(0, 0), (1, 0), (2, 0), (1, 1), (2, 1), (2, 2), (0, 3), (1, 3), (2, 3)]
    rows16 = lax.broadcasted_iota(jnp.int32, (16, 128), 0)
    stacked = jnp.zeros((16, 128), jnp.float32)
    for place, (a, b) in enumerate(order):
        line = jnp.sum(DOT[a * 4 + b], axis=0, keepdims=True)
        stacked = jnp.where(rows16 == place, line, stacked)
    folded = stacked + pltpu.roll(stacked, 64, 1)
    left = lax.broadcasted_iota(jnp.int32, (8, 128), 1) < 64
    tile = jnp.where(left, folded[0:8], folded[8:16])

    def reduce(tile, stage, buffer, me, peers, send, recv, meanwhile):
        PART[stage] = tile

        def copy(i, slot):
            return remote(PART.at[stage], buffer.at[slot], send.at[i], recv.at[slot], peers[i][0])

        for i in range(15):
            copy(i, me).start()
        buffer[me] = tile
        meanwhile()
        for i in reversed(range(15)):
            copy(i, peers[i][1]).wait_recv()
        total = buffer[0]
        for i in range(1, 16):
            total = total + buffer[i]
        for i in range(15):
            copy(i, me).wait_send()
        return total

    join = place_out == jnp.where(place_in < 128, 2 * place_in, 2 * place_in - 255)
    join = join.astype(jnp.bfloat16)

    def x_taken(j):
        for k in range(4):
            pl.when(x_me != k)(lambda k=k: along_x(j, k, k).wait_recv())
        RELAY[j] = permute(RELAY[j].reshape(256, LANES), join).reshape(4, 4, 2, EDGE, LANES)

    def x_taken_early():
        x_taken(0)
        x_taken(1)

    tile = reduce(tile, 0, ARB, b_me, b_peers, b_send, b_recv, x_taken_early)
    tile = reduce(tile, 1, ARA, a_me, a_peers, a_send, a_recv, lambda: x_taken(2))
    sums_a = jnp.sum(jnp.where(left, tile, 0.0), axis=1, keepdims=True)
    sums_b = jnp.sum(jnp.where(left, 0.0, tile), axis=1, keepdims=True)
    a00, a10, a20, a11, a21, a22, b0, b1 = [sums_a[i : i + 1] for i in range(8)]
    b2 = sums_b[0:1]
    r0 = 1.0 / jnp.sqrt(a00)
    l10 = a10 * r0
    l20 = a20 * r0
    r1 = 1.0 / jnp.sqrt(a11 - l10 * l10)
    l21 = (a21 - l20 * l10) * r1
    r2 = 1.0 / jnp.sqrt(a22 - l20 * l20 - l21 * l21)
    y0 = b0 * r0
    y1 = (b1 - l10 * y0) * r1
    y2 = (b2 - l20 * y0 - l21 * y1) * r2
    c2 = y2 * r2
    c1 = (y1 - l21 * c2) * r1
    c0 = (y0 - l10 * c1 - l20 * c2) * r0
    def back(k):
        return remote(OUT.at[k], HOME.at[:, :, rows(my_tile)], out_send.at[k], out_recv.at[my_tile], z_home[k])

    def arrive(i, holder):
        return remote(OUT.at[0], HOME.at[:, :, EDGE * i : EDGE * i + EDGE], out_send.at[0], out_recv.at[i], holder)

    def b_peer_of(i):
        tile = depth * 4 + i
        return same_xy + tile // 4 * 4, lax.rem(tile // 2, 2) * 2 + lax.rem(tile, 2)

    def stay(k):
        return pltpu.make_async_copy(OUT.at[k], HOME.at[:, :, rows(my_tile)], out_local.at[0])

    for k in range(4):
        OUT[k] = c0 * RELAY[0, k] + c1 * RELAY[1, k] + c2 * RELAY[2, k]
        pl.when(is_me(z_home[k]))(lambda k=k: stay(k).start())
        pl.when(jnp.logical_not(is_me(z_home[k])))(lambda k=k: back(k).start())

    sent(setup, *setup)

    @pl.loop(0, KRYLOV)
    def _(j):
        for c in range(4):
            all_sent(j, c)

    for t in range(5):
        for i in range(4):
            pl.when(jnp.logical_not(is_me(goes_to[i])))(lambda t=t, i=i: give(t, i).wait_send())

    for i in range(4):
        holder = b_peer_of(i)
        pl.when(is_me(holder))(lambda: stay(0).wait())
        pl.when(jnp.logical_not(is_me(holder)))(lambda i=i, holder=holder: arrive(i, holder).wait_recv())
    for c in range(3):
        vel_ref[c] = HOME[c]
    pre_ref[...] = HOME[3]
    for k in range(4):
        for j in range(KRYLOV):
            pl.when(x_me != k)(lambda j=j, k=k: along_x(j, k, x_me).wait_send())
        pl.when(jnp.logical_not(is_me(z_home[k])))(lambda k=k: back(k).wait_send())


def body(forcing, source, viscosity):
    f32 = jnp.float32
    vmem = lambda *shape: pltpu.VMEM(shape, f32)
    dma = lambda *shape: pltpu.SemaphoreType.DMA(shape)
    K = KRYLOV
    return pl.pallas_call(
        kernel,
        out_shape=(
            jax.ShapeDtypeStruct((3, 2, 32, LANES), f32),
            jax.ShapeDtypeStruct((2, 32, LANES), f32),
        ),
        in_specs=[pl.BlockSpec(memory_space=pl.ANY)] * 3,
        out_specs=(pl.BlockSpec(memory_space=pltpu.VMEM), pl.BlockSpec(memory_space=pltpu.VMEM)),
        scratch_shapes=[
            vmem(5, EDGE, EDGE, LANES),
            vmem(WIDE, WIDE, LANES),
            vmem(WIDE, WIDE, LANES),
            vmem(K + 1, 4, WIDE, WIDE, LANES),
            vmem(WIDE, WIDE, LANES),
            vmem(WIDE, WIDE, LANES),
            vmem(3, WIDE, WIDE, LANES),
            vmem(3, 2, 4, WIDE, LANES),
            vmem(WIDE, WIDE, LANES),
            vmem(WIDE, WIDE, LANES),
            vmem(WIDE, WIDE, LANES),
            vmem(WIDE, WIDE, LANES),
            vmem(WIDE, WIDE, LANES),
            vmem(WIDE, WIDE, LANES),
            vmem(WIDE, WIDE, LANES),
            vmem(3, WIDE, WIDE, LANES),
            vmem(K, 4, EDGE, EDGE, LANES),
            vmem(EDGE, EDGE, LANES),
            vmem(K, 4, EDGE, EDGE, LANES),
            vmem(4, EDGE, EDGE, LANES),
            vmem(4, EDGE, EDGE, LANES),
            vmem(4, 4, 2, EDGE, LANES),
            vmem(K, 4, 4, 2, EDGE, LANES),
            vmem(4, 2, 32, LANES),
            vmem(4 * K, 8, 128),
            vmem(16, 8, 128),
            vmem(16, 8, 128),
            vmem(2, 8, 128),
            dma(5, 4),
            dma(5, 4),
            dma(5),
            dma(6),
            dma(6),
            dma(K, 4, 8),
            dma(K, 4, 8),
            dma(K, 4),
            dma(K, 4),
            dma(4),
            dma(4),
            dma(1),
            dma(16),
            dma(16),
            dma(16),
            dma(16),
        ],
        compiler_params=pltpu.CompilerParams(
            collective_id=0, has_side_effects=True, vmem_limit_bytes=54784 * 1024
        ),
        name="stokes_cycle",
    )(forcing, source, viscosity)


def solution(mesh):
    placed = (P(None, "slab", "depth", None), P("slab", "depth", None), P("slab", "depth", None))
    return jax.shard_map(
        body,
        mesh=mesh,
        in_specs=placed,
        out_specs=(P(None, "slab", "depth", None), P("slab", "depth", None)),
        check_vma=False,
    )
```
